32 devices in a mesh: batch: 8 (over y, x, core), blk: 4 (over z).
Axes of the slice: x: 2, y: 2, z: 4, core: 2. Of those that a mesh axis runs over, the one named last changes fastest.
Arguments:
- tokens: bfloat16 [16, 1024, 512], P('batch', 'blk'), may hold values from -6 to 6
- lengths: int32 [16], P('batch'), may hold values from 256 to 1024, as said below
- w_query: bfloat16 [512, 512], replicated, may hold values from -0.25 to 0.25
- w_key: bfloat16 [512, 512], replicated, may hold values from -0.25 to 0.25
- w_value: bfloat16 [512, 512], replicated, may hold values from -0.25 to 0.25
- w_out: bfloat16 [512, 512], replicated, may hold values from -1 to 1
- w_in: bfloat16 [512, 2048], replicated, may hold values from -0.25 to 0.25
- b_in: float32 [2048], replicated, may hold values from -3 to 3
- w_back: bfloat16 [2048, 512], replicated, may hold values from -0.125 to 0.125
- b_back: float32 [512], replicated, may hold values from -3 to 3
- alpha_attn: float32 [], replicated, may hold values from 0.3 to 1.2
- alpha_ffn: float32 [], replicated, may hold values from 0.3 to 1.2
- cotangent: bfloat16 [16, 1024, 512], P('batch', 'blk'), may hold values from -6 to 6
Outputs:
- outputs: bfloat16 [16, 1024, 512], P('batch', 'blk')
- grad_input: bfloat16 [16, 1024, 512], P('batch', 'blk')
- grad_w_query: float32 [512, 512], replicated
- grad_w_key: float32 [512, 512], replicated
- grad_w_value: float32 [512, 512], replicated
- grad_w_out: float32 [512, 512], replicated
- grad_w_in: float32 [512, 2048], replicated
- grad_b_in: float32 [2048], replicated
- grad_w_back: float32 [2048, 512], replicated
- grad_b_back: float32 [512], replicated
- grad_alpha_attn: float32 [], replicated
- grad_alpha_ffn: float32 [], replicated
The draws below stay inside these ranges and needn't reach their ends.
Inputs may be any that keep to these rules, and one draw needn't show every extreme that they name: `lengths`: in each pair of sequences 2i, 2i + 1 one of the two, drawn from the seed, has length 1024; positions at or past a sequence's length are padding.
All inputs are finite; a program needn't handle non-finite values.
Results may differ from the reference program's by a relative error of at most 0.024.
Values may be sent and summed in bfloat16 or wider, within the bound.
A program may use at most 192 MiB of HBM per device.

```python
import math
import jax
import jax.numpy as jnp
from jax import lax

D = 512
HEADS = 8
HEAD_DIM = 64
FF = 2048
SEQS = 16
SEQ_LEN = 1024


def draw_lengths(key, part):
    key = jax.random.fold_in(key, 7)
    first_key, second_key, third_key = jax.random.split(key, 3)
    groups = SEQS // 2
    full_first = jax.random.randint(first_key, (groups,), 0, 2)
    shorter = jax.random.randint(second_key, (groups,), SEQ_LEN // 4, SEQ_LEN + 1)
    chosen = jax.random.randint(third_key, (), 0, groups)
    shorter = jnp.where(jnp.arange(groups) == chosen, SEQ_LEN // 4, shorter)
    first = jnp.where(full_first == 1, SEQ_LEN, shorter)
    second = jnp.where(full_first == 1, shorter, SEQ_LEN)
    return jnp.stack([first, second], axis=1).reshape(SEQS).astype(jnp.int32)


def steps_of(rng, extent, pieces, smallest, largest):
    gain, own = 1.0, jax.random.fold_in(rng, 6)
    for position, blocks in pieces:
        draws = jnp.exp(jax.random.uniform(jax.random.fold_in(own, position), (blocks,), jnp.float32, smallest / len(pieces), largest / len(pieces)))
        gain = gain * jnp.repeat(draws, extent[position] // blocks).reshape([-1 if axis == position else 1 for axis in range(len(extent))])
    return gain


def noise(rng, dims, spread, most, cuts=(), kind=jnp.bfloat16):
    values = spread * jax.random.normal(rng, dims, jnp.float32)
    if cuts:
        values = values * steps_of(rng, dims, cuts, -0.22, 0.18)
    return jnp.clip(values, -most, most).astype(kind)


def setup_inputs(seed: int = 0) -> dict:
    arg_keys = jax.random.split(jax.random.key(seed), 14)
    return {
        "tokens": noise(arg_keys[0], (SEQS, SEQ_LEN, D), 1.0, 6.0, ((0, 8), (1, 4))),
        "lengths": draw_lengths(jax.random.fold_in(arg_keys[13], 71), 0),
        "w_query": noise(arg_keys[2], (D, D), D ** -0.5, 0.25),
        "w_key": noise(arg_keys[3], (D, D), D ** -0.5, 0.25),
        "w_value": noise(arg_keys[4], (D, D), D ** -0.5, 0.25),
        "w_out": noise(arg_keys[5], (D, D), (D // 16) ** -0.5, 1.0),
        "w_in": noise(arg_keys[6], (D, FF), D ** -0.5, 0.25),
        "b_in": noise(arg_keys[7], (FF,), 0.3, 3.0, (), jnp.float32),
        "w_back": noise(arg_keys[8], (FF, D), FF ** -0.5, 0.125),
        "b_back": noise(arg_keys[9], (D,), 0.3, 3.0, (), jnp.float32),
        "alpha_attn": jnp.clip(jax.random.uniform(arg_keys[10], (), jnp.float32, 0.3, 1.2), 0.3, 1.2),
        "alpha_ffn": jnp.clip(jax.random.uniform(arg_keys[11], (), jnp.float32, 0.3, 1.2), 0.3, 1.2),
        "cotangent": noise(arg_keys[12], (SEQS, SEQ_LEN, D), 1.0, 6.0, ((0, 8), (1, 4))),
    }


precise = lax.Precision.HIGHEST

@jax.custom_vjp
def low(v):
    return lax.optimization_barrier(v.astype(jnp.bfloat16)).astype(jnp.float32)

@jax.custom_vjp
def low_back(v):
    return v

def low_keep(v):
    return (low(v), None)

def low_pass(kept, grad):
    return (grad,)

def back_keep(v):
    return (v, None)

def back_low(kept, grad):
    return (low(grad),)
low.defvjp(low_keep, low_pass)
low_back.defvjp(back_keep, back_low)

def low_both(value):
    return low(low_back(value))

def smooth(value):
    return jax.nn.gelu(value, approximate=True)

def matmul(left, right):
    return jnp.dot(left, right, precision=precise, preferred_element_type=jnp.float32)

def one_sequence(params, inputs, length):
    w_query, w_key, w_value, w_out, w_in, b_in, w_back, b_back, alpha_attn, alpha_ffn = params
    positions = jnp.arange(SEQ_LEN, dtype=jnp.int32)
    queries = low_both(matmul(inputs, w_query)).reshape(SEQ_LEN, HEADS, HEAD_DIM)
    keys_all = low_both(matmul(inputs, w_key)).reshape(SEQ_LEN, HEADS, HEAD_DIM)
    values_all = low_both(matmul(inputs, w_value)).reshape(SEQ_LEN, HEADS, HEAD_DIM)
    block_rows = math.gcd(SEQ_LEN, 512)
    block_count = SEQ_LEN // block_rows
    key_valid = positions < length

    def query_block(block_index):
        begin = (block_index * block_rows).astype(jnp.int32)
        chosen = lax.dynamic_slice_in_dim(queries, begin, block_rows, 0)
        rows = begin + jnp.arange(block_rows, dtype=jnp.int32)
        raw = low_back(jnp.einsum('qhe,khe->hqk', chosen, keys_all, precision=precise))
        scores = raw * 0.125
        allowed = (positions[None, :] <= rows[:, None]) & key_valid[None, :]
        scores = jnp.where(allowed[None], scores, -1e+30)
        top = lax.optimization_barrier(jnp.max(scores, axis=-1, keepdims=True))
        weights_raw = jnp.exp(scores - top)
        probs = weights_raw / lax.optimization_barrier(jnp.sum(weights_raw, axis=-1, keepdims=True))
        mixed = jnp.einsum('hqk,khe->qhe', low(probs), values_all, precision=precise)
        return mixed.reshape(block_rows, D)
    mixed_all = lax.map(jax.checkpoint(query_block), jnp.arange(block_count, dtype=jnp.int32))
    attn = low_both(mixed_all.reshape(SEQ_LEN, D))
    branch = low_back(matmul(attn, w_out))
    live = (positions < length).astype(jnp.float32)[:, None]
    resid = inputs + alpha_attn * live * branch
    hidden = low_back(matmul(low(resid), w_in) + b_in)
    activated = low(smooth(hidden))
    ffn_out = low_back(matmul(activated, w_back) + b_back)
    return resid + alpha_ffn * ffn_out

def forward(params, inputs_all, lengths):

    def step(carry, item):
        inputs, length = item
        layer = jax.checkpoint(one_sequence)
        return (carry, layer(params, inputs, length))
    start = jnp.zeros((), jnp.float32)
    final, outputs = lax.scan(step, start, (inputs_all, lengths))
    return outputs

def reference(tokens, lengths, w_query, w_key, w_value, w_out, w_in, b_in, w_back, b_back, alpha_attn, alpha_ffn, cotangent):
    params = tuple((item.astype(jnp.float32) for item in (w_query, w_key, w_value, w_out, w_in, b_in, w_back, b_back, alpha_attn, alpha_ffn)))

    def whole(params_now, inputs_now):
        return forward(params_now, inputs_now, lengths)
    outputs, pull = jax.vjp(whole, params, tokens.astype(jnp.float32))
    param_grads, input_grad = pull(cotangent.astype(jnp.float32))
    g_query, g_key, g_value, g_out, g_in, g_b_in, g_back, g_b_back, g_alpha_attn, g_alpha_ffn = param_grads
    return (outputs.astype(jnp.bfloat16), input_grad.astype(jnp.bfloat16), g_query, g_key, g_value, g_out, g_in, g_b_in, g_back, g_b_back, g_alpha_attn, g_alpha_ffn)
```

```python
import functools
import math

import jax
import jax.numpy as jnp
from jax import lax
from jax.experimental import pallas as pl
from jax.experimental.pallas import tpu as pltpu
from jax.sharding import PartitionSpec as P

HEADS = 8
HEAD_DIM = 64


MESH = pl.DeviceIdType.MESH
CHUNK_ROWS = 1024


class Reducer:
    def __init__(self, nb, nz, rows):
        self.rows = rows
        plane = [("batch", 1 << i) for i in range(1, nb.bit_length() - 1)]
        line = [("blk", 1 << i) for i in range(nz.bit_length() - 1)]
        self.orders = [plane + line, plane[::-1] + line]
        self.all_bits = [("batch", 1)] + plane + line
        self.steps = len(self.orders[0])
        self.halves = 0
        length, land = rows // 4, rows // 2
        self.sizes, self.lands = [], [[], []]
        for _ in range(self.steps):
            if length >= 32:
                length //= 2
                self.halves += 1
            self.sizes.append(length)
            for o in (0, 1):
                self.lands[o].append(land)
                land += length
        self.land_rows = land
        self.sems = 2 + 4 * self.steps

    def scratch(self, chunks, width):
        return [
            pltpu.VMEM((chunks, self.land_rows, width), jnp.bfloat16),
            pltpu.SemaphoreType.DMA((chunks, self.sems)),
            pltpu.SemaphoreType.DMA((chunks, self.sems)),
        ]

    def bind(self, grads, total, land, send_sem, recv_sem):
        self.grads, self.total, self.land = grads, total, land
        self.send_sem, self.recv_sem = send_sem, recv_sem
        self.at = {"batch": lax.axis_index("batch"), "blk": lax.axis_index("blk")}
        core = self.at["batch"] % 2
        half = self.rows // 2
        self.core_keep, self.core_send = core * half, (1 - core) * half
        self.keep, self.send, self.own = [[], []], [[], []], []
        for o in (0, 1):
            off = self.core_keep + o * (half // 2)
            for i, (axis, bit) in enumerate(self.orders[o]):
                mine = (self.at[axis] // bit) % 2
                if i < self.halves:
                    self.keep[o].append(off + mine * self.sizes[i])
                    self.send[o].append(off + (1 - mine) * self.sizes[i])
                    off = self.keep[o][-1]
                else:
                    self.keep[o].append(off)
                    self.send[o].append(off)
            self.own.append(off)

    def partner(self, axis, bit):
        mine = (self.at[axis] // bit) % 2
        there = self.at[axis] + bit * (1 - 2 * mine)
        if axis == "batch":
            return (there, self.at["blk"])
        return (self.at["batch"], there)

    def copy(self, c, src, src_row, dst, dst_row, size, sem, axis, bit):
        return pltpu.make_async_remote_copy(
            src_ref=src.at[c, pl.ds(pl.multiple_of(src_row, 16), size)],
            dst_ref=dst.at[c, pl.ds(pl.multiple_of(dst_row, 16), size)],
            send_sem=self.send_sem.at[c, sem],
            recv_sem=self.recv_sem.at[c, sem],
            device_id=self.partner(axis, bit),
            device_id_type=MESH,
        )

    def core_out(self, c):
        return self.copy(c, self.grads, self.core_send, self.land, 0, self.rows // 2, 0, "batch", 1)

    def core_back(self, c):
        return self.copy(
            c, self.total, self.core_keep, self.total, self.core_keep, self.rows // 2, 1, "batch", 1
        )

    def out(self, c, o, i):
        axis, bit = self.orders[o][i]
        return self.copy(
            c, self.grads, self.send[o][i], self.land, self.lands[o][i], self.sizes[i],
            2 + o * self.steps + i, axis, bit,
        )

    def back(self, c, o, i):
        axis, bit = self.orders[o][i]
        row = self.keep[o][i]
        return self.copy(
            c, self.total, row, self.total, row, self.sizes[i],
            2 + (2 + o) * self.steps + i, axis, bit,
        )

    def add(self, c, row, land_row, size, last=False):
        piece = min(size, 64)
        target = self.total if last else self.grads

        def body(k, carry):
            here = pl.ds(pl.multiple_of(row + k * piece, 16), piece)
            there = pl.ds(pl.multiple_of(land_row + k * piece, 16), piece)
            target[c, here] = self.grads[c, here] + self.land[c, there]
            return carry

        lax.fori_loop(0, size // piece, body, 0)

    def stages(self):
        return 2 * self.steps + 3 - (self.steps - self.halves)

    def stage(self, k, c):
        n = self.steps
        if k == 0:
            self.core_out(c).start()
        elif k <= n + 1:
            i = k - 2
            if k == 1:
                self.core_out(c).wait()
                self.add(c, self.core_keep, 0, self.rows // 2)
            else:
                for o in (0, 1):
                    self.out(c, o, i).wait()
                    self.add(c, self.keep[o][i], self.lands[o][i], self.sizes[i], i == n - 1)
            if i + 1 < n:
                for o in (0, 1):
                    self.out(c, o, i + 1).start()
            else:
                for o in (0, 1):
                    self.back(c, o, self.halves - 1).start()
        elif k < self.stages() - 1:
            i = self.halves - 1 - (k - n - 2)
            for o in (0, 1):
                self.back(c, o, i).wait()
            if i > 0:
                for o in (0, 1):
                    self.back(c, o, i - 1).start()
            else:
                self.core_back(c).start()
        else:
            self.core_back(c).wait()

    def small_copy(self, small, land, send_sem, recv_sem, i):
        axis, bit = self.all_bits[i]
        return pltpu.make_async_remote_copy(
            src_ref=small.at[i],
            dst_ref=land.at[i],
            send_sem=send_sem.at[i],
            recv_sem=recv_sem.at[i],
            device_id=self.partner(axis, bit),
            device_id_type=MESH,
        )


def reduce_kernel(
    plan, chunks, grads_in, small_in, total, small_out,
    grads, land, send_sem, recv_sem, small, small_land, small_send, small_recv, load_sem,
):
    plan.bind(grads, total, land, send_sem, recv_sem)
    load = pltpu.make_async_copy(grads_in, grads, load_sem)
    load.start()
    barrier = pltpu.get_barrier_semaphore()
    for axis, bit in plan.all_bits:
        pl.semaphore_signal(barrier, inc=1, device_id=plan.partner(axis, bit), device_id_type=MESH)
    pl.semaphore_wait(barrier, len(plan.all_bits))
    small[0] = small_in[...]
    load.wait()

    def tick(t, carry):
        for k in range(plan.stages() - 1, -1, -1):
            c = t - k

            @pl.when((c >= 0) & (c < chunks))
            def _():
                plan.stage(k, c)

        return carry

    lax.fori_loop(0, chunks + plan.stages() - 1, tick, 0)
    steps = len(plan.all_bits)
    for i in range(steps):
        plan.small_copy(small, small_land, small_send, small_recv, i).start()
        plan.small_copy(small, small_land, small_send, small_recv, i).wait()
        small[i + 1] = small[i] + small_land[i]
    small_out[...] = small[steps]


def reduce_all(grads, small, nb, nz):
    chunks, rows, width = grads.shape
    plan = Reducer(nb, nz, rows)
    steps = len(plan.all_bits)
    return pl.pallas_call(
        functools.partial(reduce_kernel, plan, chunks),
        out_shape=(
            jax.ShapeDtypeStruct(grads.shape, jnp.bfloat16),
            jax.ShapeDtypeStruct(small.shape, jnp.float32),
        ),
        in_specs=[pl.BlockSpec(memory_space=pl.ANY), pl.BlockSpec(memory_space=pltpu.VMEM)],
        out_specs=(pl.BlockSpec(memory_space=pltpu.VMEM), pl.BlockSpec(memory_space=pltpu.VMEM)),
        scratch_shapes=[pltpu.VMEM(grads.shape, jnp.bfloat16)]
        + plan.scratch(chunks, width)
        + [
            pltpu.VMEM((steps + 1,) + small.shape, jnp.float32),
            pltpu.VMEM((steps,) + small.shape, jnp.float32),
            pltpu.SemaphoreType.DMA((steps,)),
            pltpu.SemaphoreType.DMA((steps,)),
            pltpu.SemaphoreType.DMA,
        ],
        name="grad_sum",
        compiler_params=pltpu.CompilerParams(
            collective_id=0, has_side_effects=True, vmem_limit_bytes=48 << 20
        ),
    )(grads, small)


def smooth(value):
    return jax.nn.gelu(value, approximate=True)


def project(left, right):
    return jnp.dot(left, right, preferred_element_type=jnp.float32)


def per_device(
    tokens,
    lengths,
    w_query,
    w_key,
    w_value,
    w_out,
    w_in,
    b_in,
    w_back,
    b_back,
    alpha_attn,
    alpha_ffn,
    cotangent,
):
    seq_count, block_len, width = tokens.shape
    rows_total = seq_count * block_len
    inputs = tokens.reshape(rows_total, width)
    own_start = lax.axis_index("blk") * block_len
    query_pos = own_start + jnp.arange(block_len, dtype=jnp.int32)
    query_live = (query_pos[None, :] < lengths[:, None]).astype(jnp.float32).reshape(rows_total, 1)
    query_bf = project(inputs, w_query).astype(jnp.bfloat16)
    key_bf = project(inputs, w_key).astype(jnp.bfloat16).reshape(seq_count, block_len, width)
    value_bf = project(inputs, w_value).astype(jnp.bfloat16).reshape(seq_count, block_len, width)
    query_heads = query_bf.reshape(seq_count, block_len, HEADS, HEAD_DIM)

    def pair_mask(row_pos, col_pos):
        causal = col_pos[None, None, :] <= row_pos[None, :, None]
        inside = col_pos[None, None, :] < lengths[:, None, None]
        return causal & inside

    initial = (
        jnp.full((seq_count, HEADS, block_len), -1e30, jnp.float32),
        jnp.zeros((seq_count, HEADS, block_len), jnp.float32),
        jnp.zeros((seq_count, HEADS, block_len, HEAD_DIM), jnp.float32),
    )
    key_piece = lax.all_gather(key_bf, "blk", axis=1, tiled=True)
    value_piece = lax.all_gather(value_bf, "blk", axis=1, tiled=True)
    span = key_piece.shape[1]
    fold_step_len = math.gcd(span, 512)

    def one_step(state, block_index):
        run_max, run_sum, run_acc = state
        begin = block_index * fold_step_len
        key_block = lax.dynamic_slice_in_dim(key_piece, begin, fold_step_len, 1).reshape(
            seq_count, fold_step_len, HEADS, HEAD_DIM
        )
        value_block = lax.dynamic_slice_in_dim(value_piece, begin, fold_step_len, 1).reshape(
            seq_count, fold_step_len, HEADS, HEAD_DIM
        )
        allowed = pair_mask(query_pos, begin + jnp.arange(fold_step_len, dtype=jnp.int32))[:, None]
        scores = (
            jnp.einsum(
                "sqhe,skhe->shqk", query_heads, key_block, preferred_element_type=jnp.float32
            )
            * 0.125
        )
        scores = jnp.where(allowed, scores, -1e30)
        new_max = jnp.maximum(run_max, jnp.max(scores, axis=-1))
        weights = jnp.where(allowed, jnp.exp(scores - new_max[..., None]), 0.0)
        factor = jnp.exp(run_max - new_max)
        run_sum = run_sum * factor + jnp.sum(weights, axis=-1)
        update = jnp.einsum(
            "shqk,skhe->shqe",
            weights.astype(jnp.bfloat16),
            value_block,
            preferred_element_type=jnp.float32,
        )
        run_acc = run_acc * factor[..., None] + update
        return ((new_max, run_sum, run_acc), None)

    result, unused = lax.scan(one_step, initial, jnp.arange(span // fold_step_len, dtype=jnp.int32))
    state = result
    run_max, run_sum, run_acc = state
    log_total = run_max + jnp.log(run_sum)
    attn_heads = jnp.transpose(run_acc / run_sum[..., None], (0, 2, 1, 3))
    attn_rows = attn_heads.reshape(rows_total, width)
    attn_bf = attn_rows.astype(jnp.bfloat16)
    branch = project(attn_bf, w_out)
    resid = inputs.astype(jnp.float32) + alpha_attn * query_live * branch
    resid_bf = resid.astype(jnp.bfloat16)
    hidden = project(resid_bf, w_in) + b_in
    activated, gelu_pull = jax.vjp(smooth, hidden)
    act_bf = activated.astype(jnp.bfloat16)
    ffn_out = project(act_bf, w_back) + b_back
    outputs = (resid + alpha_ffn * ffn_out).astype(jnp.bfloat16)
    grad_out = cotangent.reshape(rows_total, width).astype(jnp.float32)
    grad_alpha_ffn = jnp.sum(grad_out * ffn_out)
    grad_ffn_bf = (alpha_ffn * grad_out).astype(jnp.bfloat16)
    grad_b_back = jnp.sum(grad_ffn_bf.astype(jnp.float32), axis=0)
    grad_w_back = project(act_bf.T, grad_ffn_bf)
    grad_act = project(grad_ffn_bf, w_back.T)
    (grad_hidden,) = gelu_pull(grad_act)
    grad_hidden_bf = grad_hidden.astype(jnp.bfloat16)
    grad_b_in = jnp.sum(grad_hidden_bf.astype(jnp.float32), axis=0)
    grad_w_in = project(resid_bf.T, grad_hidden_bf)
    grad_resid = grad_out + project(grad_hidden_bf, w_in.T)
    grad_alpha_attn = jnp.sum(grad_resid * query_live * branch)
    grad_branch_bf = (alpha_attn * query_live * grad_resid).astype(jnp.bfloat16)
    grad_w_out = project(attn_bf.T, grad_branch_bf)
    grad_attn_bf = project(grad_branch_bf, w_out.T).astype(jnp.bfloat16)
    grad_attn_heads = grad_attn_bf.reshape(seq_count, block_len, HEADS, HEAD_DIM)
    delta = jnp.sum(grad_attn_heads.astype(jnp.float32) * attn_heads, axis=-1).transpose(0, 2, 1)
    gathered = (
        lax.all_gather(key_bf, "blk", axis=1, tiled=True),
        lax.all_gather(value_bf, "blk", axis=1, tiled=True),
    )
    key_all, value_all = gathered
    full_len = key_all.shape[1]
    step_len = math.gcd(full_len, 512)

    def back_step(state_now, block_index):
        grad_query, grad_keys, grad_values = state_now
        begin = block_index * step_len
        key_block = lax.dynamic_slice_in_dim(key_all, begin, step_len, 1).reshape(
            seq_count, step_len, HEADS, HEAD_DIM
        )
        value_block = lax.dynamic_slice_in_dim(value_all, begin, step_len, 1).reshape(
            seq_count, step_len, HEADS, HEAD_DIM
        )
        allowed = pair_mask(query_pos, begin + jnp.arange(step_len, dtype=jnp.int32))[:, None]
        scores = (
            jnp.einsum(
                "sqhe,skhe->shqk", query_heads, key_block, preferred_element_type=jnp.float32
            )
            * 0.125
        )
        probs = jnp.where(allowed, jnp.exp(scores - log_total[..., None]), 0.0)
        grad_probs = jnp.einsum(
            "sqhe,skhe->shqk", grad_attn_heads, value_block, preferred_element_type=jnp.float32
        )
        grad_scores = (0.125 * (probs * (grad_probs - delta[..., None]))).astype(jnp.bfloat16)
        grad_query = grad_query + jnp.einsum(
            "shqk,skhe->sqhe", grad_scores, key_block, preferred_element_type=jnp.float32
        )
        grad_values_block = jnp.einsum(
            "shqk,sqhe->skhe",
            probs.astype(jnp.bfloat16),
            grad_attn_heads,
            preferred_element_type=jnp.float32,
        )
        grad_keys_block = jnp.einsum(
            "shqk,sqhe->skhe", grad_scores, query_heads, preferred_element_type=jnp.float32
        )
        grad_keys = lax.dynamic_update_slice_in_dim(
            grad_keys, grad_keys_block.reshape(seq_count, step_len, width), begin, 1
        )
        grad_values = lax.dynamic_update_slice_in_dim(
            grad_values, grad_values_block.reshape(seq_count, step_len, width), begin, 1
        )
        return ((grad_query, grad_keys, grad_values), None)

    query_zero = jnp.zeros((seq_count, block_len, HEADS, HEAD_DIM), jnp.float32)
    block_steps = jnp.arange(full_len // step_len, dtype=jnp.int32)
    back_start = (
        query_zero,
        jnp.zeros((seq_count, full_len, width), jnp.float32),
        jnp.zeros((seq_count, full_len, width), jnp.float32),
    )
    back_state, unused = lax.scan(back_step, back_start, block_steps)
    grad_query_all, grad_keys_all, grad_values_all = back_state
    key_sum, value_sum = (
        lax.psum_scatter(
            grad_keys_all.astype(jnp.bfloat16), "blk", scatter_dimension=1, tiled=True
        ).astype(jnp.float32),
        lax.psum_scatter(
            grad_values_all.astype(jnp.bfloat16), "blk", scatter_dimension=1, tiled=True
        ).astype(jnp.float32),
    )
    grad_query_bf = grad_query_all.reshape(rows_total, width).astype(jnp.bfloat16)
    grad_key_bf = key_sum.reshape(rows_total, width).astype(jnp.bfloat16)
    grad_value_bf = value_sum.reshape(rows_total, width).astype(jnp.bfloat16)
    grad_w_query = project(inputs.T, grad_query_bf)
    grad_w_key = project(inputs.T, grad_key_bf)
    grad_w_value = project(inputs.T, grad_value_bf)
    grad_input = (
        grad_resid
        + project(grad_query_bf, w_query.T)
        + project(grad_key_bf, w_key.T)
        + project(grad_value_bf, w_value.T)
    )
    grad_input = grad_input.astype(jnp.bfloat16).reshape(seq_count, block_len, width)
    nb, nz = lax.axis_size("batch"), lax.axis_size("blk")
    ff = grad_w_back.shape[0]
    pieces = [grad_w_query, grad_w_key, grad_w_value, grad_w_out]
    pieces += [grad_w_in[:, k * width : (k + 1) * width] for k in range(ff // width)]
    pieces += [grad_w_back]
    packed = jnp.concatenate([p.astype(jnp.bfloat16) for p in pieces], axis=0)
    packed = packed.reshape(-1, CHUNK_ROWS, width)
    small = jnp.concatenate(
        [
            grad_b_in.reshape(-1, width),
            grad_b_back.reshape(1, width),
            jnp.full((1, width), grad_alpha_attn),
            jnp.full((1, width), grad_alpha_ffn),
            jnp.zeros((1, width), jnp.float32),
        ],
        axis=0,
    )
    total, small_sum = reduce_all(packed, small, nb, nz)
    flat = total.reshape(-1, width).astype(jnp.float32)
    sum_query, sum_key, sum_value, sum_out = [flat[k * width : (k + 1) * width] for k in range(4)]
    sum_in = jnp.concatenate([flat[(4 + k) * width : (5 + k) * width] for k in range(ff // width)], axis=1)
    sum_back = flat[4 * width + ff :]
    rows_b = ff // width
    sum_b_in = small_sum[:rows_b].reshape(ff)
    sum_b_back = small_sum[rows_b]
    sum_alpha_attn = small_sum[rows_b + 1, 0]
    sum_alpha_ffn = small_sum[rows_b + 2, 0]
    return (
        outputs.reshape(seq_count, block_len, width),
        grad_input,
        sum_query,
        sum_key,
        sum_value,
        sum_out,
        sum_in,
        sum_b_in,
        sum_back,
        sum_b_back,
        sum_alpha_attn,
        sum_alpha_ffn,
    )


def solution(mesh):
    return jax.shard_map(
        per_device,
        mesh=mesh,
        in_specs=(
            P("batch", "blk", None),
            P("batch"),
            P(),
            P(),
            P(),
            P(),
            P(),
            P(),
            P(),
            P(),
            P(),
            P(),
            P("batch", "blk", None),
        ),
        out_specs=(
            P("batch", "blk", None),
            P("batch", "blk", None),
            P(),
            P(),
            P(),
            P(),
            P(),
            P(),
            P(),
            P(),
            P(),
            P(),
        ),
        check_vma=False,
    )
```

```python
import functools

import jax
import jax.numpy as jnp
from jax import lax
from jax.experimental import pallas as pl
from jax.experimental.pallas import tpu as pltpu
from jax.sharding import PartitionSpec as P

HEADS = 8
HEAD_DIM = 64
PAIR = 2 * HEAD_DIM

MESH = pl.DeviceIdType.MESH


class Reducer:
    def __init__(self, nb, nz, rows):
        self.rows = rows
        plane = [("batch", 1 << i) for i in range(1, nb.bit_length() - 1)]
        line = [("blk", 1 << i) for i in range(nz.bit_length() - 1)]
        self.orders = [plane + line, plane[::-1] + line]
        self.all_bits = [("batch", 1)] + plane + line
        self.steps = len(self.orders[0])
        self.halves = 0
        length, land = rows // 4, rows // 2
        self.sizes, self.lands = [], [[], []]
        for _ in range(self.steps):
            if length >= 32:
                length //= 2
                self.halves += 1
            self.sizes.append(length)
            for o in (0, 1):
                self.lands[o].append(land)
                land += length
        self.land_rows = land
        self.sems = 2 + 4 * self.steps

    def scratch(self, chunks, width):
        return [
            pltpu.VMEM((chunks, self.land_rows, width), jnp.bfloat16),
            pltpu.SemaphoreType.DMA((chunks, self.sems)),
            pltpu.SemaphoreType.DMA((chunks, self.sems)),
        ]

    def bind(self, grads, total, land, send_sem, recv_sem):
        self.grads, self.total, self.land = grads, total, land
        self.send_sem, self.recv_sem = send_sem, recv_sem
        self.at = {"batch": lax.axis_index("batch"), "blk": lax.axis_index("blk")}
        core = self.at["batch"] % 2
        half = self.rows // 2
        self.core_keep, self.core_send = core * half, (1 - core) * half
        self.keep, self.send, self.own = [[], []], [[], []], []
        for o in (0, 1):
            off = self.core_keep + o * (half // 2)
            for i, (axis, bit) in enumerate(self.orders[o]):
                mine = (self.at[axis] // bit) % 2
                if i < self.halves:
                    self.keep[o].append(off + mine * self.sizes[i])
                    self.send[o].append(off + (1 - mine) * self.sizes[i])
                    off = self.keep[o][-1]
                else:
                    self.keep[o].append(off)
                    self.send[o].append(off)
            self.own.append(off)

    def partner(self, axis, bit):
        mine = (self.at[axis] // bit) % 2
        there = self.at[axis] + bit * (1 - 2 * mine)
        if axis == "batch":
            return (there, self.at["blk"])
        return (self.at["batch"], there)

    def copy(self, c, src, src_row, dst, dst_row, size, sem, axis, bit):
        return pltpu.make_async_remote_copy(
            src_ref=src.at[c, pl.ds(pl.multiple_of(src_row, 16), size)],
            dst_ref=dst.at[c, pl.ds(pl.multiple_of(dst_row, 16), size)],
            send_sem=self.send_sem.at[c, sem],
            recv_sem=self.recv_sem.at[c, sem],
            device_id=self.partner(axis, bit),
            device_id_type=MESH,
        )

    def core_out(self, c):
        return self.copy(c, self.grads, self.core_send, self.land, 0, self.rows // 2, 0, "batch", 1)

    def core_back(self, c):
        return self.copy(
            c, self.total, self.core_keep, self.total, self.core_keep, self.rows // 2, 1, "batch", 1
        )

    def out(self, c, o, i):
        axis, bit = self.orders[o][i]
        return self.copy(
            c, self.grads, self.send[o][i], self.land, self.lands[o][i], self.sizes[i],
            2 + o * self.steps + i, axis, bit,
        )

    def back(self, c, o, i):
        axis, bit = self.orders[o][i]
        row = self.keep[o][i]
        return self.copy(
            c, self.total, row, self.total, row, self.sizes[i],
            2 + (2 + o) * self.steps + i, axis, bit,
        )

    def add(self, c, row, land_row, size, last=False):
        piece = min(size, 64)
        target = self.total if last else self.grads

        def body(k, carry):
            here = pl.ds(pl.multiple_of(row + k * piece, 16), piece)
            there = pl.ds(pl.multiple_of(land_row + k * piece, 16), piece)
            target[c, here] = self.grads[c, here] + self.land[c, there]
            return carry

        lax.fori_loop(0, size // piece, body, 0)

    def stages(self):
        return 2 * self.steps + 3 - (self.steps - self.halves)

    def stage(self, k, c):
        n = self.steps
        if k == 0:
            self.core_out(c).start()
        elif k <= n + 1:
            i = k - 2
            if k == 1:
                self.core_out(c).wait()
                self.add(c, self.core_keep, 0, self.rows // 2)
            else:
                for o in (0, 1):
                    self.out(c, o, i).wait()
                    self.add(c, self.keep[o][i], self.lands[o][i], self.sizes[i], i == n - 1)
            if i + 1 < n:
                for o in (0, 1):
                    self.out(c, o, i + 1).start()
            else:
                for o in (0, 1):
                    self.back(c, o, self.halves - 1).start()
        elif k < self.stages() - 1:
            i = self.halves - 1 - (k - n - 2)
            for o in (0, 1):
                self.back(c, o, i).wait()
            if i > 0:
                for o in (0, 1):
                    self.back(c, o, i - 1).start()
            else:
                self.core_back(c).start()
        else:
            self.core_back(c).wait()

    def small_copy(self, small, land, send_sem, recv_sem, i):
        axis, bit = self.all_bits[i]
        return pltpu.make_async_remote_copy(
            src_ref=small.at[i],
            dst_ref=land.at[i],
            send_sem=send_sem.at[i],
            recv_sem=recv_sem.at[i],
            device_id=self.partner(axis, bit),
            device_id_type=MESH,
        )


BF = jnp.bfloat16
F32 = jnp.float32
NEG = -1e30


def mm(left, right):
    return jnp.dot(left, right, preferred_element_type=F32)


def mm_nt(left, right):
    return lax.dot_general(left, right, (((1,), (1,)), ((), ())), preferred_element_type=F32)


def layer_kernel(plan, n, keep, lens, alphas, *refs):
    (
        tokens, cot, wq, wk, wv, wo, w_in, b_in, w_back, b_back,
        outputs, grad_input, total, small_out,
        x_all, wk_t, wv_t, x_t, k_all, v_all, k_t, v_t, q_m, do_m, top, norm, o_t, attn_t, do_t,
        live_branch, resid, resid_bf, resid_t, grad_ffn, ffn, grad_x, lse, delta,
        dq_t, dk, dv, acc, back_in,
        x_send, x_recv, r_send, r_recv,
        grads, land, send_sem, recv_sem, small, small_land, small_send, small_recv,
    ) = refs
    seqs, rows, width = tokens.shape
    chunks = grads.shape[0]
    ff_chunks = w_in.shape[1] // width
    pairs = width // PAIR
    plan.bind(grads, total, land, send_sem, recv_sem)
    b, z = lax.axis_index("batch"), lax.axis_index("blk")
    has_up, has_down = z < n - 1, z > 0
    alpha_attn, alpha_ffn = alphas[0], alphas[1]

    def x_copy(s, j):
        return pltpu.make_async_remote_copy(
            src_ref=x_all.at[s, j], dst_ref=x_all.at[s, j],
            send_sem=x_send.at[s, j], recv_sem=x_recv.at[s, j],
            device_id=(b, z + 1), device_id_type=MESH,
        )

    def r_copy(s, j, src):
        return pltpu.make_async_remote_copy(
            src_ref=src.at[s, j], dst_ref=back_in.at[s, j],
            send_sem=r_send.at[s, j], recv_sem=r_recv.at[s, j],
            device_id=(b, z - 1), device_id_type=MESH,
        )

    barrier = pltpu.get_barrier_semaphore()
    for axis, bit in plan.all_bits:
        pl.semaphore_signal(barrier, inc=1, device_id=plan.partner(axis, bit), device_id_type=MESH)

    @pl.when(has_up)
    def _():
        pl.semaphore_signal(barrier, inc=1, device_id=(b, z + 1), device_id_type=MESH)

    @pl.when(has_down)
    def _():
        pl.semaphore_signal(barrier, inc=1, device_id=(b, z - 1), device_id_type=MESH)

    for s in range(seqs):
        x_all[s, z] = tokens[s]
    pl.semaphore_wait(barrier, len(plan.all_bits) + jnp.where(has_up, 1, 0) + jnp.where(has_down, 1, 0))

    @pl.when(has_up)
    def _():
        for s in range(seqs):
            x_copy(s, z).start()

    wk_t[...] = wk[...].T
    wv_t[...] = wv[...].T
    small[0] = jnp.zeros_like(small[0])
    acc[...] = jnp.zeros_like(acc)
    low_lanes = lax.broadcasted_iota(jnp.int32, (rows, PAIR), 1) < HEAD_DIM
    key_iota = lax.broadcasted_iota(jnp.int32, (rows, rows), 0)
    query_pos = z * rows + lax.broadcasted_iota(jnp.int32, (1, rows), 1)

    def split_heads(value, target, s):
        for h in range(HEADS):
            pair = value[:, (h // 2) * PAIR : (h // 2 + 1) * PAIR]
            mask = low_lanes if h % 2 == 0 else jnp.logical_not(low_lanes)
            target[s, h] = jnp.where(mask, pair, 0.0).astype(BF)

    def slot(s, j):
        return s * n + j if keep else 0

    def project(s, j):
        here = slot(s, j)
        x = x_all[s, j]
        k_all[here] = mm(x, wk[...]).astype(BF)
        v_all[here] = mm(x, wv[...]).astype(BF)
        k_t[here] = mm_nt(wk_t[...], x).astype(BF)
        v_t[here] = mm_nt(wv_t[...], x).astype(BF)
        x_t[here] = x.T

    def allowed(s, j):
        limit = jnp.minimum(query_pos + 1, lens[s]) - j * rows
        return key_iota < limit

    def head_rows(head):
        return pl.ds(pl.multiple_of(head * HEAD_DIM, HEAD_DIM), HEAD_DIM)

    def pair_lanes(p):
        return pl.ds(pl.multiple_of(p * PAIR, PAIR), PAIR)

    def forward_tile(s, j):
        here = slot(s, j)
        mask = allowed(s, j)

        def pair_step(p, carry):
            keys = k_all[here, :, pair_lanes(p)]
            for h in (0, 1):
                head = 2 * p + h
                scores = jnp.where(mask, mm_nt(keys, q_m[s, head]), NEG)
                old = top[s, head]
                new = jnp.maximum(old, jnp.max(scores, axis=0, keepdims=True))
                weights = jnp.exp(scores - new)
                factor = jnp.exp(old - new)
                top[s, head] = new
                norm[s, head] = norm[s, head] * factor + jnp.sum(weights, axis=0, keepdims=True)
                part = mm(v_t[here, head_rows(head)], weights.astype(BF))
                o_t[s, head_rows(head)] = o_t[s, head_rows(head)] * factor + part
            return carry

        lax.fori_loop(0, pairs, pair_step, 0)

    def pass_on(s, j):
        x_copy(s, j).wait_recv()

        @pl.when(has_up)
        def _():
            x_copy(s, j).start()

    early = 2

    def start_seq(s):
        q = mm(x_all[s, z], wq[...]).astype(BF).astype(F32) * 0.125
        split_heads(q, q_m, s)
        top[s] = jnp.full_like(top[s], NEG)
        norm[s] = jnp.zeros_like(norm[s])
        o_t[s] = jnp.zeros_like(o_t[s])
        project(s, z)
        forward_tile(s, z)

    def attention(s):
        def block(i, carry):
            if s == 0:
                pass_on(s, z - i)
            else:
                @pl.when((i > early) | jnp.logical_not(has_up))
                def _():
                    pass_on(s, z - i)
            project(s, z - i)
            forward_tile(s, z - i)
            return carry

        lax.fori_loop(1, z + 1, block, 0)
        for h in range(HEADS):
            here = slice(h * HEAD_DIM, (h + 1) * HEAD_DIM)
            o_t[s, here] = o_t[s, here] / norm[s, h]
            lse[s, h] = top[s, h] + jnp.log(norm[s, h])
        attn_t[s] = o_t[s].astype(BF)
        branch = mm(attn_t[s].T, wo[...])
        position = z * rows + lax.broadcasted_iota(jnp.int32, (rows, 1), 0)
        live = (position < lens[s]).astype(F32)
        live_branch[s] = live * branch
        resid[...] = tokens[s].astype(F32) + alpha_attn * live_branch[s]
        resid_bf[...] = resid[...].astype(BF)
        resid_t[...] = resid_bf[...].T

    def feed_forward(s):
        grad_out = cot[s].astype(F32)
        grad_ffn[...] = (alpha_ffn * grad_out).astype(BF)
        ffn[...] = jnp.zeros_like(ffn)
        grad_x[s] = grad_out
        small[0, ff_chunks : ff_chunks + 1] += jnp.sum(
            grad_ffn[...].astype(F32), axis=0, keepdims=True
        )

        def column(c, carry):
            if s == 0:
                for i in range(1, early + 1):
                    @pl.when((c == 2 * (i - 1)) & (z >= i) & has_up)
                    def _():
                        pass_on(1, z - i)
            lanes = pl.ds(pl.multiple_of(c * width, width), width)
            hidden = mm(resid_bf[...], w_in[:, lanes]) + b_in[pl.ds(c, 1)]
            square = hidden * hidden
            tan = jnp.tanh(0.7978845608 * hidden * (1.0 + 0.044715 * square))
            half = 0.5 * (1.0 + tan)
            act = (hidden * half).astype(BF)
            slope = half + 0.5 * hidden * (1.0 - tan * tan) * (
                0.7978845608 * (1.0 + 3 * 0.044715 * square)
            )
            back = w_back[lanes]
            ffn[...] += mm(act, back)
            grad_hidden = (mm_nt(grad_ffn[...], back) * slope).astype(BF)
            small[0, pl.ds(c, 1)] += jnp.sum(grad_hidden.astype(F32), axis=0, keepdims=True)
            grad_x[s] += mm_nt(grad_hidden, w_in[:, lanes])
            grad_back = mm(act.T, grad_ffn[...])
            grad_in = mm(resid_t[...], grad_hidden)
            if s > 0:
                grad_back += grads[c, :width].astype(F32)
                grad_in += grads[c, width:].astype(F32)
            grads[c, :width] = grad_back.astype(BF)
            grads[c, width:] = grad_in.astype(BF)
            return carry

        lax.fori_loop(0, ff_chunks, column, 0)
        ffn_out = ffn[...] + b_back[...]
        outputs[s] = (resid[...] + alpha_ffn * ffn_out).astype(BF)
        small[0, ff_chunks + 2 : ff_chunks + 3] += jnp.sum(
            cot[s].astype(F32) * ffn_out, axis=0, keepdims=True
        )
        small[0, ff_chunks + 1 : ff_chunks + 2] += jnp.sum(
            grad_x[s] * live_branch[s], axis=0, keepdims=True
        )

    def attention_back(s):
        position = z * rows + lax.broadcasted_iota(jnp.int32, (rows, 1), 0)
        live = (position < lens[s]).astype(F32)
        grad_branch = (alpha_attn * live * grad_x[s]).astype(BF)
        acc[0] += mm(attn_t[s], grad_branch)
        do = mm_nt(grad_branch, wo[...]).astype(BF)
        split_heads(do, do_m, 0)
        do_t[...] = mm_nt(wo[...], grad_branch).astype(BF)
        for h in range(HEADS):
            here = slice(h * HEAD_DIM, (h + 1) * HEAD_DIM)
            delta[h] = jnp.sum(do_t[here].astype(F32) * o_t[s, here], axis=0, keepdims=True)
        dq_t[...] = jnp.zeros_like(dq_t)

        def block(j, carry):
            here = slot(s, j)
            if not keep:
                project(s, j)
            mask = allowed(s, j)

            def pair_step(p, carry_pair):
                keys = k_all[here, :, pair_lanes(p)]
                values = v_all[here, :, pair_lanes(p)]
                grad_key = jnp.zeros((rows, PAIR), F32)
                grad_value = jnp.zeros((rows, PAIR), F32)
                for h in (0, 1):
                    head = 2 * p + h
                    scores = mm_nt(keys, q_m[s, head])
                    probs = jnp.where(mask, jnp.exp(scores - lse[s, head]), 0.0)
                    grad_probs = mm_nt(values, do_m[0, head])
                    grad_scores = (probs * (grad_probs - delta[head])).astype(BF)
                    grad_value += mm(probs.astype(BF), do_m[0, head])
                    grad_key += mm(grad_scores, q_m[s, head])
                    dq_t[head_rows(head)] += mm(k_t[here, head_rows(head)], grad_scores)
                dk[:, pair_lanes(p)] = grad_key.astype(BF)
                dv[:, pair_lanes(p)] = grad_value.astype(BF)
                return carry_pair

            lax.fori_loop(0, pairs, pair_step, 0)
            part = mm_nt(dk[...], wk[...]) + mm_nt(dv[...], wv[...])
            acc[2] += mm(x_t[here], dk[...])
            acc[3] += mm(x_t[here], dv[...])

            @pl.when(j < z)
            def _():
                x_all[s, j] = part.astype(BF)

                @pl.when(jnp.logical_not(has_up))
                def _():
                    r_copy(s, j, x_all).start()

            @pl.when(j == z)
            def _():
                grad_x[s] += part

            return carry

        @pl.when(has_up)
        def _():
            def sent(j, carry):
                x_copy(s, j).wait_send()
                return carry

            lax.fori_loop(0, z + 1, sent, 0)

        lax.fori_loop(0, z + 1, block, 0)
        dq = (dq_t[...] * 0.125).T.astype(BF)
        if not keep:
            x_t[0] = tokens[s].T
        acc[1] += mm(x_t[slot(s, z)], dq)
        grad_x[s] += mm_nt(dq, wq[...])

    def send_back(s):
        def block(j, carry):
            @pl.when(has_up)
            def _():
                r_copy(s, j, back_in).wait_recv()

                @pl.when(j < z)
                def _():
                    back_in[s, j] = back_in[s, j] + x_all[s, j]
                    r_copy(s, j, back_in).start()

            return carry

        lax.fori_loop(0, z + 1, block, 0)

        @pl.when(has_up)
        def _():
            grad_input[s] = (grad_x[s] + back_in[s, z].astype(F32)).astype(BF)

        @pl.when(jnp.logical_not(has_up))
        def _():
            grad_input[s] = grad_x[s].astype(BF)

    for s in range(seqs):
        start_seq(s)
    for s in range(seqs):
        attention(s)
        feed_forward(s)
    for s in range(seqs):
        attention_back(s)
    for k in range(4):
        place = 2 * ff_chunks + k
        grads[place // 2, pl.ds((place % 2) * width, width)] = acc[k].astype(BF)
    for s in range(seqs):
        send_back(s)

    def tick(t, carry):
        for k in range(plan.stages() - 1, -1, -1):
            c = t - k

            @pl.when((c >= 0) & (c < chunks))
            def _():
                plan.stage(k, c)

        return carry

    lax.fori_loop(0, chunks + plan.stages() - 1, tick, 0)
    steps = len(plan.all_bits)
    for i in range(steps):
        plan.small_copy(small, small_land, small_send, small_recv, i).start()
        plan.small_copy(small, small_land, small_send, small_recv, i).wait()
        small[i + 1] = small[i] + small_land[i]
    small_out[...] = small[steps]

    @pl.when(has_down)
    def _():
        def sent(j, carry):
            for s in range(seqs):
                r_copy(s, j, back_in).wait_send()
            return carry

        lax.fori_loop(0, z, sent, 0)


def per_device(
    tokens, lengths, w_query, w_key, w_value, w_out, w_in, b_in, w_back, b_back,
    alpha_attn, alpha_ffn, cotangent,
):
    seqs, rows, width = tokens.shape
    ff = w_in.shape[1]
    nb, n = lax.axis_size("batch"), lax.axis_size("blk")
    keep = n <= 4
    slots = seqs * n if keep else 1
    ff_chunks = ff // width
    chunks = ff_chunks + 2
    plan = Reducer(nb, n, 2 * width)
    steps = len(plan.all_bits)
    small_rows = -(-(ff_chunks + 3) // 8) * 8
    vmem = pl.BlockSpec(memory_space=pltpu.VMEM)
    smem = pl.BlockSpec(memory_space=pltpu.SMEM)
    square = (rows, width)
    dma = pltpu.SemaphoreType.DMA
    outputs, grad_input, total, small = pl.pallas_call(
        functools.partial(layer_kernel, plan, n, keep),
        out_shape=(
            jax.ShapeDtypeStruct(tokens.shape, BF),
            jax.ShapeDtypeStruct(tokens.shape, BF),
            jax.ShapeDtypeStruct((chunks, 2 * width, width), BF),
            jax.ShapeDtypeStruct((small_rows, width), F32),
        ),
        in_specs=[smem, smem] + [vmem] * 10,
        out_specs=(vmem,) * 4,
        scratch_shapes=[
            pltpu.VMEM((seqs, n) + square, BF),
            pltpu.VMEM((width, width), BF),
            pltpu.VMEM((width, width), BF),
            pltpu.VMEM((slots, width, rows), BF),
            pltpu.VMEM((slots,) + square, BF),
            pltpu.VMEM((slots,) + square, BF),
            pltpu.VMEM((slots, width, rows), BF),
            pltpu.VMEM((slots, width, rows), BF),
            pltpu.VMEM((seqs, HEADS, rows, PAIR), BF),
            pltpu.VMEM((1, HEADS, rows, PAIR), BF),
            pltpu.VMEM((seqs, HEADS, 1, rows), F32),
            pltpu.VMEM((seqs, HEADS, 1, rows), F32),
            pltpu.VMEM((seqs, width, rows), F32),
            pltpu.VMEM((seqs, width, rows), BF),
            pltpu.VMEM((width, rows), BF),
            pltpu.VMEM((seqs,) + square, F32),
            pltpu.VMEM(square, F32),
            pltpu.VMEM(square, BF),
            pltpu.VMEM((width, rows), BF),
            pltpu.VMEM(square, BF),
            pltpu.VMEM(square, F32),
            pltpu.VMEM((seqs,) + square, F32),
            pltpu.VMEM((seqs, HEADS, 1, rows), F32),
            pltpu.VMEM((HEADS, 1, rows), F32),
            pltpu.VMEM((width, rows), F32),
            pltpu.VMEM(square, BF),
            pltpu.VMEM(square, BF),
            pltpu.VMEM((4, width, width), F32),
            pltpu.VMEM((seqs, n) + square, BF),
            dma((seqs, n)), dma((seqs, n)), dma((seqs, n)), dma((seqs, n)),
            pltpu.VMEM((chunks, 2 * width, width), BF),
        ]
        + plan.scratch(chunks, width)
        + [
            pltpu.VMEM((steps + 1, small_rows, width), F32),
            pltpu.VMEM((steps, small_rows, width), F32),
            dma((steps,)),
            dma((steps,)),
        ],
        name="layer",
        compiler_params=pltpu.CompilerParams(
            collective_id=0, has_side_effects=True, vmem_limit_bytes=60 << 20
        ),
    )(
        lengths, jnp.stack([alpha_attn, alpha_ffn]), tokens, cotangent,
        w_query, w_key, w_value, w_out, w_in, b_in.reshape(ff_chunks, width), w_back,
        b_back.reshape(1, width),
    )
    sum_back = total[:ff_chunks, :width].reshape(ff, width).astype(F32)
    sum_in = jnp.concatenate([total[c, width:] for c in range(ff_chunks)], axis=1).astype(F32)
    sum_out, sum_query = total[ff_chunks, :width].astype(F32), total[ff_chunks, width:].astype(F32)
    sum_key, sum_value = total[ff_chunks + 1, :width].astype(F32), total[ff_chunks + 1, width:].astype(F32)
    return (
        outputs, grad_input, sum_query, sum_key, sum_value, sum_out, sum_in,
        small[:ff_chunks].reshape(ff), sum_back, small[ff_chunks],
        jnp.sum(small[ff_chunks + 1]), jnp.sum(small[ff_chunks + 2]),
    )


def solution(mesh):
    return jax.shard_map(
        per_device,
        mesh=mesh,
        in_specs=(
            P("batch", "blk", None),
            P("batch"),
            P(),
            P(),
            P(),
            P(),
            P(),
            P(),
            P(),
            P(),
            P(),
            P(),
            P("batch", "blk", None),
        ),
        out_specs=(
            P("batch", "blk", None),
            P("batch", "blk", None),
            P(),
            P(),
            P(),
            P(),
            P(),
            P(),
            P(),
            P(),
            P(),
            P(),
        ),
        check_vma=False,
    )
```

```python
import functools

import jax
import jax.numpy as jnp
from jax import lax
from jax.experimental import pallas as pl
from jax.experimental.pallas import tpu as pltpu
from jax.sharding import PartitionSpec as P

HEADS = 8
HEAD_DIM = 64
PAIR = 2 * HEAD_DIM
MESH = pl.DeviceIdType.MESH
BF = jnp.bfloat16
F32 = jnp.float32
NEG = -1e30
GELU_A = 0.7978845608
GELU_B = 0.7978845608 * 0.044715

ORDER = (
    ("start_back", 0), ("block", 0, 0), ("send", 0, 0), ("block", 0, 1), ("block", 0, 2), ("send", 0, 1),
    ("block", 0, 3), ("send", 0, 2), ("end_back", 0), ("attention", 1), ("start_ff", 1), ("pass", 0, 0, 0),
    ("column", 1, 0), ("column", 1, 1), ("column", 1, 2), ("pass", 0, 1, 0), ("sum", 0, 2), ("column", 1, 3),
    ("end_ff", 1), ("small", 0), ("sum", 0, 0), ("start_back", 1), ("pass", 0, 2, 0), ("pass", 0, 0, 1),
    ("sum", 1, 2), ("block", 1, 0), ("small", 1), ("send", 1, 0), ("sum", 1, 0), ("sum", 2, 2), ("sum", 0, 3),
    ("sum", 0, 1), ("block", 1, 1), ("sum", 2, 0), ("sum", 3, 2), ("sum", 1, 3), ("sum", 3, 0), ("block", 1, 2),
    ("small", 2), ("send", 1, 1), ("block", 1, 3), ("small", 3), ("sum", 1, 1), ("pass", 1, 0, 0), ("end_back", 1),
    ("sum", 0, 4), ("sum", 0, 5), ("sum", 4, 2), ("sum", 2, 3), ("sum", 2, 1), ("pass", 1, 1, 0), ("pass", 0, 1, 1),
    ("sum", 1, 5), ("sum", 1, 4), ("sum", 4, 0), ("sum", 3, 1), ("sum", 5, 2), ("sum", 2, 5), ("sum", 3, 3),
    ("sum", 2, 4), ("pass", 0, 0, 2), ("sum", 5, 0), ("sum", 4, 1), ("pass", 1, 2, 0), ("sum", 6, 2), ("sum", 4, 3),
    ("sum", 3, 4), ("sum", 6, 0), ("sum", 5, 1), ("sum", 3, 5), ("sum", 5, 3), ("sum", 6, 1), ("sum", 7, 2),
    ("sum", 4, 4), ("sum", 8, 2), ("sum", 6, 3), ("sum", 4, 5), ("sum", 7, 0), ("sum", 5, 4), ("sum", 7, 3),
    ("sum", 5, 5), ("sum", 6, 4), ("sum", 7, 1), ("send", 1, 2), ("sum", 6, 5), ("sum", 8, 1), ("pass", 1, 0, 1),
    ("sum", 7, 4), ("sum", 7, 5), ("sum", 8, 4), ("sum", 8, 0), ("pass", 1, 1, 1), ("pass", 1, 0, 2), ("sum", 8, 3),
    ("sum", 8, 5),
)


class Reducer:
    def __init__(self, nb, nz, rows):
        self.rows, self.nz = rows, nz
        plane = [("batch", 1 << i) for i in range(1, nb.bit_length() - 1)]
        line = [("blk", 1 << i) for i in range(nz.bit_length() - 1)]
        self.all_bits = [("batch", 1)] + plane + line
        direct = (rows // 4 >> len(plane)) // nz >= 16
        steps = line if not direct else [("blk", 0)]
        self.orders = [plane + steps, plane[::-1] + steps]
        self.steps = len(self.orders[0])
        self.kinds, self.sizes, self.lands = [], [], [[], []]
        self.sem_at = [[], []]
        length, land, sem = rows // 4, rows // 2, 2
        for axis, bit in self.orders[0]:
            if bit == 0:
                kind, length, messages = "direct", length // nz, nz - 1
            elif length >= 32:
                kind, length, messages = "half", length // 2, 1
            else:
                kind, messages = "full", 1
            self.kinds.append(kind)
            self.sizes.append(length)
            for o in (0, 1):
                self.lands[o].append(land)
                self.sem_at[o].append(sem)
                land += length * messages
                sem += 2 * messages
        self.land_rows, self.sems = land, sem
        self.back_steps = [i for i in range(self.steps) if self.kinds[i] != "full"][::-1]
        self.stages = 3 + self.steps + len(self.back_steps)

    def scratch(self, chunks, width):
        return [
            pltpu.VMEM((chunks, self.land_rows, width), BF),
            pltpu.SemaphoreType.DMA((chunks, self.sems)),
            pltpu.SemaphoreType.DMA((chunks, self.sems)),
        ]

    def bind(self, grads, total, land, send_sem, recv_sem):
        self.grads, self.total, self.land = grads, total, land
        self.send_sem, self.recv_sem = send_sem, recv_sem
        self.at = {"batch": lax.axis_index("batch"), "blk": lax.axis_index("blk")}
        core = self.at["batch"] % 2
        half = self.rows // 2
        self.core_keep, self.core_send = core * half, (1 - core) * half
        self.start, self.keep, self.send = [[], []], [[], []], [[], []]
        for o in (0, 1):
            off = self.core_keep + o * (half // 2)
            for i, (axis, bit) in enumerate(self.orders[o]):
                size, here = self.sizes[i], self.at[axis]
                self.start[o].append(off)
                if self.kinds[i] == "half":
                    mine = (here // bit) % 2
                    self.keep[o].append(off + mine * size)
                    self.send[o].append(off + (1 - mine) * size)
                elif self.kinds[i] == "direct":
                    self.keep[o].append(off + here * size)
                    self.send[o].append(None)
                else:
                    self.keep[o].append(off)
                    self.send[o].append(off)
                off = self.keep[o][-1]

    def partner(self, axis, bit):
        mine = (self.at[axis] // bit) % 2
        there = self.at[axis] + bit * (1 - 2 * mine)
        if axis == "batch":
            return (there, self.at["blk"])
        return (self.at["batch"], there)

    def copy(self, c, src, src_row, dst, dst_row, size, sem, device):
        return pltpu.make_async_remote_copy(
            src_ref=src.at[c, pl.ds(pl.multiple_of(src_row, 16), size)],
            dst_ref=dst.at[c, pl.ds(pl.multiple_of(dst_row, 16), size)],
            send_sem=self.send_sem.at[c, sem],
            recv_sem=self.recv_sem.at[c, sem],
            device_id=device,
            device_id_type=MESH,
        )

    def core_out(self, c):
        there = self.partner("batch", 1)
        return self.copy(c, self.grads, self.core_send, self.land, 0, self.rows // 2, 0, there)

    def core_back(self, c):
        there, row = self.partner("batch", 1), self.core_keep
        return self.copy(c, self.total, row, self.total, row, self.rows // 2, 1, there)

    def out(self, c, o, i):
        axis, bit = self.orders[o][i]
        size, sem, land = self.sizes[i], self.sem_at[o][i], self.lands[o][i]
        if self.kinds[i] != "direct":
            there = self.partner(axis, bit)
            return [self.copy(c, self.grads, self.send[o][i], self.land, land, size, sem, there)]
        copies = []
        for d in range(1, self.nz):
            there = (self.at["blk"] + d) % self.nz
            row = self.start[o][i] + there * size
            copies.append(
                self.copy(
                    c, self.grads, row, self.land, land + (d - 1) * size, size,
                    sem + d - 1, (self.at["batch"], there),
                )
            )
        return copies

    def back(self, c, o, i):
        axis, bit = self.orders[o][i]
        size, row, sem = self.sizes[i], self.keep[o][i], self.sem_at[o][i]
        if self.kinds[i] != "direct":
            there = self.partner(axis, bit)
            return [self.copy(c, self.total, row, self.total, row, size, sem + 1, there)]
        copies = []
        for d in range(1, self.nz):
            there = (self.at["blk"] + d) % self.nz
            copies.append(
                self.copy(
                    c, self.total, row, self.total, row, size,
                    sem + self.nz - 2 + d, (self.at["batch"], there),
                )
            )
        return copies

    def add(self, c, row, land_row, size, pieces=1, last=False):
        part = min(size, 64)
        target = self.total if last else self.grads

        def body(k, carry):
            here = pl.ds(pl.multiple_of(row + k * part, 16), part)
            value = self.grads[c, here]
            if pieces > 1:
                value = value.astype(F32)
            for d in range(pieces):
                there = pl.ds(pl.multiple_of(land_row + d * size + k * part, 16), part)
                value = value + self.land[c, there].astype(value.dtype)
            target[c, here] = value.astype(BF)
            return carry

        lax.fori_loop(0, size // part, body, 0)

    def stage(self, k, c):
        if k == 0:
            self.core_out(c).start()
            return
        if k == 1:
            self.core_out(c).wait()
            self.add(c, self.core_keep, 0, self.rows // 2)
        elif k <= self.steps + 1:
            i = k - 2
            for o in (0, 1):
                for one in self.out(c, o, i):
                    one.wait()
                pieces = self.nz - 1 if self.kinds[i] == "direct" else 1
                last = i == self.steps - 1
                self.add(c, self.keep[o][i], self.lands[o][i], self.sizes[i], pieces, last)
        elif k < self.stages - 1:
            for o in (0, 1):
                for one in self.back(c, o, self.back_steps[k - self.steps - 2]):
                    one.wait()
        else:
            self.core_back(c).wait()
            return
        if k <= self.steps:
            for o in (0, 1):
                for one in self.out(c, o, k - 1):
                    one.start()
        elif k < self.stages - 2:
            for o in (0, 1):
                for one in self.back(c, o, self.back_steps[k - self.steps - 1]):
                    one.start()
        else:
            self.core_back(c).start()


def mm(left, right):
    return jnp.dot(left, right, preferred_element_type=F32)


def mm_nt(left, right):
    return lax.dot_general(left, right, (((1,), (1,)), ((), ())), preferred_element_type=F32)


def mm_tn(left, right):
    return lax.dot_general(left, right, (((0,), (0,)), ((), ())), preferred_element_type=F32)


def layer_kernel(plan, n, keep, lens, alpha_attn_ref, alpha_ffn_ref, b_in, b_back, *refs):
    (
        tokens_hbm, cot_hbm, wq_hbm, wk_hbm, wv_hbm, wo_hbm, w_in_hbm, w_back_hbm,
        outputs, grad_input, total_out, small_out,
        cot, wq, wk, wv, wo, w_in, w_back, load_sem,
        x_all, wk_t, wv_t, x_t, k_all, v_all, k_t, v_t, q_m, do_m, score, prob_bf, grad_bf, top, norm, o_t, attn_t, do_t,
        live_branch, resid, resid_bf, resid_t, grad_ffn, ffn, grad_x, lse, delta,
        dq_t, dk, dv, acc, back_in,
        x_send, x_recv, r_send, r_recv,
        grads, total, store_sem, land, send_sem, recv_sem, small, small_land, small_line, small_send, small_recv,
    ) = refs
    seqs, _, rows, width = x_all.shape
    chunks = grads.shape[0]
    ff_cols = w_in.shape[1] // width
    pairs = width // PAIR
    plan.bind(grads, total, land, send_sem, recv_sem)
    b, z = lax.axis_index("batch"), lax.axis_index("blk")
    has_up, has_down = z < n - 1, z > 0
    alpha_attn, alpha_ffn = alpha_attn_ref[0], alpha_ffn_ref[0]

    def load(i):
        if i < seqs:
            return pltpu.make_async_copy(tokens_hbm.at[i], x_all.at[i, z], load_sem.at[i])
        pairs_of = [
            (wk_hbm, wk), (wv_hbm, wv), (wq_hbm, wq), (wo_hbm, wo),
            (w_in_hbm, w_in), (w_back_hbm, w_back), (cot_hbm, cot),
        ]
        src, dst = pairs_of[i - seqs]
        return pltpu.make_async_copy(src, dst, load_sem.at[i])

    for i in range(seqs + 7):
        load(i).start()

    def x_copy(s, j):
        return pltpu.make_async_remote_copy(
            src_ref=x_all.at[s, j], dst_ref=x_all.at[s, j],
            send_sem=x_send.at[s, j], recv_sem=x_recv.at[s, j],
            device_id=(b, z + 1), device_id_type=MESH,
        )

    def r_copy(s, j, src):
        return pltpu.make_async_remote_copy(
            src_ref=src.at[s, j], dst_ref=back_in.at[s, j],
            send_sem=r_send.at[s, j], recv_sem=r_recv.at[s, j],
            device_id=(b, z - 1), device_id_type=MESH,
        )

    barrier = pltpu.get_barrier_semaphore()
    plane = [(axis, bit) for axis, bit in plan.all_bits if axis == "batch"]
    peers = [plan.partner(axis, bit) for axis, bit in plane] + [(b, (z + d) % n) for d in range(1, n)]
    for peer in peers:
        pl.semaphore_signal(barrier, inc=1, device_id=peer, device_id_type=MESH)
    pl.semaphore_wait(barrier, len(peers))

    def send_own(s):
        @pl.when(has_up)
        def _():
            x_copy(s, z).start()

    for s in range(seqs):
        load(s).wait()
        if s == 0:
            send_own(0)

    load(seqs).wait()
    wk_t[...] = wk[...].T
    load(seqs + 1).wait()
    wv_t[...] = wv[...].T
    small[0] = jnp.zeros_like(small[0])
    low_lanes = lax.broadcasted_iota(jnp.int32, (rows, PAIR), 1) < HEAD_DIM
    key_iota = lax.broadcasted_iota(jnp.int32, (rows, rows), 0)
    query_pos = z * rows + lax.broadcasted_iota(jnp.int32, (1, rows), 1)

    def split_heads(value, target):
        for h in range(HEADS):
            pair = value[:, (h // 2) * PAIR : (h // 2 + 1) * PAIR]
            mask = low_lanes if h % 2 == 0 else jnp.logical_not(low_lanes)
            target[h // 2, h % 2 * rows : (h % 2 + 1) * rows] = jnp.where(mask, pair, 0.0).astype(BF)

    def slot(s, j):
        return s * n + j if keep else 0

    def project(s, j):
        here = slot(s, j)
        x = x_all[s, j]
        k_all[here] = mm(x, wk[...]).astype(BF)
        v_all[here] = mm(x, wv[...]).astype(BF)
        k_t[here] = mm_nt(wk_t[...], x).astype(BF)
        v_t[here] = mm_nt(wv_t[...], x).astype(BF)
        x_t[here] = x.T

    def allowed(s, j):
        limit = jnp.minimum(query_pos + 1, lens[s]) - j * rows
        return key_iota < limit

    def forward_tile(s, j):
        here = slot(s, j)
        mask = allowed(s, j)

        for head in range(HEADS):
            lanes = slice(head // 2 * PAIR, (head // 2 + 1) * PAIR)
            score[head] = jnp.where(mask, mm_nt(k_all[here, :, lanes], q_m[s, head // 2, head % 2 * rows : (head % 2 + 1) * rows]), NEG)
        for head in range(HEADS):
            own = slice(head * HEAD_DIM, (head + 1) * HEAD_DIM)
            scores = score[head]
            old = top[s, head]
            new = jnp.maximum(old, jnp.max(scores, axis=0, keepdims=True))
            weights = jnp.exp(scores - new)
            factor = jnp.exp(old - new)
            top[s, head] = new
            norm[s, head] = norm[s, head] * factor + jnp.sum(weights, axis=0, keepdims=True)
            o_t[s, own] = o_t[s, own] * factor + mm(v_t[here, own], weights.astype(BF))

    def pass_on(s, j):
        x_copy(s, j).wait_recv()

        @pl.when(has_up)
        def _():
            x_copy(s, j).start()

    early = 2

    def start_seq(s):
        if s == 0:
            load(seqs + 2).wait()
        q = mm(x_all[s, z], wq[...]).astype(BF).astype(F32) * 0.125
        split_heads(q, q_m.at[s])
        top[s] = jnp.full_like(top[s], NEG)
        norm[s] = jnp.zeros_like(norm[s])
        o_t[s] = jnp.zeros_like(o_t[s])
        project(s, z)
        forward_tile(s, z)

    def attention(s):
        def block(i, carry):
            if s == 0:
                pass_on(s, z - i)

            else:
                @pl.when((i > early) | jnp.logical_not(has_up))
                def _():
                    pass_on(s, z - i)
            project(s, z - i)
            forward_tile(s, z - i)
            return carry

        lax.fori_loop(1, z + 1, block, 0)
        if s == 0:
            @pl.when(z > 0)
            def _():
                send_own(1)

            load(seqs + 3).wait()
        for h in range(HEADS):
            here = slice(h * HEAD_DIM, (h + 1) * HEAD_DIM)
            o_t[s, here] = o_t[s, here] / norm[s, h]
            lse[s, h] = top[s, h] + jnp.log(norm[s, h])
        attn_t[s] = o_t[s].astype(BF)
        branch = mm(attn_t[s].T, wo[...])
        position = z * rows + lax.broadcasted_iota(jnp.int32, (rows, 1), 0)
        live = (position < lens[s]).astype(F32)
        live_branch[s] = live * branch
        resid[...] = x_all[s, z].astype(F32) + alpha_attn * live_branch[s]
        resid_bf[...] = resid[...].astype(BF)
        resid_t[...] = resid_bf[...].T

    def start_feed_forward(s):
        if s == 0:
            for i in (4, 5, 6):
                load(seqs + i).wait()
        grad_out = cot[s].astype(F32)
        grad_ffn[...] = (alpha_ffn * grad_out).astype(BF)
        ffn[...] = jnp.zeros_like(ffn)
        grad_x[s] = grad_out
        small[0, ff_cols : ff_cols + 1] += jnp.sum(
            grad_ffn[...].astype(F32), axis=0, keepdims=True
        )

    def column(s, c):
        lanes = slice(c * width, (c + 1) * width)
        hidden = mm(resid_bf[...], w_in[:, lanes]) + b_in[:, lanes]
        square = hidden * hidden
        half = 0.5 + 0.5 * jnp.tanh(hidden * (GELU_A + GELU_B * square))
        product = hidden * half
        act = product.astype(BF)
        slope = half + product * (1.0 - half) * (2 * GELU_A + 6 * GELU_B * square)
        back = w_back[lanes]
        ffn[...] += mm(act, back)
        grad_hidden = (mm_nt(grad_ffn[...], back) * slope).astype(BF)
        small[0, c : c + 1] += jnp.sum(grad_hidden.astype(F32), axis=0, keepdims=True)
        grad_x[s] += mm_nt(grad_hidden, w_in[:, lanes])
        grad_back = mm(act.T, grad_ffn[...])
        grad_in = mm(resid_t[...], grad_hidden)
        upper, lower = slice(0, width), slice(width, 2 * width)
        if s > 0:
            grad_back += grads[c, upper].astype(F32)
            grad_in += grads[c, lower].astype(F32)
        grads[c, upper] = grad_back.astype(BF)
        grads[c, lower] = grad_in.astype(BF)

    def end_feed_forward(s):
        ffn_out = ffn[...] + b_back[...]
        outputs[s] = (resid[...] + alpha_ffn * ffn_out).astype(BF)
        small[0, ff_cols + 2 : ff_cols + 3] += jnp.sum(
            cot[s].astype(F32) * ffn_out, axis=0, keepdims=True
        )
        small[0, ff_cols + 1 : ff_cols + 2] += jnp.sum(
            grad_x[s] * live_branch[s], axis=0, keepdims=True
        )

    def add_to(k, value, s):
        if s == 0:
            acc[k] = value
        else:
            acc[k] += value

    def start_back(s):
        position = z * rows + lax.broadcasted_iota(jnp.int32, (rows, 1), 0)
        live = (position < lens[s]).astype(F32)
        grad_branch = (alpha_attn * live * grad_x[s]).astype(BF)
        add_to(0, mm(attn_t[s], grad_branch), s)
        do = mm_nt(grad_branch, wo[...]).astype(BF)
        split_heads(do, do_m)
        do_t[...] = mm_nt(wo[...], grad_branch).astype(BF)
        for h in range(HEADS):
            here = slice(h * HEAD_DIM, (h + 1) * HEAD_DIM)
            delta[h] = jnp.sum(do_t[here].astype(F32) * o_t[s, here], axis=0, keepdims=True)
        dq_t[...] = jnp.zeros_like(dq_t)
        if s == 0:
            acc[2] = jnp.zeros_like(acc[2])
            acc[3] = jnp.zeros_like(acc[3])

        @pl.when(has_up)
        def _():
            def sent(j, carry):
                x_copy(s, j).wait_send()
                return carry

            lax.fori_loop(0, z + 1, sent, 0)

    def block(s, j):
        here = slot(s, j)
        if not keep:
            project(s, j)
        mask = allowed(s, j)

        for head in range(HEADS):
            p, half = head // 2, slice(head % 2 * rows, (head % 2 + 1) * rows)
            lanes = slice(p * PAIR, (p + 1) * PAIR)
            scores = mm_nt(k_all[here, :, lanes], q_m[s, p, half])
            probs = jnp.where(mask, jnp.exp(scores - lse[s, head]), 0.0)
            grad_probs = mm_nt(v_all[here, :, lanes], do_m[p, half])
            prob_bf[p, :, half] = probs.astype(BF)
            grad_bf[p, :, half] = (probs * (grad_probs - delta[head])).astype(BF)
        for p in range(pairs):
            lanes = slice(p * PAIR, (p + 1) * PAIR)
            dv[:, lanes] = mm(prob_bf[p], do_m[p]).astype(BF)
            dk[:, lanes] = mm(grad_bf[p], q_m[s, p]).astype(BF)
            for h in (0, 1):
                own = slice(p * PAIR + h * HEAD_DIM, p * PAIR + (h + 1) * HEAD_DIM)
                dq_t[own] += mm(k_t[here, own], grad_bf[p, :, h * rows : (h + 1) * rows])
        part = mm_nt(dk[...], wk[...]) + mm_nt(dv[...], wv[...])
        acc[2] += mm(x_t[here], dk[...])
        acc[3] += mm(x_t[here], dv[...])

        @pl.when(j < z)
        def _():
            x_all[s, j] = part.astype(BF)

        @pl.when(j == z)
        def _():
            grad_x[s] += part

    def send_part(s, j):
        @pl.when(jnp.logical_not(has_up) & (j < z))
        def _():
            r_copy(s, j, x_all).start()

    def end_back(s):
        dq = (dq_t[...] * 0.125).T.astype(BF)
        if not keep:
            x_t[0] = x_all[s, z].T
        add_to(1, mm(x_t[slot(s, z)], dq), s)
        grad_x[s] += mm_nt(dq, wq[...])

    def pass_back(s, hop, j):
        @pl.when(z == n - 2 - hop)
        def _():
            r_copy(s, j, back_in).wait_recv()

            @pl.when(j < z)
            def _():
                back_in[s, j] = back_in[s, j] + x_all[s, j]
                r_copy(s, j, back_in).start()

    def finish_input(s):
        @pl.when(has_up)
        def _():
            grad_input[s] = (grad_x[s] + back_in[s, z].astype(F32)).astype(BF)

        @pl.when(jnp.logical_not(has_up))
        def _():
            grad_input[s] = grad_x[s].astype(BF)

    def small_bit(i):
        return pltpu.make_async_remote_copy(
            src_ref=small.at[i], dst_ref=small_land.at[i],
            send_sem=small_send.at[i], recv_sem=small_recv.at[i],
            device_id=plan.partner(*plane[i]), device_id_type=MESH,
        )

    def small_to(d):
        sem = len(plane) + d - 1
        return pltpu.make_async_remote_copy(
            src_ref=small.at[len(plane)], dst_ref=small_line.at[z],
            send_sem=small_send.at[sem], recv_sem=small_recv.at[sem],
            device_id=(b, (z + d) % n), device_id_type=MESH,
        )

    def small_step(i):
        if i > 0:
            small_bit(i - 1).wait()
            small[i] = small[i - 1] + small_land[i - 1]
        if i < len(plane):
            small_bit(i).start()
        else:
            for d in range(1, n):
                small_to(d).start()

    def small_end():
        for d in range(1, n):
            small_to(d).wait()
        small_line[z] = small[len(plane)]
        value = small_line[0]
        for d in range(1, n):
            value = value + small_line[d]
        small_out[...] = value

    def store(c):
        return pltpu.make_async_copy(total.at[c], total_out.at[c], store_sem.at[c])

    def sum_stage(k, c):
        if k == 0 and c >= ff_cols:
            for i in (0, 1):
                part = acc[2 * (c - ff_cols) + i]
                grads[c, i * width : (i + 1) * width] = part.astype(BF)
        plan.stage(k, c)
        if k == plan.stages - 1:
            store(c).start()

    def loop(f, count):
        def body(j, carry):
            f(j)
            return carry

        lax.fori_loop(0, count, body, 0)

    steps = {
        "attention": attention, "start_ff": start_feed_forward, "column": column, "end_ff": end_feed_forward,
        "start_back": start_back, "block": block, "end_back": end_back, "send": send_part,
        "pass": pass_back, "sum": sum_stage, "small": small_step,
    }

    for s in range(seqs):
        start_seq(s)

    @pl.when(z == 0)
    def _():
        send_own(1)

    attention(0)
    start_feed_forward(0)
    for c in range(ff_cols):
        if c % 2 == 0 and c // 2 < early:
            @pl.when((z > c // 2) & has_up)
            def _():
                pass_on(1, z - c // 2 - 1)
        column(0, c)
    end_feed_forward(0)
    if n == 4 and ff_cols == 4 and plan.stages == 9:
        for name, *what in ORDER:
            if name == "block":
                @pl.when(what[1] <= z)
                def _():
                    block(*what)
            else:
                steps[name](*what)
    else:
        for s in range(seqs):
            if s > 0:
                attention(s)
                start_feed_forward(s)
                for c in range(ff_cols):
                    column(s, c)
                end_feed_forward(s)
            start_back(s)
            loop(functools.partial(block, s), z + 1)
            end_back(s)
            loop(functools.partial(send_part, s), z)
        for s in range(seqs):
            for hop in range(n - 1):
                loop(functools.partial(pass_back, s, hop), n - 1 - hop)
        for i in range(len(plane) + 1):
            small_step(i)
        for t in range(plan.stages + chunks - 1):
            for k in range(plan.stages - 1, -1, -1):
                if 0 <= t - k < chunks:
                    sum_stage(k, t - k)
    for s in range(seqs):
        finish_input(s)
    small_end()
    for c in range(chunks):
        store(c).wait()

    @pl.when(has_down)
    def _():
        for s in range(seqs):
            loop(lambda j: r_copy(s, j, back_in).wait_send(), z)


def expand_kernel(
    cols, total, small, outputs_in, input_in,
    back, w_in, out, query, key, value, outputs, grad_input, b_in, b_back, alpha_attn, alpha_ffn,
):
    width = total.shape[2]
    i = pl.program_id(0)
    upper, lower = total[0, :width].astype(F32), total[0, width:].astype(F32)

    @pl.when(i < cols)
    def _():
        back[...] = upper
        w_in[...] = lower

    @pl.when(i == 0)
    def _():
        outputs[...] = outputs_in[...]
        grad_input[...] = input_in[...]
        for c in range(cols):
            b_in[:, c * width : (c + 1) * width] = small[c : c + 1]
        b_back[...] = small[cols : cols + 1]
        alpha_attn[0] = jnp.sum(small[cols + 1 : cols + 2])
        alpha_ffn[0] = jnp.sum(small[cols + 2 : cols + 3])

    @pl.when(i == cols)
    def _():
        out[...] = upper
        query[...] = lower

    @pl.when(i == cols + 1)
    def _():
        key[...] = upper
        value[...] = lower


def expand(total, small, outputs, grad_input, ff):
    width = total.shape[2]
    cols = ff // width
    whole = pl.BlockSpec(outputs.shape, lambda i: (0, 0, 0))
    one = pl.BlockSpec((width, width), lambda i: (0, 0))
    square = jax.ShapeDtypeStruct((width, width), F32)
    scalar = jax.ShapeDtypeStruct((1,), F32)
    smem = pl.BlockSpec(memory_space=pltpu.SMEM)
    return pl.pallas_call(
        functools.partial(expand_kernel, cols),
        grid=(cols + 2,),
        out_shape=(
            jax.ShapeDtypeStruct((ff, width), F32),
            jax.ShapeDtypeStruct((width, ff), F32),
            square, square, square, square,
            jax.ShapeDtypeStruct(outputs.shape, BF),
            jax.ShapeDtypeStruct(outputs.shape, BF),
            jax.ShapeDtypeStruct((1, ff), F32),
            jax.ShapeDtypeStruct((1, width), F32),
            scalar, scalar,
        ),
        in_specs=[
            pl.BlockSpec((1, 2 * width, width), lambda i: (i, 0, 0)),
            pl.BlockSpec(small.shape, lambda i: (0, 0)),
            whole, whole,
        ],
        out_specs=(
            pl.BlockSpec((width, width), lambda i: (jnp.minimum(i, cols - 1), 0)),
            pl.BlockSpec((width, width), lambda i: (0, jnp.minimum(i, cols - 1))),
            one, one, one, one, whole, whole,
            pl.BlockSpec((1, ff), lambda i: (0, 0)),
            pl.BlockSpec((1, width), lambda i: (0, 0)),
            smem, smem,
        ),
        name="expand",
        compiler_params=pltpu.CompilerParams(vmem_limit_bytes=63 << 20),
    )(total, small, outputs, grad_input)


def per_device(
    tokens, lengths, w_query, w_key, w_value, w_out, w_in, b_in, w_back, b_back,
    alpha_attn, alpha_ffn, cotangent,
):
    seqs, rows, width = tokens.shape
    ff = w_in.shape[1]
    nb, n = lax.axis_size("batch"), lax.axis_size("blk")
    keep = n <= 4
    slots = seqs * n if keep else 1
    ff_cols = ff // width
    chunks = ff_cols + 2
    plan = Reducer(nb, n, 2 * width)
    steps = nb.bit_length() - 1
    small_rows = -(-(ff_cols + 3) // 8) * 8
    vmem = pl.BlockSpec(memory_space=pltpu.VMEM)
    smem = pl.BlockSpec(memory_space=pltpu.SMEM)
    hbm = pl.BlockSpec(memory_space=pl.ANY)
    square = (rows, width)
    dma = pltpu.SemaphoreType.DMA
    outputs, grad_input, total, small = pl.pallas_call(
        functools.partial(layer_kernel, plan, n, keep),
        out_shape=(
            jax.ShapeDtypeStruct(tokens.shape, BF),
            jax.ShapeDtypeStruct(tokens.shape, BF),
            jax.ShapeDtypeStruct((chunks, 2 * width, width), BF),
            jax.ShapeDtypeStruct((small_rows, width), F32),
        ),
        in_specs=[smem] * 3 + [vmem] * 2 + [hbm] * 8,
        out_specs=(vmem, vmem, hbm, vmem),
        scratch_shapes=[
            pltpu.VMEM(tokens.shape, BF),
            pltpu.VMEM((width, width), BF), pltpu.VMEM((width, width), BF),
            pltpu.VMEM((width, width), BF), pltpu.VMEM((width, width), BF),
            pltpu.VMEM(w_in.shape, BF), pltpu.VMEM(w_back.shape, BF),
            dma((seqs + 7,)),
            pltpu.VMEM((seqs, n) + square, BF),
            pltpu.VMEM((width, width), BF),
            pltpu.VMEM((width, width), BF),
            pltpu.VMEM((slots, width, rows), BF),
            pltpu.VMEM((slots,) + square, BF),
            pltpu.VMEM((slots,) + square, BF),
            pltpu.VMEM((slots, width, rows), BF),
            pltpu.VMEM((slots, width, rows), BF),
            pltpu.VMEM((seqs, HEADS // 2, 2 * rows, PAIR), BF),
            pltpu.VMEM((HEADS // 2, 2 * rows, PAIR), BF),
            pltpu.VMEM((HEADS, rows, rows), F32),
            pltpu.VMEM((HEADS // 2, rows, 2 * rows), BF),
            pltpu.VMEM((HEADS // 2, rows, 2 * rows), BF),
            pltpu.VMEM((seqs, HEADS, 1, rows), F32),
            pltpu.VMEM((seqs, HEADS, 1, rows), F32),
            pltpu.VMEM((seqs, width, rows), F32),
            pltpu.VMEM((seqs, width, rows), BF),
            pltpu.VMEM((width, rows), BF),
            pltpu.VMEM((seqs,) + square, F32),
            pltpu.VMEM(square, F32),
            pltpu.VMEM(square, BF),
            pltpu.VMEM((width, rows), BF),
            pltpu.VMEM(square, BF),
            pltpu.VMEM(square, F32),
            pltpu.VMEM((seqs,) + square, F32),
            pltpu.VMEM((seqs, HEADS, 1, rows), F32),
            pltpu.VMEM((HEADS, 1, rows), F32),
            pltpu.VMEM((width, rows), F32),
            pltpu.VMEM(square, BF),
            pltpu.VMEM(square, BF),
            pltpu.VMEM((4, width, width), F32),
            pltpu.VMEM((seqs, n) + square, BF),
            dma((seqs, n)), dma((seqs, n)), dma((seqs, n)), dma((seqs, n)),
            pltpu.VMEM((chunks, 2 * width, width), BF),
            pltpu.VMEM((chunks, 2 * width, width), BF),
            dma((chunks,)),
        ]
        + plan.scratch(chunks, width)
        + [
            pltpu.VMEM((steps + 1, small_rows, width), F32),
            pltpu.VMEM((steps, small_rows, width), F32),
            pltpu.VMEM((n, small_rows, width), F32),
            dma((steps + n - 1,)),
            dma((steps + n - 1,)),
        ],
        name="layer",
        compiler_params=pltpu.CompilerParams(
            collective_id=0, has_side_effects=True, vmem_limit_bytes=63 << 20
        ),
    )(
        lengths, alpha_attn.reshape(1), alpha_ffn.reshape(1), b_in.reshape(1, ff),
        b_back.reshape(1, width), tokens, cotangent, w_query, w_key, w_value, w_out, w_in, w_back,
    )
    back, grad_in, out, query, key, value, outputs, grad_input, b_in, b_back, attn, ffn = expand(
        total, small, outputs, grad_input, ff
    )
    return (
        outputs, grad_input, query, key, value, out, grad_in, b_in.reshape(ff), back,
        b_back.reshape(width), attn.reshape(()), ffn.reshape(()),
    )


def solution(mesh):
    return jax.shard_map(
        per_device,
        mesh=mesh,
        in_specs=(
            P("batch", "blk", None),
            P("batch"),
            P(),
            P(),
            P(),
            P(),
            P(),
            P(),
            P(),
            P(),
            P(),
            P(),
            P("batch", "blk", None),
        ),
        out_specs=(
            P("batch", "blk", None),
            P("batch", "blk", None),
            P(),
            P(),
            P(),
            P(),
            P(),
            P(),
            P(),
            P(),
            P(),
            P(),
        ),
        check_vma=False,
    )
```

```python
import functools

import jax
import jax.numpy as jnp
from jax import lax
from jax.experimental import pallas as pl
from jax.experimental.pallas import tpu as pltpu
from jax.sharding import PartitionSpec as P

HEADS = 8
HEAD_DIM = 64
PAIR = 2 * HEAD_DIM
MESH = pl.DeviceIdType.MESH
BF = jnp.bfloat16
F32 = jnp.float32
NEG = -1e30
GELU_A = 0.7978845608
GELU_B = 0.7978845608 * 0.044715

ORDER = (
    ("start_back", 0), ("block", 0, 0), ("block", 0, 1), ("send", 0, 0), ("attention", 1), ("start_ff", 1),
    ("column", 1, 0), ("sum", 0, 0), ("send", 0, 1), ("sum", 0, 1), ("column", 1, 1),
    ("end_ff", 1), ("small", 0), ("sum", 1, 1), ("sum", 0, 3), ("block", 0, 2), ("sum", 1, 0),
    ("block", 0, 3), ("send", 0, 2), ("sum", 0, 2), ("pass", 0, 0, 0), ("sum", 2, 1), ("end_back", 0),
    ("start_back", 1), ("sum", 1, 3), ("block", 1, 0), ("small", 1), ("sum", 1, 2), ("sum", 3, 1), ("pass", 0, 1, 0),
    ("send", 1, 0), ("pass", 0, 0, 1), ("block", 1, 1), ("sum", 2, 0), ("block", 1, 2), ("small", 2), ("sum", 2, 3),
    ("block", 1, 3), ("small", 3), ("sum", 2, 2), ("sum", 3, 0), ("sum", 3, 2), ("pass", 0, 0, 2), ("sum", 4, 1),
    ("end_back", 1), ("sum", 0, 4), ("sum", 3, 3), ("sum", 0, 5), ("sum", 1, 4), ("sum", 4, 0), ("sum", 1, 5),
    ("sum", 5, 1), ("sum", 4, 2), ("sum", 2, 4), ("send", 1, 2), ("sum", 2, 5), ("pass", 0, 2, 0), ("sum", 6, 1),
    ("sum", 5, 0), ("sum", 5, 2), ("sum", 3, 4), ("sum", 4, 3), ("pass", 0, 1, 1), ("sum", 3, 5), ("sum", 6, 0),
    ("sum", 4, 4), ("sum", 6, 2), ("sum", 5, 3), ("sum", 4, 5), ("sum", 7, 0), ("sum", 5, 4), ("send", 1, 1),
    ("sum", 7, 2), ("pass", 1, 0, 0), ("pass", 1, 0, 2), ("sum", 6, 3), ("sum", 5, 5), ("sum", 6, 4), ("sum", 8, 2),
    ("sum", 6, 5), ("sum", 7, 1), ("pass", 1, 0, 1), ("sum", 8, 0), ("pass", 1, 1, 0), ("sum", 7, 4), ("sum", 8, 1),
    ("sum", 7, 3), ("sum", 7, 5), ("sum", 8, 4), ("sum", 8, 3), ("pass", 1, 2, 0), ("sum", 8, 5), ("pass", 1, 1, 1),
)


class Reducer:
    def __init__(self, nb, nz, rows):
        self.rows, self.nz = rows, nz
        plane = [("batch", 1 << i) for i in range(1, nb.bit_length() - 1)]
        line = [("blk", 1 << i) for i in range(nz.bit_length() - 1)]
        self.all_bits = [("batch", 1)] + plane + line
        direct = (rows // 4 >> len(plane)) // nz >= 16
        steps = line if not direct else [("blk", 0)]
        self.orders = [plane + steps, plane[::-1] + steps]
        self.steps = len(self.orders[0])
        self.kinds, self.sizes, self.lands = [], [], [[], []]
        self.messages = []
        length, land = rows // 4, rows // 2
        for axis, bit in self.orders[0]:
            if bit == 0:
                kind, length, messages = "direct", length // nz, nz - 1
            elif length >= 32:
                kind, length, messages = "half", length // 2, 1
            else:
                kind, messages = "full", 1
            self.kinds.append(kind)
            self.sizes.append(length)
            self.messages.append(messages)
            for o in (0, 1):
                self.lands[o].append(land)
                land += length * messages
        self.land_rows = land
        self.back_steps = [i for i in range(self.steps) if self.kinds[i] != "full"][::-1]
        self.stages = 3 + self.steps + len(self.back_steps)

    def scratch(self, chunks, width):
        return [
            pltpu.VMEM((chunks, self.land_rows, width), BF),
            pltpu.SemaphoreType.DMA((chunks, self.stages - 1)),
            pltpu.SemaphoreType.DMA((chunks, self.stages - 1)),
        ]

    def bind(self, grads, total, land, send_sem, recv_sem):
        self.grads, self.total, self.land = grads, total, land
        self.send_sem, self.recv_sem = send_sem, recv_sem
        self.at = {"batch": lax.axis_index("batch"), "blk": lax.axis_index("blk")}
        core = self.at["batch"] % 2
        half = self.rows // 2
        self.core_keep, self.core_send = core * half, (1 - core) * half
        self.start, self.keep, self.send = [[], []], [[], []], [[], []]
        for o in (0, 1):
            off = self.core_keep + o * (half // 2)
            for i, (axis, bit) in enumerate(self.orders[o]):
                size, here = self.sizes[i], self.at[axis]
                self.start[o].append(off)
                if self.kinds[i] == "half":
                    mine = (here // bit) % 2
                    self.keep[o].append(off + mine * size)
                    self.send[o].append(off + (1 - mine) * size)
                elif self.kinds[i] == "direct":
                    self.keep[o].append(off + here * size)
                    self.send[o].append(None)
                else:
                    self.keep[o].append(off)
                    self.send[o].append(off)
                off = self.keep[o][-1]

    def partner(self, axis, bit):
        mine = (self.at[axis] // bit) % 2
        there = self.at[axis] + bit * (1 - 2 * mine)
        if axis == "batch":
            return (there, self.at["blk"])
        return (self.at["batch"], there)

    def copy(self, c, src, src_row, dst, dst_row, size, sem, device):
        return pltpu.make_async_remote_copy(
            src_ref=src.at[c, pl.ds(pl.multiple_of(src_row, 16), size)],
            dst_ref=dst.at[c, pl.ds(pl.multiple_of(dst_row, 16), size)],
            send_sem=self.send_sem.at[c, sem],
            recv_sem=self.recv_sem.at[c, sem],
            device_id=device,
            device_id_type=MESH,
        )

    def core_out(self, c):
        there = self.partner("batch", 1)
        return self.copy(c, self.grads, self.core_send, self.land, 0, self.rows // 2, 0, there)

    def core_back(self, c):
        there, row, sem = self.partner("batch", 1), self.core_keep, self.stages - 2
        return self.copy(c, self.total, row, self.total, row, self.rows // 2, sem, there)

    def start_out(self, c, i):
        size = self.sizes[i]
        for o in (0, 1):
            axis, bit = self.orders[o][i]
            land = self.lands[o][i]
            if self.kinds[i] != "direct":
                there = self.partner(axis, bit)
                self.copy(c, self.grads, self.send[o][i], self.land, land, size, i + 1, there).start()
                continue
            for d in range(1, self.nz):
                there = (self.at["blk"] + d) % self.nz
                row, peer = self.start[o][i] + there * size, (self.at["batch"], there)
                self.copy(
                    c, self.grads, row, self.land, land + (d - 1) * size, size, i + 1, peer
                ).start()

    def start_back(self, c, place):
        i, sem = self.back_steps[place], self.steps + 1 + place
        for o in (0, 1):
            axis, bit = self.orders[o][i]
            size, row = self.sizes[i], self.keep[o][i]
            peers = [self.partner(axis, bit)]
            if self.kinds[i] == "direct":
                peers = [(self.at["batch"], (self.at["blk"] + d) % self.nz) for d in range(1, self.nz)]
            for peer in peers:
                self.copy(c, self.total, row, self.total, row, size, sem, peer).start()

    def wait(self, c, ref, i, sem):
        rows = 2 * self.sizes[i] * self.messages[i]
        every = self.copy(c, ref, 0, ref, 0, rows, sem, self.partner("batch", 1))
        every.wait_send()
        every.wait_recv()

    def add(self, c, row, land_row, size, pieces=1, last=False):
        part = min(size, 64)
        target = self.total if last else self.grads

        def body(k, carry):
            here = pl.ds(pl.multiple_of(row + k * part, 16), part)
            value = self.grads[c, here]
            if pieces > 1:
                value = value.astype(F32)
            for d in range(pieces):
                there = pl.ds(pl.multiple_of(land_row + d * size + k * part, 16), part)
                value = value + self.land[c, there].astype(value.dtype)
            target[c, here] = value.astype(BF)
            return carry

        lax.fori_loop(0, size // part, body, 0)

    def stage(self, k, c):
        if k == 0:
            self.core_out(c).start()
            return
        if k == 1:
            self.core_out(c).wait()
            self.add(c, self.core_keep, 0, self.rows // 2)
        elif k <= self.steps + 1:
            i = k - 2
            self.wait(c, self.land, i, k - 1)
            pieces = self.nz - 1 if self.kinds[i] == "direct" else 1
            last = i == self.steps - 1
            for o in (0, 1):
                self.add(c, self.keep[o][i], self.lands[o][i], self.sizes[i], pieces, last)
        elif k < self.stages - 1:
            self.wait(c, self.total, self.back_steps[k - self.steps - 2], k - 1)
        else:
            self.core_back(c).wait()
            return
        if k <= self.steps:
            self.start_out(c, k - 1)
        elif k < self.stages - 2:
            self.start_back(c, k - self.steps - 1)
        else:
            self.core_back(c).start()


def mm(left, right):
    return jnp.dot(left, right, preferred_element_type=F32)


def mm_nt(left, right):
    return lax.dot_general(left, right, (((1,), (1,)), ((), ())), preferred_element_type=F32)


def mm_tn(left, right):
    return lax.dot_general(left, right, (((0,), (0,)), ((), ())), preferred_element_type=F32)


def default_order(stages, n, ff_cols, chunks, plane_bits):
    order = [("start_back", 0)] + [("block", 0, j) for j in range(n)] + [("end_back", 0)]
    order += [("attention", 1), ("start_ff", 1)] + [("column", 1, c) for c in range(ff_cols // 2)] + [("end_ff", 1)]
    order += [("start_back", 1)] + [("block", 1, j) for j in range(n)] + [("end_back", 1)]
    order += [("sends", 0), ("sends", 1)]
    order += [("passes", s, hop) for s in (0, 1) for hop in range(n - 1)]
    order += [("small", i) for i in range(plane_bits + 1)]
    for t in range(stages + chunks - 1):
        order += [("sum", k, t - k) for k in range(stages - 1, -1, -1) if 0 <= t - k < chunks]
    return order


def layer_kernel(plan, n, keep, lens, alpha_attn_ref, alpha_ffn_ref, b_in, b_back, *refs):
    (
        tokens_hbm, cot_hbm, wq_hbm, wk_hbm, wv_hbm, wo_hbm, w_in_hbm, w_back_hbm,
        outputs, grad_input, total_out, small_out,
        cot, wq, wk, wv, wo, w_in, w_back, load_sem,
        x_all, wk_t, wv_t, x_t, k_all, v_all, k_t, v_t, q_m, do_m, score, prob_bf, grad_bf, top, norm, o_t, attn_t, do_t,
        live_branch, resid, resid_bf, resid_t, grad_ffn, ffn, grad_x, lse, delta,
        dq_t, dk, dv, acc, back_in,
        x_send, x_recv, r_send, r_recv,
        grads, total, store_sem, land, send_sem, recv_sem, small, small_land, small_line, small_send, small_recv,
    ) = refs
    seqs, _, rows, width = x_all.shape
    chunks = grads.shape[0]
    ff_cols = w_in.shape[1] // width
    pairs = width // PAIR
    plan.bind(grads, total, land, send_sem, recv_sem)
    b, z = lax.axis_index("batch"), lax.axis_index("blk")
    has_up, has_down = z < n - 1, z > 0
    alpha_attn, alpha_ffn = alpha_attn_ref[0], alpha_ffn_ref[0]

    def loop(f, count):
        def body(j, carry):
            f(j)
            return carry

        lax.fori_loop(0, count, body, 0)

    def load(i):
        if i < seqs:
            return pltpu.make_async_copy(tokens_hbm.at[i], x_all.at[i, z], load_sem.at[i])
        pairs_of = [
            (wk_hbm, wk), (wv_hbm, wv), (wq_hbm, wq), (wo_hbm, wo),
            (w_in_hbm, w_in), (w_back_hbm, w_back), (cot_hbm, cot),
        ]
        src, dst = pairs_of[i - seqs]
        return pltpu.make_async_copy(src, dst, load_sem.at[i])

    for i in range(seqs + 7):
        load(i).start()

    def x_copy(s, j, h):
        here = pl.ds(h * (rows // 2), rows // 2)
        return pltpu.make_async_remote_copy(
            src_ref=x_all.at[s, j, here], dst_ref=x_all.at[s, j, here],
            send_sem=x_send.at[s, j, h], recv_sem=x_recv.at[s, j, h],
            device_id=(b, z + 1), device_id_type=MESH,
        )

    def r_copy(s, j, src):
        return pltpu.make_async_remote_copy(
            src_ref=src.at[s, j], dst_ref=back_in.at[s, j],
            send_sem=r_send.at[s, j], recv_sem=r_recv.at[s, j],
            device_id=(b, z - 1), device_id_type=MESH,
        )

    barrier = pltpu.get_barrier_semaphore()
    plane = [(axis, bit) for axis, bit in plan.all_bits if axis == "batch"]
    peers = [plan.partner(axis, bit) for axis, bit in plane] + [(b, (z + d) % n) for d in range(1, n)]
    for peer in peers:
        pl.semaphore_signal(barrier, inc=1, device_id=peer, device_id_type=MESH)
    pl.semaphore_wait(barrier, len(peers))

    def send_own(s):
        @pl.when(has_up)
        def _():
            for h in (0, 1):
                x_copy(s, z, h).start()

    for s in range(seqs):
        load(s).wait()
        if s == 0:
            send_own(0)

    load(seqs).wait()
    wk_t[...] = wk[...].T
    load(seqs + 1).wait()
    wv_t[...] = wv[...].T
    small[0] = jnp.zeros_like(small[0])
    low_lanes = lax.broadcasted_iota(jnp.int32, (rows, PAIR), 1) < HEAD_DIM
    key_iota = lax.broadcasted_iota(jnp.int32, (rows, rows), 0)
    query_pos = z * rows + lax.broadcasted_iota(jnp.int32, (1, rows), 1)

    def split_heads(value, target):
        for h in range(HEADS):
            pair = value[:, (h // 2) * PAIR : (h // 2 + 1) * PAIR]
            mask = low_lanes if h % 2 == 0 else jnp.logical_not(low_lanes)
            target[h // 2, h % 2 * rows : (h % 2 + 1) * rows] = jnp.where(mask, pair, 0.0).astype(BF)

    def slot(s, j):
        return s * n + j if keep else 0

    def forward_slot(s, j):
        return jnp.where((s > 0) & (j == z), n, j) if keep else 0

    def project(s, j):
        here, front = slot(s, j), forward_slot(s, j)
        x = x_all[s, j]
        k_all[front] = mm(x, wk[...]).astype(BF)
        v_all[here] = mm(x, wv[...]).astype(BF)
        k_t[here] = mm_nt(wk_t[...], x).astype(BF)
        v_t[front] = mm_nt(wv_t[...], x).astype(BF)

    def allowed(s, j):
        limit = jnp.minimum(query_pos + 1, lens[s]) - j * rows
        return key_iota < limit

    def scores_of(s, j, head, mask):
        p, half = head // 2, slice(head % 2 * rows, (head % 2 + 1) * rows)
        keys = k_all[forward_slot(s, j), :, p * PAIR : (p + 1) * PAIR]
        return jnp.where(mask, mm_nt(keys, q_m[s, p, half]), NEG)

    def statistics(s, j):
        mask = allowed(s, j)
        for head in range(HEADS):
            score[head] = scores_of(s, j, head, mask)
        for head in range(HEADS):
            old = top[s, head]
            new = jnp.maximum(old, jnp.max(score[head], axis=0, keepdims=True))
            below = jnp.sum(jnp.exp(score[head] - new), axis=0, keepdims=True)
            norm[s, head] = norm[s, head] * jnp.exp(old - new) + below
            top[s, head] = new

    def probabilities(s, j):
        mask = allowed(s, j)
        for head in range(HEADS):
            p, half = head // 2, slice(head % 2 * rows, (head % 2 + 1) * rows)
            probs = jnp.exp(scores_of(s, j, head, mask) - lse[s, head])
            prob_bf[slot(s, j), p, :, half] = probs.astype(BF)

    def mix_values(s, j):
        if not keep:
            project(s, j)
        probabilities(s, j)
        for head in range(HEADS):
            p, half = head // 2, slice(head % 2 * rows, (head % 2 + 1) * rows)
            own = slice(head * HEAD_DIM, (head + 1) * HEAD_DIM)
            o_t[s, own] += mm(v_t[forward_slot(s, j), own], prob_bf[slot(s, j), p, :, half])

    def pass_on(s, j, h):
        x_copy(s, j, h).wait_recv()

        @pl.when(has_up)
        def _():
            x_copy(s, j, h).start()

    def start_seq(s):
        q = mm(x_all[s, z], wq[...]).astype(BF).astype(F32) * 0.125
        split_heads(q, q_m.at[s])
        top[s] = jnp.full_like(top[s], NEG)
        norm[s] = jnp.zeros_like(norm[s])
        o_t[s] = jnp.zeros_like(o_t[s])
        project(s, z)
        statistics(s, z)

    def attention(s):
        def block(i, carry):
            if s == 0:
                for h in (0, 1):
                    pass_on(s, z - i, h)
            else:
                @pl.when((2 * i > ff_cols) | jnp.logical_not(has_up))
                def _():
                    for h in (0, 1):
                        pass_on(s, z - i, h)
            project(s, z - i)
            statistics(s, z - i)
            return carry

        lax.fori_loop(1, z + 1, block, 0)
        if s == 0:
            @pl.when(z > 0)
            def _():
                send_own(1)

            load(seqs + 3).wait()
        lse[s] = top[s] + jnp.log(norm[s])
        loop(functools.partial(mix_values, s), z + 1)
        attn_t[s] = o_t[s].astype(BF)
        branch = mm(attn_t[s].T, wo[...])
        position = z * rows + lax.broadcasted_iota(jnp.int32, (rows, 1), 0)
        live = (position < lens[s]).astype(F32)
        live_branch[s] = live * branch
        resid[...] = x_all[s, z].astype(F32) + alpha_attn * live_branch[s]
        resid_bf[...] = resid[...].astype(BF)
        resid_t[...] = resid_bf[...].T

    def start_feed_forward(s):
        if s == 0:
            for i in (4, 5, 6):
                load(seqs + i).wait()
        grad_out = cot[s].astype(F32)
        grad_ffn[...] = (alpha_ffn * grad_out).astype(BF)
        ffn[...] = jnp.zeros_like(ffn)
        grad_x[s] = grad_out
        small[0, ff_cols : ff_cols + 1] += jnp.sum(
            grad_ffn[...].astype(F32), axis=0, keepdims=True
        )

    def column(s, c):
        lanes = pl.ds(pl.multiple_of(2 * c * width, 2 * width), 2 * width)
        hidden = mm(resid_bf[...], w_in[:, lanes]) + b_in[:, lanes]
        square = hidden * hidden
        half = 0.5 + 0.5 * jnp.tanh(hidden * (GELU_A + GELU_B * square))
        product = hidden * half
        act = product.astype(BF)
        slope = half + product * (1.0 - half) * (2 * GELU_A + 6 * GELU_B * square)
        back = w_back[lanes]
        ffn[...] += mm(act, back)
        grad_hidden = (mm_nt(grad_ffn[...], back) * slope).astype(BF)
        grad_bias = jnp.sum(grad_hidden.astype(F32), axis=0, keepdims=True)
        grad_x[s] += mm_nt(grad_hidden, w_in[:, lanes])
        grad_back = mm(act.T, grad_ffn[...])
        grad_in = mm(resid_t[...], grad_hidden)
        for i in (0, 1):
            chunk, part = 2 * c + i, slice(i * width, (i + 1) * width)
            upper, lower = grad_back[part], grad_in[:, part]
            if s > 0:
                upper += grads[chunk, :width].astype(F32)
                lower += grads[chunk, width:].astype(F32)
            grads[chunk, :width] = upper.astype(BF)
            grads[chunk, width:] = lower.astype(BF)
            small[0, pl.ds(chunk, 1)] += grad_bias[:, part]

    def end_feed_forward(s):
        ffn_out = ffn[...] + b_back[...]
        outputs[s] = (resid[...] + alpha_ffn * ffn_out).astype(BF)
        small[0, ff_cols + 2 : ff_cols + 3] += jnp.sum(
            cot[s].astype(F32) * ffn_out, axis=0, keepdims=True
        )
        small[0, ff_cols + 1 : ff_cols + 2] += jnp.sum(
            grad_x[s] * live_branch[s], axis=0, keepdims=True
        )

    def add_to(k, value, s):
        if s == 0:
            acc[k] = value
        else:
            acc[k] += value

    def start_back(s):
        position = z * rows + lax.broadcasted_iota(jnp.int32, (rows, 1), 0)
        live = (position < lens[s]).astype(F32)
        grad_branch = (alpha_attn * live * grad_x[s]).astype(BF)
        add_to(0, mm(attn_t[s], grad_branch), s)
        do = mm_nt(grad_branch, wo[...]).astype(BF)
        split_heads(do, do_m)
        do_t[...] = mm_nt(wo[...], grad_branch).astype(BF)
        for h in range(HEADS):
            here = slice(h * HEAD_DIM, (h + 1) * HEAD_DIM)
            delta[h] = jnp.sum(do_t[here].astype(F32) * o_t[s, here], axis=0, keepdims=True)
        dq_t[...] = jnp.zeros_like(dq_t)
        if s == 0:
            acc[2] = jnp.zeros_like(acc[2])
            acc[3] = jnp.zeros_like(acc[3])

        @pl.when(has_up)
        def _():
            def sent(j):
                for h in (0, 1):
                    x_copy(s, j, h).wait_send()

            loop(sent, z + 1)

    def block(s, j):
        here = slot(s, j)
        if not keep:
            project(s, j)
            probabilities(s, j)
        for head in range(HEADS):
            p, half = head // 2, slice(head % 2 * rows, (head % 2 + 1) * rows)
            grad_probs = mm_nt(v_all[here, :, p * PAIR : (p + 1) * PAIR], do_m[p, half])
            probs = prob_bf[here, p, :, half].astype(F32)
            grad_bf[p, :, half] = (probs * (grad_probs - delta[head])).astype(BF)
        for p in range(pairs):
            lanes = slice(p * PAIR, (p + 1) * PAIR)
            dv[:, lanes] = mm(prob_bf[here, p], do_m[p]).astype(BF)
            dk[:, lanes] = mm(grad_bf[p], q_m[s, p]).astype(BF)
            for h in (0, 1):
                own = slice(p * PAIR + h * HEAD_DIM, p * PAIR + (h + 1) * HEAD_DIM)
                dq_t[own] += mm(k_t[here, own], grad_bf[p, :, h * rows : (h + 1) * rows])
        part = mm_nt(dk[...], wk[...]) + mm_nt(dv[...], wv[...])
        x_t[...] = x_all[s, j].T
        acc[2] += mm(x_t[...], dk[...])
        acc[3] += mm(x_t[...], dv[...])

        @pl.when(j < z)
        def _():
            x_all[s, j] = part.astype(BF)

        @pl.when(j == z)
        def _():
            grad_x[s] += part

    def send_part(s, j):
        @pl.when(jnp.logical_not(has_up) & (j < z))
        def _():
            r_copy(s, j, x_all).start()

    def end_back(s):
        dq = (dq_t[...] * 0.125).T.astype(BF)
        x_t[...] = x_all[s, z].T
        add_to(1, mm(x_t[...], dq), s)
        grad_x[s] += mm_nt(dq, wq[...])

    def pass_back(s, hop, j):
        @pl.when(z == n - 2 - hop)
        def _():
            r_copy(s, j, back_in).wait_recv()

            @pl.when(j < z)
            def _():
                back_in[s, j] = back_in[s, j] + x_all[s, j]
                r_copy(s, j, back_in).start()

    def finish_input(s):
        @pl.when(has_up)
        def _():
            grad_input[s] = (grad_x[s] + back_in[s, z].astype(F32)).astype(BF)

        @pl.when(jnp.logical_not(has_up))
        def _():
            grad_input[s] = grad_x[s].astype(BF)

    def small_bit(i):
        return pltpu.make_async_remote_copy(
            src_ref=small.at[i], dst_ref=small_land.at[i],
            send_sem=small_send.at[i], recv_sem=small_recv.at[i],
            device_id=plan.partner(*plane[i]), device_id_type=MESH,
        )

    def small_to(d):
        sem = len(plane) + d - 1
        return pltpu.make_async_remote_copy(
            src_ref=small.at[len(plane)], dst_ref=small_line.at[z],
            send_sem=small_send.at[sem], recv_sem=small_recv.at[sem],
            device_id=(b, (z + d) % n), device_id_type=MESH,
        )

    def small_step(i):
        if i > 0:
            small_bit(i - 1).wait()
            small[i] = small[i - 1] + small_land[i - 1]
        if i < len(plane):
            small_bit(i).start()
        else:
            for d in range(1, n):
                small_to(d).start()

    def small_end():
        for d in range(1, n):
            small_to(d).wait()
        small_line[z] = small[len(plane)]
        value = small_line[0]
        for d in range(1, n):
            value = value + small_line[d]
        small_out[...] = value

    def store(c):
        return pltpu.make_async_copy(total.at[c], total_out.at[c], store_sem.at[c])

    def sum_stage(k, c):
        if k == 0 and c >= ff_cols:
            for i in (0, 1):
                part = acc[2 * (c - ff_cols) + i]
                grads[c, i * width : (i + 1) * width] = part.astype(BF)
        plan.stage(k, c)
        if k == plan.stages - 1:
            store(c).start()

    steps = {
        "attention": attention, "start_ff": start_feed_forward, "end_ff": end_feed_forward,
        "start_back": start_back, "block": block, "end_back": end_back, "send": send_part,
        "pass": pass_back, "sum": sum_stage, "small": small_step,
        "sends": lambda s: loop(functools.partial(send_part, s), z),
        "passes": lambda s, hop: loop(functools.partial(pass_back, s, hop), n - 1 - hop),
    }

    load(seqs + 2).wait()
    loop(start_seq, seqs)

    @pl.when(z == 0)
    def _():
        send_own(1)

    attention(0)
    start_feed_forward(0)

    def first_column(c):
        @pl.when((z > c) & has_up)
        def _():
            for h in (0, 1):
                pass_on(1, z - c - 1, h)

        column(0, c)

    loop(first_column, ff_cols // 2)
    end_feed_forward(0)

    if n == 4 and ff_cols == 4 and plan.stages == 9 and seqs == 2:
        order = ORDER
    else:
        order = default_order(plan.stages, n, ff_cols, chunks, len(plane))

    def run(step):
        @pl.when(z >= 0)
        def _():
            steps[step[0]](*step[1:])

    def run_between(group):
        at = [i for i, step in enumerate(group) if step[0] == "column"]
        if not at:
            for step in group:
                run(step)
            return
        for step in group[: at[0]]:
            run(step)

        def one(c):
            column(seqs - 1, c)
            for k in range(ff_cols // 2 - 1):
                inside = group[at[k] + 1 : at[k + 1]]
                if inside:
                    @pl.when(c == k)
                    def _():
                        for step in inside:
                            run(step)

        loop(one, ff_cols // 2)
        for step in group[at[-1] + 1 :]:
            run(step)

    at = [i for i, step in enumerate(order) if step[0] == "block"]
    for step in order[: at[0]]:
        run(step)

    def one_block(t):
        s, j = t // n, t % n

        @pl.when(j <= z)
        def _():
            block(s, j)

        for k in range(len(at) - 1):
            group = order[at[k] + 1 : at[k + 1]]
            if group:
                @pl.when(t == k)
                def _():
                    run_between(group)

    loop(one_block, len(at))
    for step in order[at[-1] + 1 :]:
        run(step)
    for s in range(seqs):
        finish_input(s)
    small_end()
    for c in range(chunks):
        store(c).wait()

    @pl.when(has_down)
    def _():
        for s in range(seqs):
            loop(lambda j: r_copy(s, j, back_in).wait_send(), z)


def expand_kernel(
    cols, total, small, outputs_in, input_in,
    back, w_in, out, query, key, value, outputs, grad_input, b_in, b_back, alpha_attn, alpha_ffn,
    half, full, through, load_sem, store_sem, pass_sem,
):
    chunks, _, width = half.shape
    loads = [pltpu.make_async_copy(total.at[c], half.at[c], load_sem.at[c]) for c in range(chunks)]
    for one in loads:
        one.start()
    arrivals = [
        pltpu.make_async_copy(outputs_in, through.at[0], pass_sem.at[0]),
        pltpu.make_async_copy(input_in, through.at[1], pass_sem.at[1]),
    ]
    for one in arrivals:
        one.start()
    places = []
    for c in range(cols):
        here = pl.ds(c * width, width)
        places.append((back.at[here], w_in.at[:, here]))
    places += [(out, query), (key, value)]
    stores = []
    for c in range(chunks):
        loads[c].wait()
        for i in (0, 1):
            full[c, i] = half[c, i * width : (i + 1) * width].astype(F32)
            stores.append(pltpu.make_async_copy(full.at[c, i], places[c][i], store_sem.at[c, i]))
            stores[-1].start()
    for c in range(cols):
        b_in[:, c * width : (c + 1) * width] = small[c : c + 1]
    b_back[...] = small[cols : cols + 1]
    alpha_attn[...] = jnp.sum(small[cols + 1 : cols + 2], axis=1, keepdims=True)
    alpha_ffn[...] = jnp.sum(small[cols + 2 : cols + 3], axis=1, keepdims=True)
    for i, target in enumerate((outputs, grad_input)):
        arrivals[i].wait()
        stores.append(pltpu.make_async_copy(through.at[i], target, pass_sem.at[2 + i]))
        stores[-1].start()
    for one in stores:
        one.wait()


def expand(total, small, outputs, grad_input, ff):
    chunks, _, width = total.shape
    cols = ff // width
    square = jax.ShapeDtypeStruct((width, width), F32)
    scalar = jax.ShapeDtypeStruct((1, 1), F32)
    vmem = pl.BlockSpec(memory_space=pltpu.VMEM)
    hbm = pl.BlockSpec(memory_space=pl.ANY)
    return pl.pallas_call(
        functools.partial(expand_kernel, cols),
        out_shape=(
            jax.ShapeDtypeStruct((ff, width), F32),
            jax.ShapeDtypeStruct((width, ff), F32),
            square, square, square, square,
            jax.ShapeDtypeStruct(outputs.shape, BF),
            jax.ShapeDtypeStruct(outputs.shape, BF),
            jax.ShapeDtypeStruct((1, ff), F32),
            jax.ShapeDtypeStruct((1, width), F32),
            scalar, scalar,
        ),
        in_specs=[hbm, vmem, hbm, hbm],
        out_specs=(hbm,) * 8 + (vmem,) * 4,
        scratch_shapes=[
            pltpu.VMEM(total.shape, BF),
            pltpu.VMEM((chunks, 2, width, width), F32),
            pltpu.VMEM((2,) + outputs.shape, BF),
            pltpu.SemaphoreType.DMA((chunks,)),
            pltpu.SemaphoreType.DMA((chunks, 2)),
            pltpu.SemaphoreType.DMA((4,)),
        ],
        name="expand",
        compiler_params=pltpu.CompilerParams(vmem_limit_bytes=63 << 20),
    )(total, small, outputs, grad_input)


def per_device(
    tokens, lengths, w_query, w_key, w_value, w_out, w_in, b_in, w_back, b_back,
    alpha_attn, alpha_ffn, cotangent,
):
    seqs, rows, width = tokens.shape
    ff = w_in.shape[1]
    nb, n = lax.axis_size("batch"), lax.axis_size("blk")
    keep = n <= 4
    slots = seqs * n if keep else 1
    ff_cols = ff // width
    chunks = ff_cols + 2
    plan = Reducer(nb, n, 2 * width)
    steps = nb.bit_length() - 1
    small_rows = -(-(ff_cols + 3) // 8) * 8
    vmem = pl.BlockSpec(memory_space=pltpu.VMEM)
    smem = pl.BlockSpec(memory_space=pltpu.SMEM)
    hbm = pl.BlockSpec(memory_space=pl.ANY)
    square = (rows, width)
    dma = pltpu.SemaphoreType.DMA
    outputs, grad_input, total, small = pl.pallas_call(
        functools.partial(layer_kernel, plan, n, keep),
        out_shape=(
            jax.ShapeDtypeStruct(tokens.shape, BF),
            jax.ShapeDtypeStruct(tokens.shape, BF),
            jax.ShapeDtypeStruct((chunks, 2 * width, width), BF),
            jax.ShapeDtypeStruct((small_rows, width), F32),
        ),
        in_specs=[smem] * 3 + [vmem] * 2 + [hbm] * 8,
        out_specs=(vmem, vmem, hbm, vmem),
        scratch_shapes=[
            pltpu.VMEM(tokens.shape, BF),
            pltpu.VMEM((width, width), BF), pltpu.VMEM((width, width), BF),
            pltpu.VMEM((width, width), BF), pltpu.VMEM((width, width), BF),
            pltpu.VMEM(w_in.shape, BF), pltpu.VMEM(w_back.shape, BF),
            dma((seqs + 7,)),
            pltpu.VMEM((seqs, n) + square, BF),
            pltpu.VMEM((width, width), BF),
            pltpu.VMEM((width, width), BF),
            pltpu.VMEM((width, rows), BF),
            pltpu.VMEM((n + 1 if keep else 1,) + square, BF),
            pltpu.VMEM((slots,) + square, BF),
            pltpu.VMEM((slots, width, rows), BF),
            pltpu.VMEM((n + 1 if keep else 1, width, rows), BF),
            pltpu.VMEM((seqs, HEADS // 2, 2 * rows, PAIR), BF),
            pltpu.VMEM((HEADS // 2, 2 * rows, PAIR), BF),
            pltpu.VMEM((HEADS, rows, rows), F32),
            pltpu.VMEM((slots, HEADS // 2, rows, 2 * rows), BF),
            pltpu.VMEM((HEADS // 2, rows, 2 * rows), BF),
            pltpu.VMEM((seqs, HEADS, 1, rows), F32),
            pltpu.VMEM((seqs, HEADS, 1, rows), F32),
            pltpu.VMEM((seqs, width, rows), F32),
            pltpu.VMEM((seqs, width, rows), BF),
            pltpu.VMEM((width, rows), BF),
            pltpu.VMEM((seqs,) + square, F32),
            pltpu.VMEM(square, F32),
            pltpu.VMEM(square, BF),
            pltpu.VMEM((width, rows), BF),
            pltpu.VMEM(square, BF),
            pltpu.VMEM(square, F32),
            pltpu.VMEM((seqs,) + square, F32),
            pltpu.VMEM((seqs, HEADS, 1, rows), F32),
            pltpu.VMEM((HEADS, 1, rows), F32),
            pltpu.VMEM((width, rows), F32),
            pltpu.VMEM(square, BF),
            pltpu.VMEM(square, BF),
            pltpu.VMEM((4, width, width), F32),
            pltpu.VMEM((seqs, n) + square, BF),
            dma((seqs, n, 2)), dma((seqs, n, 2)), dma((seqs, n)), dma((seqs, n)),
            pltpu.VMEM((chunks, 2 * width, width), BF),
            pltpu.VMEM((chunks, 2 * width, width), BF),
            dma((chunks,)),
        ]
        + plan.scratch(chunks, width)
        + [
            pltpu.VMEM((steps + 1, small_rows, width), F32),
            pltpu.VMEM((steps, small_rows, width), F32),
            pltpu.VMEM((n, small_rows, width), F32),
            dma((steps + n - 1,)),
            dma((steps + n - 1,)),
        ],
        name="layer",
        compiler_params=pltpu.CompilerParams(
            collective_id=0, has_side_effects=True, vmem_limit_bytes=63 << 20
        ),
    )(
        lengths, alpha_attn.reshape(1), alpha_ffn.reshape(1), b_in.reshape(1, ff),
        b_back.reshape(1, width), tokens, cotangent, w_query, w_key, w_value, w_out, w_in, w_back,
    )
    back, grad_in, out, query, key, value, outputs, grad_input, b_in, b_back, attn, ffn = expand(
        total, small, outputs, grad_input, ff
    )
    return (
        outputs, grad_input, query, key, value, out, grad_in, b_in.reshape(ff), back,
        b_back.reshape(width), attn.reshape(()), ffn.reshape(()),
    )


def solution(mesh):
    return jax.shard_map(
        per_device,
        mesh=mesh,
        in_specs=(
            P("batch", "blk", None),
            P("batch"),
            P(),
            P(),
            P(),
            P(),
            P(),
            P(),
            P(),
            P(),
            P(),
            P(),
            P("batch", "blk", None),
        ),
        out_specs=(
            P("batch", "blk", None),
            P("batch", "blk", None),
            P(),
            P(),
            P(),
            P(),
            P(),
            P(),
            P(),
            P(),
            P(),
            P(),
        ),
        check_vma=False,
    )
```

```python
import functools

import jax
import jax.numpy as jnp
from jax import lax
from jax.experimental import pallas as pl
from jax.experimental.pallas import tpu as pltpu
from jax.sharding import PartitionSpec as P

HEADS = 8
HEAD_DIM = 64
PAIR = 2 * HEAD_DIM
MESH = pl.DeviceIdType.MESH
BF = jnp.bfloat16
F32 = jnp.float32
NEG = -1e30
GELU_A = 0.7978845608
GELU_B = 0.7978845608 * 0.044715

ORDER = (
    ("start_back", 0), ("block", 0, 0), ("send", 0, 0), ("block", 0, 1), ("send", 0, 1), ("attention", 1),
    ("start_ff", 1), ("column", 1, 0), ("sum", 0, 1), ("column", 1, 1), ("sum", 0, 0), ("sum", 0, 2), ("sum", 0, 3),
    ("sum", 1, 1), ("pass", 0, 0, 0), ("pass", 0, 0, 1), ("end_ff", 1), ("small", 0), ("block", 0, 2),
    ("block", 0, 3), ("send", 0, 2), ("sum", 1, 0), ("end_back", 0), ("sum", 1, 2), ("start_back", 1),
    ("block", 1, 0), ("small", 1), ("block", 1, 1), ("send", 1, 1), ("sum", 2, 0), ("block", 1, 2), ("small", 2),
    ("pass", 0, 1, 0), ("sum", 2, 1), ("sum", 2, 2), ("block", 1, 3), ("small", 3), ("sum", 3, 0), ("end_back", 1),
    ("sum", 0, 4), ("sum", 1, 3), ("sum", 3, 1), ("sum", 3, 2), ("sum", 1, 4), ("sum", 0, 5), ("sum", 1, 5),
    ("sum", 4, 0), ("sum", 2, 4), ("sum", 4, 2), ("sum", 2, 5), ("sum", 2, 3), ("sum", 4, 1), ("sum", 3, 5),
    ("sum", 5, 2), ("sum", 3, 4), ("sum", 5, 0), ("sum", 5, 1), ("sum", 6, 2), ("sum", 3, 3), ("sum", 6, 0),
    ("sum", 4, 5), ("sum", 4, 4), ("send", 1, 0), ("sum", 4, 3), ("sum", 6, 1), ("sum", 5, 5), ("sum", 7, 2),
    ("sum", 5, 4), ("send", 1, 2), ("sum", 6, 5), ("pass", 1, 0, 0), ("sum", 5, 3), ("sum", 6, 4), ("pass", 0, 1, 1),
    ("sum", 7, 5), ("pass", 1, 0, 1), ("pass", 0, 0, 2), ("sum", 6, 3), ("pass", 1, 1, 0), ("sum", 7, 1),
    ("sum", 7, 0), ("sum", 8, 5), ("sum", 7, 4), ("sum", 7, 3), ("pass", 1, 0, 2), ("pass", 1, 1, 1), ("sum", 8, 4),
    ("sum", 8, 2), ("pass", 0, 2, 0), ("sum", 8, 0), ("pass", 1, 2, 0), ("sum", 8, 1), ("sum", 8, 3),
)


class Reducer:
    def __init__(self, nb, nz, rows):
        self.rows, self.nz = rows, nz
        plane = [("batch", 1 << i) for i in range(1, nb.bit_length() - 1)]
        line = [("blk", 1 << i) for i in range(nz.bit_length() - 1)]
        self.all_bits = [("batch", 1)] + plane + line
        direct = (rows // 4 >> len(plane)) // nz >= 16
        steps = line if not direct else [("blk", 0)]
        self.orders = [plane + steps, plane[::-1] + steps]
        self.steps = len(self.orders[0])
        self.kinds, self.sizes, self.lands = [], [], [[], []]
        self.messages = []
        length, land = rows // 4, rows // 2
        for axis, bit in self.orders[0]:
            if bit == 0:
                kind, length, messages = "direct", length // nz, nz - 1
            elif length >= 32:
                kind, length, messages = "half", length // 2, 1
            else:
                kind, messages = "full", 1
            self.kinds.append(kind)
            self.sizes.append(length)
            self.messages.append(messages)
            for o in (0, 1):
                self.lands[o].append(land)
                land += length * messages
        self.land_rows = land
        self.back_steps = [i for i in range(self.steps) if self.kinds[i] != "full"][::-1]
        self.stages = 3 + self.steps + len(self.back_steps)

    def scratch(self, chunks, width):
        return [
            pltpu.VMEM((chunks, self.land_rows, width), BF),
            pltpu.SemaphoreType.DMA((chunks, self.stages - 1)),
            pltpu.SemaphoreType.DMA((chunks, self.stages - 1)),
        ]

    def bind(self, grads, total, land, send_sem, recv_sem):
        self.grads, self.total, self.land = grads, total, land
        self.send_sem, self.recv_sem = send_sem, recv_sem
        self.at = {"batch": lax.axis_index("batch"), "blk": lax.axis_index("blk")}
        core = self.at["batch"] % 2
        half = self.rows // 2
        self.core_keep, self.core_send = core * half, (1 - core) * half
        self.start, self.keep, self.send = [[], []], [[], []], [[], []]
        for o in (0, 1):
            off = self.core_keep + o * (half // 2)
            for i, (axis, bit) in enumerate(self.orders[o]):
                size, here = self.sizes[i], self.at[axis]
                self.start[o].append(off)
                if self.kinds[i] == "half":
                    mine = (here // bit) % 2
                    self.keep[o].append(off + mine * size)
                    self.send[o].append(off + (1 - mine) * size)
                elif self.kinds[i] == "direct":
                    self.keep[o].append(off + here * size)
                    self.send[o].append(None)
                else:
                    self.keep[o].append(off)
                    self.send[o].append(off)
                off = self.keep[o][-1]

    def partner(self, axis, bit):
        mine = (self.at[axis] // bit) % 2
        there = self.at[axis] + bit * (1 - 2 * mine)
        if axis == "batch":
            return (there, self.at["blk"])
        return (self.at["batch"], there)

    def copy(self, c, src, src_row, dst, dst_row, size, sem, device):
        return pltpu.make_async_remote_copy(
            src_ref=src.at[c, pl.ds(pl.multiple_of(src_row, 16), size)],
            dst_ref=dst.at[c, pl.ds(pl.multiple_of(dst_row, 16), size)],
            send_sem=self.send_sem.at[c, sem],
            recv_sem=self.recv_sem.at[c, sem],
            device_id=device,
            device_id_type=MESH,
        )

    def core_out(self, c):
        there = self.partner("batch", 1)
        return self.copy(c, self.grads, self.core_send, self.land, 0, self.rows // 2, 0, there)

    def core_back(self, c):
        there, row, sem = self.partner("batch", 1), self.core_keep, self.stages - 2
        return self.copy(c, self.total, row, self.total, row, self.rows // 2, sem, there)

    def start_out(self, c, i):
        size = self.sizes[i]
        for o in (0, 1):
            axis, bit = self.orders[o][i]
            land = self.lands[o][i]
            if self.kinds[i] != "direct":
                there = self.partner(axis, bit)
                self.copy(c, self.grads, self.send[o][i], self.land, land, size, i + 1, there).start()
                continue
            for d in range(1, self.nz):
                there = (self.at["blk"] + d) % self.nz
                row, peer = self.start[o][i] + there * size, (self.at["batch"], there)
                self.copy(
                    c, self.grads, row, self.land, land + (d - 1) * size, size, i + 1, peer
                ).start()

    def start_back(self, c, place):
        i, sem = self.back_steps[place], self.steps + 1 + place
        for o in (0, 1):
            axis, bit = self.orders[o][i]
            size, row = self.sizes[i], self.keep[o][i]
            peers = [self.partner(axis, bit)]
            if self.kinds[i] == "direct":
                peers = [(self.at["batch"], (self.at["blk"] + d) % self.nz) for d in range(1, self.nz)]
            for peer in peers:
                self.copy(c, self.total, row, self.total, row, size, sem, peer).start()

    def wait(self, c, ref, i, sem):
        rows = 2 * self.sizes[i] * self.messages[i]
        every = self.copy(c, ref, 0, ref, 0, rows, sem, self.partner("batch", 1))
        every.wait_send()
        every.wait_recv()

    def add(self, c, row, land_row, size, pieces=1, last=False):
        part = min(size, 64)
        target = self.total if last else self.grads

        def body(k, carry):
            here = pl.ds(pl.multiple_of(row + k * part, 16), part)
            value = self.grads[c, here]
            if pieces > 1:
                value = value.astype(F32)
            for d in range(pieces):
                there = pl.ds(pl.multiple_of(land_row + d * size + k * part, 16), part)
                value = value + self.land[c, there].astype(value.dtype)
            target[c, here] = value.astype(BF)
            return carry

        lax.fori_loop(0, size // part, body, 0)

    def stage(self, k, c):
        if k == 0:
            self.core_out(c).start()
            return
        if k == 1:
            self.core_out(c).wait()
            self.add(c, self.core_keep, 0, self.rows // 2)
        elif k <= self.steps + 1:
            i = k - 2
            self.wait(c, self.land, i, k - 1)
            pieces = self.nz - 1 if self.kinds[i] == "direct" else 1
            last = i == self.steps - 1
            for o in (0, 1):
                self.add(c, self.keep[o][i], self.lands[o][i], self.sizes[i], pieces, last)
        elif k < self.stages - 1:
            self.wait(c, self.total, self.back_steps[k - self.steps - 2], k - 1)
        else:
            self.core_back(c).wait()
            return
        if k <= self.steps:
            self.start_out(c, k - 1)
        elif k < self.stages - 2:
            self.start_back(c, k - self.steps - 1)
        else:
            self.core_back(c).start()


def mm(left, right):
    return jnp.dot(left, right, preferred_element_type=F32)


def mm_nt(left, right):
    return lax.dot_general(left, right, (((1,), (1,)), ((), ())), preferred_element_type=F32)


def mm_tn(left, right):
    return lax.dot_general(left, right, (((0,), (0,)), ((), ())), preferred_element_type=F32)


def default_order(stages, n, ff_cols, chunks, plane_bits):
    order = [("start_back", 0)] + [("block", 0, j) for j in range(n)] + [("end_back", 0)]
    order += [("attention", 1), ("start_ff", 1)] + [("column", 1, c) for c in range(ff_cols // 2)] + [("end_ff", 1)]
    order += [("start_back", 1)] + [("block", 1, j) for j in range(n)] + [("end_back", 1)]
    order += [("sends", 0), ("sends", 1)]
    order += [("passes", s, hop) for s in (0, 1) for hop in range(n - 1)]
    order += [("small", i) for i in range(plane_bits + 1)]
    for t in range(stages + chunks - 1):
        order += [("sum", k, t - k) for k in range(stages - 1, -1, -1) if 0 <= t - k < chunks]
    return order


def layer_kernel(plan, n, keep, lens, alpha_attn_ref, alpha_ffn_ref, b_in, b_back, *refs):
    (
        tokens_hbm, cot_hbm, wq_hbm, wk_hbm, wv_hbm, wo_hbm, w_in_hbm, w_back_hbm,
        outputs, grad_input, total, small_out,
        cot, wq, wk, wv, wo, w_in, w_back, load_sem,
        x_all, wk_t, wv_t, x_t, k_all, v_all, k_t, v_t, q_m, do_m, score, prob_bf, grad_bf, top, norm, o_t, attn_t, do_t,
        live_branch, resid, resid_bf, resid_t, grad_ffn, ffn, grad_x, lse, delta,
        dq_t, dk, dv, acc, back_in,
        x_send, x_recv, r_send, r_recv,
        grads, land, send_sem, recv_sem, small, small_land, small_line, small_send, small_recv,
    ) = refs
    seqs, _, rows, width = x_all.shape
    chunks = grads.shape[0]
    ff_cols = w_in.shape[1] // width
    pairs = width // PAIR
    plan.bind(grads, total, land, send_sem, recv_sem)
    b, z = lax.axis_index("batch"), lax.axis_index("blk")
    has_up, has_down = z < n - 1, z > 0
    alpha_attn, alpha_ffn = alpha_attn_ref[0], alpha_ffn_ref[0]

    def loop(f, count):
        def body(j, carry):
            f(j)
            return carry

        lax.fori_loop(0, count, body, 0)

    def load(i):
        if i < seqs:
            return pltpu.make_async_copy(tokens_hbm.at[i], x_all.at[i, z], load_sem.at[i])
        pairs_of = [
            (wk_hbm, wk), (wv_hbm, wv), (wq_hbm, wq), (wo_hbm, wo),
            (w_in_hbm, w_in), (w_back_hbm, w_back), (cot_hbm, cot),
        ]
        src, dst = pairs_of[i - seqs]
        return pltpu.make_async_copy(src, dst, load_sem.at[i])

    for i in range(seqs + 7):
        load(i).start()

    def x_copy(s, j, h):
        here = pl.ds(h * (rows // 2), rows // 2)
        return pltpu.make_async_remote_copy(
            src_ref=x_all.at[s, j, here], dst_ref=x_all.at[s, j, here],
            send_sem=x_send.at[s, j, h], recv_sem=x_recv.at[s, j, h],
            device_id=(b, z + 1), device_id_type=MESH,
        )

    def r_copy(s, j, src):
        return pltpu.make_async_remote_copy(
            src_ref=src.at[s, j], dst_ref=back_in.at[s, j],
            send_sem=r_send.at[s, j], recv_sem=r_recv.at[s, j],
            device_id=(b, z - 1), device_id_type=MESH,
        )

    barrier = pltpu.get_barrier_semaphore()
    plane = [(axis, bit) for axis, bit in plan.all_bits if axis == "batch"]
    peers = [plan.partner(axis, bit) for axis, bit in plane] + [(b, (z + d) % n) for d in range(1, n)]
    for peer in peers:
        pl.semaphore_signal(barrier, inc=1, device_id=peer, device_id_type=MESH)
    pl.semaphore_wait(barrier, len(peers))

    def send_own(s):
        @pl.when(has_up)
        def _():
            for h in (0, 1):
                x_copy(s, z, h).start()

    for s in range(seqs):
        load(s).wait()
        if s == 0:
            send_own(0)

    load(seqs).wait()
    wk_t[...] = wk[...].T
    load(seqs + 1).wait()
    wv_t[...] = wv[...].T
    small[0] = jnp.zeros_like(small[0])
    low_lanes = lax.broadcasted_iota(jnp.int32, (rows, PAIR), 1) < HEAD_DIM
    key_iota = lax.broadcasted_iota(jnp.int32, (rows, rows), 0)
    query_pos = z * rows + lax.broadcasted_iota(jnp.int32, (1, rows), 1)

    def split_heads(value, target):
        for h in range(HEADS):
            pair = value[:, (h // 2) * PAIR : (h // 2 + 1) * PAIR]
            mask = low_lanes if h % 2 == 0 else jnp.logical_not(low_lanes)
            target[h // 2, h % 2 * rows : (h % 2 + 1) * rows] = jnp.where(mask, pair, 0.0).astype(BF)

    def slot(s, j):
        return s * n + j if keep else 0

    def forward_slot(s, j):
        return jnp.where((s > 0) & (j == z), n, j) if keep else 0

    def project(s, j):
        here, front = slot(s, j), forward_slot(s, j)
        x = x_all[s, j]
        k_all[front] = mm(x, wk[...]).astype(BF)
        v_all[here] = mm(x, wv[...]).astype(BF)
        k_t[here] = mm_nt(wk_t[...], x).astype(BF)
        v_t[front] = mm_nt(wv_t[...], x).astype(BF)

    def allowed(s, j):
        limit = jnp.minimum(query_pos + 1, lens[s]) - j * rows
        return key_iota < limit

    def scores_of(s, j, head, mask):
        p, half = head // 2, slice(head % 2 * rows, (head % 2 + 1) * rows)
        keys = k_all[forward_slot(s, j), :, p * PAIR : (p + 1) * PAIR]
        return jnp.where(mask, mm_nt(keys, q_m[s, p, half]), NEG)

    def statistics(s, j):
        mask = allowed(s, j)
        for head in range(HEADS):
            score[head] = scores_of(s, j, head, mask)
        for head in range(HEADS):
            old = top[s, head]
            new = jnp.maximum(old, jnp.max(score[head], axis=0, keepdims=True))
            below = jnp.sum(jnp.exp(score[head] - new), axis=0, keepdims=True)
            norm[s, head] = norm[s, head] * jnp.exp(old - new) + below
            top[s, head] = new

    def probabilities(s, j):
        mask = allowed(s, j)
        for head in range(HEADS):
            p, half = head // 2, slice(head % 2 * rows, (head % 2 + 1) * rows)
            probs = jnp.exp(scores_of(s, j, head, mask) - lse[s, head])
            prob_bf[slot(s, j), p, :, half] = probs.astype(BF)

    def mix_values(s, j):
        if not keep:
            project(s, j)
        probabilities(s, j)
        for head in range(HEADS):
            p, half = head // 2, slice(head % 2 * rows, (head % 2 + 1) * rows)
            own = slice(head * HEAD_DIM, (head + 1) * HEAD_DIM)
            o_t[s, own] += mm(v_t[forward_slot(s, j), own], prob_bf[slot(s, j), p, :, half])

    def pass_on(s, j, h):
        x_copy(s, j, h).wait_recv()

        @pl.when(has_up)
        def _():
            x_copy(s, j, h).start()

    def start_seq(s):
        q = mm(x_all[s, z], wq[...]).astype(BF).astype(F32) * 0.125
        split_heads(q, q_m.at[s])
        top[s] = jnp.full_like(top[s], NEG)
        norm[s] = jnp.zeros_like(norm[s])
        o_t[s] = jnp.zeros_like(o_t[s])
        project(s, z)
        statistics(s, z)

    def attention(s):
        def block(i, carry):
            if s == 0:
                for h in (0, 1):
                    pass_on(s, z - i, h)
            else:
                @pl.when((2 * i > ff_cols) | jnp.logical_not(has_up))
                def _():
                    for h in (0, 1):
                        pass_on(s, z - i, h)
            project(s, z - i)
            statistics(s, z - i)
            return carry

        lax.fori_loop(1, z + 1, block, 0)
        if s == 0:
            @pl.when(z > 0)
            def _():
                send_own(1)

            load(seqs + 3).wait()
        lse[s] = top[s] + jnp.log(norm[s])
        loop(functools.partial(mix_values, s), z + 1)
        attn_t[s] = o_t[s].astype(BF)
        branch = mm(attn_t[s].T, wo[...])
        position = z * rows + lax.broadcasted_iota(jnp.int32, (rows, 1), 0)
        live = (position < lens[s]).astype(F32)
        live_branch[s] = live * branch
        resid[...] = x_all[s, z].astype(F32) + alpha_attn * live_branch[s]
        resid_bf[...] = resid[...].astype(BF)
        resid_t[...] = resid_bf[...].T

    def start_feed_forward(s):
        if s == 0:
            for i in (4, 5, 6):
                load(seqs + i).wait()
        grad_out = cot[s].astype(F32)
        grad_ffn[...] = (alpha_ffn * grad_out).astype(BF)
        ffn[...] = jnp.zeros_like(ffn)
        grad_x[s] = grad_out
        small[0, ff_cols : ff_cols + 1] += jnp.sum(
            grad_ffn[...].astype(F32), axis=0, keepdims=True
        )

    def column(s, c):
        lanes = pl.ds(pl.multiple_of(2 * c * width, 2 * width), 2 * width)
        hidden = mm(resid_bf[...], w_in[:, lanes]) + b_in[:, lanes]
        square = hidden * hidden
        half = 0.5 + 0.5 * jnp.tanh(hidden * (GELU_A + GELU_B * square))
        product = hidden * half
        act = product.astype(BF)
        slope = half + product * (1.0 - half) * (2 * GELU_A + 6 * GELU_B * square)
        back = w_back[lanes]
        ffn[...] += mm(act, back)
        grad_hidden = (mm_nt(grad_ffn[...], back) * slope).astype(BF)
        grad_bias = jnp.sum(grad_hidden.astype(F32), axis=0, keepdims=True)
        grad_x[s] += mm_nt(grad_hidden, w_in[:, lanes])
        grad_back = mm(act.T, grad_ffn[...])
        grad_in = mm(resid_t[...], grad_hidden)
        for i in (0, 1):
            chunk, part = 2 * c + i, slice(i * width, (i + 1) * width)
            upper, lower = grad_back[part], grad_in[:, part]
            if s > 0:
                upper += grads[chunk, :width].astype(F32)
                lower += grads[chunk, width:].astype(F32)
            grads[chunk, :width] = upper.astype(BF)
            grads[chunk, width:] = lower.astype(BF)
            small[0, pl.ds(chunk, 1)] += grad_bias[:, part]

    def end_feed_forward(s):
        ffn_out = ffn[...] + b_back[...]
        outputs[s] = (resid[...] + alpha_ffn * ffn_out).astype(BF)
        small[0, ff_cols + 2 : ff_cols + 3] += jnp.sum(
            cot[s].astype(F32) * ffn_out, axis=0, keepdims=True
        )
        small[0, ff_cols + 1 : ff_cols + 2] += jnp.sum(
            grad_x[s] * live_branch[s], axis=0, keepdims=True
        )

    def add_to(k, value, s):
        if s == 0:
            acc[k] = value
        else:
            acc[k] += value

    def start_back(s):
        position = z * rows + lax.broadcasted_iota(jnp.int32, (rows, 1), 0)
        live = (position < lens[s]).astype(F32)
        grad_branch = (alpha_attn * live * grad_x[s]).astype(BF)
        add_to(0, mm(attn_t[s], grad_branch), s)
        do = mm_nt(grad_branch, wo[...]).astype(BF)
        split_heads(do, do_m)
        do_t[...] = mm_nt(wo[...], grad_branch).astype(BF)
        for h in range(HEADS):
            here = slice(h * HEAD_DIM, (h + 1) * HEAD_DIM)
            delta[h] = jnp.sum(do_t[here].astype(F32) * o_t[s, here], axis=0, keepdims=True)
        dq_t[...] = jnp.zeros_like(dq_t)
        if s == 0:
            acc[2] = jnp.zeros_like(acc[2])
            acc[3] = jnp.zeros_like(acc[3])

        @pl.when(has_up)
        def _():
            def sent(j):
                for h in (0, 1):
                    x_copy(s, j, h).wait_send()

            loop(sent, z + 1)

    def block(s, j):
        here = slot(s, j)
        if not keep:
            project(s, j)
            probabilities(s, j)
        for head in range(HEADS):
            p, half = head // 2, slice(head % 2 * rows, (head % 2 + 1) * rows)
            grad_probs = mm_nt(v_all[here, :, p * PAIR : (p + 1) * PAIR], do_m[p, half])
            probs = prob_bf[here, p, :, half].astype(F32)
            grad_bf[p, :, half] = (probs * (grad_probs - delta[head])).astype(BF)
        for p in range(pairs):
            lanes = slice(p * PAIR, (p + 1) * PAIR)
            dv[:, lanes] = mm(prob_bf[here, p], do_m[p]).astype(BF)
            dk[:, lanes] = mm(grad_bf[p], q_m[s, p]).astype(BF)
            for h in (0, 1):
                own = slice(p * PAIR + h * HEAD_DIM, p * PAIR + (h + 1) * HEAD_DIM)
                dq_t[own] += mm(k_t[here, own], grad_bf[p, :, h * rows : (h + 1) * rows])
        part = mm_nt(dk[...], wk[...]) + mm_nt(dv[...], wv[...])
        x_t[...] = x_all[s, j].T
        acc[2] += mm(x_t[...], dk[...])
        acc[3] += mm(x_t[...], dv[...])

        @pl.when(j < z)
        def _():
            x_all[s, j] = part.astype(BF)

        @pl.when(j == z)
        def _():
            grad_x[s] += part

    def send_part(s, j):
        @pl.when(jnp.logical_not(has_up) & (j < z))
        def _():
            r_copy(s, j, x_all).start()

    def end_back(s):
        dq = (dq_t[...] * 0.125).T.astype(BF)
        x_t[...] = x_all[s, z].T
        add_to(1, mm(x_t[...], dq), s)
        grad_x[s] += mm_nt(dq, wq[...])

    def pass_back(s, hop, j):
        @pl.when(z == n - 2 - hop)
        def _():
            r_copy(s, j, back_in).wait_recv()

            @pl.when(j < z)
            def _():
                back_in[s, j] = back_in[s, j] + x_all[s, j]
                r_copy(s, j, back_in).start()

    def finish_input(s):
        @pl.when(has_up)
        def _():
            grad_input[s] = (grad_x[s] + back_in[s, z].astype(F32)).astype(BF)

        @pl.when(jnp.logical_not(has_up))
        def _():
            grad_input[s] = grad_x[s].astype(BF)

    def small_bit(i):
        return pltpu.make_async_remote_copy(
            src_ref=small.at[i], dst_ref=small_land.at[i],
            send_sem=small_send.at[i], recv_sem=small_recv.at[i],
            device_id=plan.partner(*plane[i]), device_id_type=MESH,
        )

    def small_to(d):
        sem = len(plane) + d - 1
        return pltpu.make_async_remote_copy(
            src_ref=small.at[len(plane)], dst_ref=small_line.at[z],
            send_sem=small_send.at[sem], recv_sem=small_recv.at[sem],
            device_id=(b, (z + d) % n), device_id_type=MESH,
        )

    def small_step(i):
        if i > 0:
            small_bit(i - 1).wait()
            small[i] = small[i - 1] + small_land[i - 1]
        if i < len(plane):
            small_bit(i).start()
        else:
            for d in range(1, n):
                small_to(d).start()

    def small_end():
        for d in range(1, n):
            small_to(d).wait()
        small_line[z] = small[len(plane)]
        value = small_line[0]
        for d in range(1, n):
            value = value + small_line[d]
        small_out[...] = value

    def sum_stage(k, c):
        if k == 0 and c >= ff_cols:
            for i in (0, 1):
                part = acc[2 * (c - ff_cols) + i]
                grads[c, i * width : (i + 1) * width] = part.astype(BF)
        plan.stage(k, c)

    steps = {
        "attention": attention, "start_ff": start_feed_forward, "end_ff": end_feed_forward,
        "start_back": start_back, "block": block, "end_back": end_back, "send": send_part,
        "pass": pass_back, "sum": sum_stage, "small": small_step,
        "sends": lambda s: loop(functools.partial(send_part, s), z),
        "passes": lambda s, hop: loop(functools.partial(pass_back, s, hop), n - 1 - hop),
    }

    load(seqs + 2).wait()
    loop(start_seq, seqs)

    @pl.when(z == 0)
    def _():
        send_own(1)

    attention(0)
    start_feed_forward(0)

    def first_column(c):
        @pl.when((z > c) & has_up)
        def _():
            for h in (0, 1):
                pass_on(1, z - c - 1, h)

        column(0, c)

    loop(first_column, ff_cols // 2)
    end_feed_forward(0)

    if n == 4 and ff_cols == 4 and plan.stages == 9 and seqs == 2:
        order = ORDER
    else:
        order = default_order(plan.stages, n, ff_cols, chunks, len(plane))

    def run(step):
        @pl.when(z >= 0)
        def _():
            steps[step[0]](*step[1:])

    def run_between(group):
        at = [i for i, step in enumerate(group) if step[0] == "column"]
        if not at:
            for step in group:
                run(step)
            return
        for step in group[: at[0]]:
            run(step)

        def one(c):
            column(seqs - 1, c)
            for k in range(ff_cols // 2 - 1):
                inside = group[at[k] + 1 : at[k + 1]]
                if inside:
                    @pl.when(c == k)
                    def _():
                        for step in inside:
                            run(step)

        loop(one, ff_cols // 2)
        for step in group[at[-1] + 1 :]:
            run(step)

    at = [i for i, step in enumerate(order) if step[0] == "block"]
    for step in order[: at[0]]:
        run(step)

    def one_block(t):
        s, j = t // n, t % n

        @pl.when(j <= z)
        def _():
            block(s, j)

        for k in range(len(at) - 1):
            group = order[at[k] + 1 : at[k + 1]]
            if group:
                @pl.when(t == k)
                def _():
                    run_between(group)

    loop(one_block, len(at))
    for step in order[at[-1] + 1 :]:
        run(step)
    for s in range(seqs):
        finish_input(s)
    small_end()
    @pl.when(has_down)
    def _():
        for s in range(seqs):
            loop(lambda j: r_copy(s, j, back_in).wait_send(), z)


def expand_kernel(
    cols, total, small, outputs_in, input_in,
    back, w_in, out, query, key, value, outputs, grad_input, b_in, b_back, alpha_attn, alpha_ffn,
    full, store_sem, pass_sem,
):
    chunks, _, width = total.shape
    stores = [
        pltpu.make_async_copy(outputs_in, outputs, pass_sem.at[0]),
        pltpu.make_async_copy(input_in, grad_input, pass_sem.at[1]),
    ]
    for one in stores:
        one.start()
    places = []
    for c in range(cols):
        here = pl.ds(c * width, width)
        places.append((back.at[here], w_in.at[:, here]))
    places += [(out, query), (key, value)]
    for c in range(chunks):
        for i in (0, 1):
            full[c, i] = total[c, i * width : (i + 1) * width].astype(F32)
            stores.append(pltpu.make_async_copy(full.at[c, i], places[c][i], store_sem.at[c, i]))
            stores[-1].start()
    for c in range(cols):
        b_in[:, c * width : (c + 1) * width] = small[c : c + 1]
    b_back[...] = small[cols : cols + 1]
    alpha_attn[...] = jnp.sum(small[cols + 1 : cols + 2], axis=1, keepdims=True)
    alpha_ffn[...] = jnp.sum(small[cols + 2 : cols + 3], axis=1, keepdims=True)
    for one in stores:
        one.wait()


def expand(total, small, outputs, grad_input, ff):
    chunks, _, width = total.shape
    cols = ff // width
    square = jax.ShapeDtypeStruct((width, width), F32)
    scalar = jax.ShapeDtypeStruct((1, 1), F32)
    vmem = pl.BlockSpec(memory_space=pltpu.VMEM)
    hbm = pl.BlockSpec(memory_space=pl.ANY)
    return pl.pallas_call(
        functools.partial(expand_kernel, cols),
        out_shape=(
            jax.ShapeDtypeStruct((ff, width), F32),
            jax.ShapeDtypeStruct((width, ff), F32),
            square, square, square, square,
            jax.ShapeDtypeStruct(outputs.shape, BF),
            jax.ShapeDtypeStruct(outputs.shape, BF),
            jax.ShapeDtypeStruct((1, ff), F32),
            jax.ShapeDtypeStruct((1, width), F32),
            scalar, scalar,
        ),
        in_specs=[vmem] * 4,
        out_specs=(hbm,) * 8 + (vmem,) * 4,
        scratch_shapes=[
            pltpu.VMEM((chunks, 2, width, width), F32),
            pltpu.SemaphoreType.DMA((chunks, 2)),
            pltpu.SemaphoreType.DMA((2,)),
        ],
        name="expand",
        compiler_params=pltpu.CompilerParams(vmem_limit_bytes=40 << 20),
    )(total, small, outputs, grad_input)


def per_device(
    tokens, lengths, w_query, w_key, w_value, w_out, w_in, b_in, w_back, b_back,
    alpha_attn, alpha_ffn, cotangent,
):
    seqs, rows, width = tokens.shape
    ff = w_in.shape[1]
    nb, n = lax.axis_size("batch"), lax.axis_size("blk")
    keep = n <= 4
    slots = seqs * n if keep else 1
    ff_cols = ff // width
    chunks = ff_cols + 2
    plan = Reducer(nb, n, 2 * width)
    steps = nb.bit_length() - 1
    small_rows = -(-(ff_cols + 3) // 8) * 8
    vmem = pl.BlockSpec(memory_space=pltpu.VMEM)
    smem = pl.BlockSpec(memory_space=pltpu.SMEM)
    hbm = pl.BlockSpec(memory_space=pl.ANY)
    square = (rows, width)
    dma = pltpu.SemaphoreType.DMA
    outputs, grad_input, total, small = pl.pallas_call(
        functools.partial(layer_kernel, plan, n, keep),
        out_shape=(
            pltpu.VMEM(tokens.shape, BF),
            pltpu.VMEM(tokens.shape, BF),
            pltpu.VMEM((chunks, 2 * width, width), BF),
            pltpu.VMEM((small_rows, width), F32),
        ),
        in_specs=[smem] * 3 + [vmem] * 2 + [hbm] * 8,
        out_specs=(vmem,) * 4,
        scratch_shapes=[
            pltpu.VMEM(tokens.shape, BF),
            pltpu.VMEM((width, width), BF), pltpu.VMEM((width, width), BF),
            pltpu.VMEM((width, width), BF), pltpu.VMEM((width, width), BF),
            pltpu.VMEM(w_in.shape, BF), pltpu.VMEM(w_back.shape, BF),
            dma((seqs + 7,)),
            pltpu.VMEM((seqs, n) + square, BF),
            pltpu.VMEM((width, width), BF),
            pltpu.VMEM((width, width), BF),
            pltpu.VMEM((width, rows), BF),
            pltpu.VMEM((n + 1 if keep else 1,) + square, BF),
            pltpu.VMEM((slots,) + square, BF),
            pltpu.VMEM((slots, width, rows), BF),
            pltpu.VMEM((n + 1 if keep else 1, width, rows), BF),
            pltpu.VMEM((seqs, HEADS // 2, 2 * rows, PAIR), BF),
            pltpu.VMEM((HEADS // 2, 2 * rows, PAIR), BF),
            pltpu.VMEM((HEADS, rows, rows), F32),
            pltpu.VMEM((slots, HEADS // 2, rows, 2 * rows), BF),
            pltpu.VMEM((HEADS // 2, rows, 2 * rows), BF),
            pltpu.VMEM((seqs, HEADS, 1, rows), F32),
            pltpu.VMEM((seqs, HEADS, 1, rows), F32),
            pltpu.VMEM((seqs, width, rows), F32),
            pltpu.VMEM((seqs, width, rows), BF),
            pltpu.VMEM((width, rows), BF),
            pltpu.VMEM((seqs,) + square, F32),
            pltpu.VMEM(square, F32),
            pltpu.VMEM(square, BF),
            pltpu.VMEM((width, rows), BF),
            pltpu.VMEM(square, BF),
            pltpu.VMEM(square, F32),
            pltpu.VMEM((seqs,) + square, F32),
            pltpu.VMEM((seqs, HEADS, 1, rows), F32),
            pltpu.VMEM((HEADS, 1, rows), F32),
            pltpu.VMEM((width, rows), F32),
            pltpu.VMEM(square, BF),
            pltpu.VMEM(square, BF),
            pltpu.VMEM((4, width, width), F32),
            pltpu.VMEM((seqs, n) + square, BF),
            dma((seqs, n, 2)), dma((seqs, n, 2)), dma((seqs, n)), dma((seqs, n)),
            pltpu.VMEM((chunks, 2 * width, width), BF),
        ]
        + plan.scratch(chunks, width)
        + [
            pltpu.VMEM((steps + 1, small_rows, width), F32),
            pltpu.VMEM((steps, small_rows, width), F32),
            pltpu.VMEM((n, small_rows, width), F32),
            dma((steps + n - 1,)),
            dma((steps + n - 1,)),
        ],
        name="layer",
        compiler_params=pltpu.CompilerParams(
            collective_id=0, has_side_effects=True, vmem_limit_bytes=113 << 19
        ),
    )(
        lengths, alpha_attn.reshape(1), alpha_ffn.reshape(1), b_in.reshape(1, ff),
        b_back.reshape(1, width), tokens, cotangent, w_query, w_key, w_value, w_out, w_in, w_back,
    )
    back, grad_in, out, query, key, value, outputs, grad_input, b_in, b_back, attn, ffn = expand(
        total, small, outputs, grad_input, ff
    )
    return (
        outputs, grad_input, query, key, value, out, grad_in, b_in.reshape(ff), back,
        b_back.reshape(width), attn.reshape(()), ffn.reshape(()),
    )


def solution(mesh):
    return jax.shard_map(
        per_device,
        mesh=mesh,
        in_specs=(
            P("batch", "blk", None),
            P("batch"),
            P(),
            P(),
            P(),
            P(),
            P(),
            P(),
            P(),
            P(),
            P(),
            P(),
            P("batch", "blk", None),
        ),
        out_specs=(
            P("batch", "blk", None),
            P("batch", "blk", None),
            P(),
            P(),
            P(),
            P(),
            P(),
            P(),
            P(),
            P(),
            P(),
            P(),
        ),
        check_vma=False,
    )
```

```python
import functools

import jax
import jax.numpy as jnp
from jax import lax
from jax.experimental import pallas as pl
from jax.experimental.pallas import tpu as pltpu
from jax.sharding import PartitionSpec as P

HEADS = 8
HEAD_DIM = 64
PAIR = 2 * HEAD_DIM
MESH = pl.DeviceIdType.MESH
BF = jnp.bfloat16
F32 = jnp.float32
NEG = -1e30
GELU_A = 0.7978845608
GELU_B = 0.7978845608 * 0.044715

ORDER = (
    ("start_back", 0), ("block", 0, 0), ("block", 0, 1), ("send", 0, 0), ("attention", 1), ("start_ff", 1),
    ("column", 1, 0), ("sum", 0, 0), ("send", 0, 1), ("column", 1, 1), ("sum", 0, 2), ("end_ff", 1), ("small", 0),
    ("sum", 1, 0), ("sum", 0, 1), ("pass", 0, 0, 0), ("block", 0, 2), ("sum", 1, 2), ("send", 0, 2), ("sum", 0, 3),
    ("block", 0, 3), ("sum", 2, 0), ("end_back", 0), ("pass", 0, 1, 0), ("sum", 1, 3), ("start_back", 1),
    ("block", 1, 0), ("small", 1), ("sum", 3, 0), ("pass", 0, 0, 1), ("sum", 2, 2), ("block", 1, 1), ("send", 1, 1),
    ("sum", 1, 1), ("block", 1, 2), ("small", 2), ("block", 1, 3), ("small", 3), ("end_back", 1), ("pass", 0, 0, 2),
    ("pass", 0, 1, 1), ("sum", 0, 4), ("sum", 2, 3), ("sum", 2, 1), ("sum", 0, 5), ("sum", 3, 2), ("sum", 4, 0),
    ("sum", 1, 4), ("sum", 1, 5), ("sum", 3, 1), ("sum", 3, 3), ("sum", 4, 2), ("sum", 2, 4), ("sum", 5, 0),
    ("sum", 4, 1), ("sum", 2, 5), ("sum", 3, 4), ("sum", 5, 2), ("sum", 3, 5), ("sum", 6, 0), ("sum", 5, 1),
    ("sum", 4, 3), ("sum", 6, 2), ("send", 1, 0), ("sum", 6, 1), ("sum", 4, 5), ("sum", 4, 4), ("sum", 5, 3),
    ("send", 1, 2), ("pass", 1, 0, 0), ("sum", 7, 1), ("sum", 6, 3), ("sum", 5, 5), ("pass", 1, 0, 1), ("sum", 5, 4),
    ("sum", 6, 5), ("pass", 1, 1, 0), ("sum", 6, 4), ("sum", 7, 3), ("sum", 7, 2), ("sum", 7, 0), ("pass", 0, 2, 0),
    ("sum", 7, 5), ("sum", 8, 1), ("sum", 7, 4), ("pass", 1, 2, 0), ("sum", 8, 3), ("sum", 8, 2), ("sum", 8, 0),
    ("pass", 1, 0, 2), ("sum", 8, 4), ("pass", 1, 1, 1), ("sum", 8, 5),
)


class Reducer:
    def __init__(self, nb, nz, rows):
        self.rows, self.nz = rows, nz
        plane = [("batch", 1 << i) for i in range(1, nb.bit_length() - 1)]
        line = [("blk", 1 << i) for i in range(nz.bit_length() - 1)]
        self.all_bits = [("batch", 1)] + plane + line
        direct = (rows // 4 >> len(plane)) // nz >= 16
        steps = line if not direct else [("blk", 0)]
        self.orders = [plane + steps, plane[::-1] + steps]
        self.steps = len(self.orders[0])
        self.kinds, self.sizes, self.lands = [], [], [[], []]
        self.messages = []
        length, land = rows // 4, rows // 2
        for axis, bit in self.orders[0]:
            if bit == 0:
                kind, length, messages = "direct", length // nz, nz - 1
            elif length >= 32:
                kind, length, messages = "half", length // 2, 1
            else:
                kind, messages = "full", 1
            self.kinds.append(kind)
            self.sizes.append(length)
            self.messages.append(messages)
            for o in (0, 1):
                self.lands[o].append(land)
                land += length * messages
        self.land_rows = land
        self.back_steps = [i for i in range(self.steps) if self.kinds[i] != "full"][::-1]
        self.stages = 3 + self.steps + len(self.back_steps)

    def scratch(self, chunks, width):
        return [
            pltpu.VMEM((chunks, self.land_rows, width), BF),
            pltpu.SemaphoreType.DMA((chunks, self.stages - 1)),
            pltpu.SemaphoreType.DMA((chunks, self.stages - 1)),
        ]

    def bind(self, grads, total, land, send_sem, recv_sem):
        self.grads, self.total, self.land = grads, total, land
        self.send_sem, self.recv_sem = send_sem, recv_sem
        self.at = {"batch": lax.axis_index("batch"), "blk": lax.axis_index("blk")}
        core = self.at["batch"] % 2
        half = self.rows // 2
        self.core_keep, self.core_send = core * half, (1 - core) * half
        self.start, self.keep, self.send = [[], []], [[], []], [[], []]
        for o in (0, 1):
            off = self.core_keep + o * (half // 2)
            for i, (axis, bit) in enumerate(self.orders[o]):
                size, here = self.sizes[i], self.at[axis]
                self.start[o].append(off)
                if self.kinds[i] == "half":
                    mine = (here // bit) % 2
                    self.keep[o].append(off + mine * size)
                    self.send[o].append(off + (1 - mine) * size)
                elif self.kinds[i] == "direct":
                    self.keep[o].append(off + here * size)
                    self.send[o].append(None)
                else:
                    self.keep[o].append(off)
                    self.send[o].append(off)
                off = self.keep[o][-1]

    def partner(self, axis, bit):
        mine = (self.at[axis] // bit) % 2
        there = self.at[axis] + bit * (1 - 2 * mine)
        if axis == "batch":
            return (there, self.at["blk"])
        return (self.at["batch"], there)

    def copy(self, c, src, src_row, dst, dst_row, size, sem, device):
        return pltpu.make_async_remote_copy(
            src_ref=src.at[c, pl.ds(pl.multiple_of(src_row, 16), size)],
            dst_ref=dst.at[c, pl.ds(pl.multiple_of(dst_row, 16), size)],
            send_sem=self.send_sem.at[c, sem],
            recv_sem=self.recv_sem.at[c, sem],
            device_id=device,
            device_id_type=MESH,
        )

    def core_out(self, c):
        there = self.partner("batch", 1)
        return self.copy(c, self.grads, self.core_send, self.land, 0, self.rows // 2, 0, there)

    def core_back(self, c):
        there, row, sem = self.partner("batch", 1), self.core_keep, self.stages - 2
        return self.copy(c, self.total, row, self.total, row, self.rows // 2, sem, there)

    def start_out(self, c, i):
        size = self.sizes[i]
        for o in (0, 1):
            axis, bit = self.orders[o][i]
            land = self.lands[o][i]
            if self.kinds[i] != "direct":
                there = self.partner(axis, bit)
                self.copy(c, self.grads, self.send[o][i], self.land, land, size, i + 1, there).start()
                continue
            for d in range(1, self.nz):
                there = (self.at["blk"] + d) % self.nz
                row, peer = self.start[o][i] + there * size, (self.at["batch"], there)
                self.copy(
                    c, self.grads, row, self.land, land + (d - 1) * size, size, i + 1, peer
                ).start()

    def start_back(self, c, place):
        i, sem = self.back_steps[place], self.steps + 1 + place
        for o in (0, 1):
            axis, bit = self.orders[o][i]
            size, row = self.sizes[i], self.keep[o][i]
            peers = [self.partner(axis, bit)]
            if self.kinds[i] == "direct":
                peers = [(self.at["batch"], (self.at["blk"] + d) % self.nz) for d in range(1, self.nz)]
            for peer in peers:
                self.copy(c, self.total, row, self.total, row, size, sem, peer).start()

    def wait(self, c, ref, i, sem):
        rows = 2 * self.sizes[i] * self.messages[i]
        every = self.copy(c, ref, 0, ref, 0, rows, sem, self.partner("batch", 1))
        every.wait_send()
        every.wait_recv()

    def add(self, c, row, land_row, size, pieces=1, last=False):
        part = min(size, 64)
        target = self.total if last else self.grads

        def body(k, carry):
            here = pl.ds(pl.multiple_of(row + k * part, 16), part)
            value = self.grads[c, here]
            if pieces > 1:
                value = value.astype(F32)
            for d in range(pieces):
                there = pl.ds(pl.multiple_of(land_row + d * size + k * part, 16), part)
                value = value + self.land[c, there].astype(value.dtype)
            target[c, here] = value.astype(BF)
            return carry

        lax.fori_loop(0, size // part, body, 0)

    def stage(self, k, c):
        if k == 0:
            self.core_out(c).start()
            return
        if k == 1:
            self.core_out(c).wait()
            self.add(c, self.core_keep, 0, self.rows // 2)
        elif k <= self.steps + 1:
            i = k - 2
            self.wait(c, self.land, i, k - 1)
            pieces = self.nz - 1 if self.kinds[i] == "direct" else 1
            last = i == self.steps - 1
            for o in (0, 1):
                self.add(c, self.keep[o][i], self.lands[o][i], self.sizes[i], pieces, last)
        elif k < self.stages - 1:
            self.wait(c, self.total, self.back_steps[k - self.steps - 2], k - 1)
        else:
            self.core_back(c).wait()
            return
        if k <= self.steps:
            self.start_out(c, k - 1)
        elif k < self.stages - 2:
            self.start_back(c, k - self.steps - 1)
        else:
            self.core_back(c).start()


def mm(left, right):
    return jnp.dot(left, right, preferred_element_type=F32)


def mm_nt(left, right):
    return lax.dot_general(left, right, (((1,), (1,)), ((), ())), preferred_element_type=F32)


def mm_tn(left, right):
    return lax.dot_general(left, right, (((0,), (0,)), ((), ())), preferred_element_type=F32)


def default_order(stages, n, ff_cols, chunks, plane_bits):
    order = [("start_back", 0)] + [("block", 0, j) for j in range(n)] + [("end_back", 0)]
    order += [("attention", 1), ("start_ff", 1)] + [("column", 1, c) for c in range(ff_cols // 2)] + [("end_ff", 1)]
    order += [("start_back", 1)] + [("block", 1, j) for j in range(n)] + [("end_back", 1)]
    order += [("sends", 0), ("sends", 1)]
    order += [("passes", s, hop) for s in (0, 1) for hop in range(n - 1)]
    order += [("small", i) for i in range(plane_bits + 1)]
    for t in range(stages + chunks - 1):
        order += [("sum", k, t - k) for k in range(stages - 1, -1, -1) if 0 <= t - k < chunks]
    return order


def layer_kernel(plan, n, keep, lens, alpha_attn_ref, alpha_ffn_ref, *refs):
    (
        b_in_hbm, b_back_hbm, tokens_hbm, cot_hbm, wq_hbm, wk_hbm, wv_hbm, wo_hbm, w_in_hbm, w_back_hbm,
        outputs, grad_input, total, small_out,
        b_in, b_back, cot, wq, wk, wv, wo, w_in, w_back, load_sem,
        x_all, x_t, k_all, v_all, k_t, v_t, q_m, do_m, score, prob_bf, grad_bf, top, norm, o_t, attn_t, do_t,
        live_branch, resid, resid_bf, resid_t, grad_ffn, ffn, grad_x, lse, delta,
        dq_t, dk, dv, acc, back_in,
        x_send, x_recv, r_send, r_recv,
        grads, land, send_sem, recv_sem, small, small_land, small_line, small_send, small_recv,
    ) = refs
    seqs, _, rows, width = x_all.shape
    chunks = grads.shape[0]
    ff_cols = w_in.shape[1] // width
    pairs = width // PAIR
    plan.bind(grads, total, land, send_sem, recv_sem)
    b, z = lax.axis_index("batch"), lax.axis_index("blk")
    has_up, has_down = z < n - 1, z > 0
    alpha_attn, alpha_ffn = alpha_attn_ref[0], alpha_ffn_ref[0]

    def loop(f, count):
        def body(j, carry):
            f(j)
            return carry

        lax.fori_loop(0, count, body, 0)

    def load(i):
        if i < seqs:
            return pltpu.make_async_copy(tokens_hbm.at[i], x_all.at[i, z], load_sem.at[i])
        pairs_of = [
            (wk_hbm, wk), (wv_hbm, wv), (wq_hbm, wq), (wo_hbm, wo),
            (w_in_hbm, w_in), (w_back_hbm, w_back), (cot_hbm, cot), (b_in_hbm, b_in), (b_back_hbm, b_back),
        ]
        src, dst = pairs_of[i - seqs]
        return pltpu.make_async_copy(src, dst, load_sem.at[i])

    for i in range(seqs + 9):
        load(i).start()

    def x_copy(s, j, h):
        here = pl.ds(h * (rows // 2), rows // 2)
        return pltpu.make_async_remote_copy(
            src_ref=x_all.at[s, j, here], dst_ref=x_all.at[s, j, here],
            send_sem=x_send.at[s, j, h], recv_sem=x_recv.at[s, j, h],
            device_id=(b, z + 1), device_id_type=MESH,
        )

    def r_copy(s, j, src):
        return pltpu.make_async_remote_copy(
            src_ref=src.at[s, j], dst_ref=back_in.at[s, j],
            send_sem=r_send.at[s, j], recv_sem=r_recv.at[s, j],
            device_id=(b, z - 1), device_id_type=MESH,
        )

    barrier = pltpu.get_barrier_semaphore()
    plane = [(axis, bit) for axis, bit in plan.all_bits if axis == "batch"]
    peers = [plan.partner(axis, bit) for axis, bit in plane] + [(b, (z + d) % n) for d in range(1, n)]
    for peer in peers:
        pl.semaphore_signal(barrier, inc=1, device_id=peer, device_id_type=MESH)
    pl.semaphore_wait(barrier, len(peers))

    def send_own(s):
        @pl.when(has_up)
        def _():
            for h in (0, 1):
                x_copy(s, z, h).start()

    for s in range(seqs):
        load(s).wait()
        if s == 0:
            send_own(0)

    for i in range(3):
        load(seqs + i).wait()
    small[0] = jnp.zeros_like(small[0])
    low_lanes = lax.broadcasted_iota(jnp.int32, (rows, PAIR), 1) < HEAD_DIM
    key_iota = lax.broadcasted_iota(jnp.int32, (rows, rows), 0)
    query_pos = z * rows + lax.broadcasted_iota(jnp.int32, (1, rows), 1)

    def split_heads(value, target):
        for h in range(HEADS):
            pair = value[:, (h // 2) * PAIR : (h // 2 + 1) * PAIR]
            mask = low_lanes if h % 2 == 0 else jnp.logical_not(low_lanes)
            target[h // 2, h % 2 * rows : (h % 2 + 1) * rows] = jnp.where(mask, pair, 0.0).astype(BF)

    def slot(s, j):
        return s * n + j if keep else 0

    def forward_slot(s, j):
        return jnp.where((s > 0) & (j == z), n, j) if keep else 0

    def project(s, j):
        here, front = slot(s, j), forward_slot(s, j)
        x = x_all[s, j]
        keys, values = mm(x, wk[...]).astype(BF), mm(x, wv[...]).astype(BF)
        k_all[front], v_all[here] = keys, values
        k_t[here], v_t[front] = keys.T, values.T

    def allowed(s, j):
        limit = jnp.minimum(query_pos + 1, lens[s]) - j * rows
        return key_iota < limit

    def scores_of(s, j, head, mask):
        p, half = head // 2, slice(head % 2 * rows, (head % 2 + 1) * rows)
        keys = k_all[forward_slot(s, j), :, p * PAIR : (p + 1) * PAIR]
        return jnp.where(mask, mm_nt(keys, q_m[s, p, half]), NEG)

    def statistics(s, j):
        mask = allowed(s, j)
        for head in range(HEADS):
            score[head] = scores_of(s, j, head, mask)
        for head in range(HEADS):
            old = top[s, head]
            new = jnp.maximum(old, jnp.max(score[head], axis=0, keepdims=True))
            below = jnp.sum(jnp.exp(score[head] - new), axis=0, keepdims=True)
            norm[s, head] = norm[s, head] * jnp.exp(old - new) + below
            top[s, head] = new

    def probabilities(s, j):
        mask = allowed(s, j)
        for head in range(HEADS):
            p, half = head // 2, slice(head % 2 * rows, (head % 2 + 1) * rows)
            probs = jnp.exp(scores_of(s, j, head, mask) - lse[s, head])
            prob_bf[slot(s, j), p, :, half] = probs.astype(BF)

    def mix_values(s, j):
        if not keep:
            project(s, j)
        probabilities(s, j)
        for head in range(HEADS):
            p, half = head // 2, slice(head % 2 * rows, (head % 2 + 1) * rows)
            own = slice(head * HEAD_DIM, (head + 1) * HEAD_DIM)
            o_t[s, own] += mm(v_t[forward_slot(s, j), own], prob_bf[slot(s, j), p, :, half])

    def pass_on(s, j, h):
        x_copy(s, j, h).wait_recv()

        @pl.when(has_up)
        def _():
            x_copy(s, j, h).start()

    def start_seq(s):
        q = mm(x_all[s, z], wq[...]).astype(BF).astype(F32) * 0.125
        split_heads(q, q_m.at[s])
        top[s] = jnp.full_like(top[s], NEG)
        norm[s] = jnp.zeros_like(norm[s])
        o_t[s] = jnp.zeros_like(o_t[s])
        project(s, z)
        statistics(s, z)

    def attention(s):
        def block(i, carry):
            if s == 0:
                for h in (0, 1):
                    pass_on(s, z - i, h)
            else:
                @pl.when((2 * i > ff_cols) | jnp.logical_not(has_up))
                def _():
                    for h in (0, 1):
                        pass_on(s, z - i, h)
            project(s, z - i)
            statistics(s, z - i)
            return carry

        lax.fori_loop(1, z + 1, block, 0)
        if s == 0:
            @pl.when(z > 0)
            def _():
                send_own(1)

            load(seqs + 3).wait()
        lse[s] = top[s] + jnp.log(norm[s])
        loop(functools.partial(mix_values, s), z + 1)
        attn_t[s] = o_t[s].astype(BF)
        branch = mm(attn_t[s].T, wo[...])
        position = z * rows + lax.broadcasted_iota(jnp.int32, (rows, 1), 0)
        live = (position < lens[s]).astype(F32)
        live_branch[s] = live * branch
        resid[...] = x_all[s, z].astype(F32) + alpha_attn * live_branch[s]
        resid_bf[...] = resid[...].astype(BF)
        resid_t[...] = resid_bf[...].T

    def start_feed_forward(s):
        if s == 0:
            for i in range(4, 9):
                load(seqs + i).wait()
        grad_out = cot[s].astype(F32)
        grad_ffn[...] = (alpha_ffn * grad_out).astype(BF)
        ffn[...] = jnp.zeros_like(ffn)
        grad_x[s] = grad_out
        small[0, ff_cols : ff_cols + 1] += jnp.sum(
            grad_ffn[...].astype(F32), axis=0, keepdims=True
        )

    def column(s, c):
        lanes = pl.ds(pl.multiple_of(2 * c * width, 2 * width), 2 * width)
        hidden = mm(resid_bf[...], w_in[:, lanes]) + b_in[:, lanes]
        square = hidden * hidden
        half = 0.5 + 0.5 * jnp.tanh(hidden * (GELU_A + GELU_B * square))
        product = hidden * half
        act = product.astype(BF)
        slope = half + product * (1.0 - half) * (2 * GELU_A + 6 * GELU_B * square)
        back = w_back[lanes]
        ffn[...] += mm(act, back)
        grad_hidden = (mm_nt(grad_ffn[...], back) * slope).astype(BF)
        grad_bias = jnp.sum(grad_hidden.astype(F32), axis=0, keepdims=True)
        grad_x[s] += mm_nt(grad_hidden, w_in[:, lanes])
        grad_back = mm(act.T, grad_ffn[...])
        grad_in = mm(resid_t[...], grad_hidden)
        for i in (0, 1):
            chunk, part = 2 * c + i, slice(i * width, (i + 1) * width)
            upper, lower = grad_back[part], grad_in[:, part]
            if s > 0:
                upper += grads[chunk, :width].astype(F32)
                lower += grads[chunk, width:].astype(F32)
            grads[chunk, :width] = upper.astype(BF)
            grads[chunk, width:] = lower.astype(BF)
            small[0, pl.ds(chunk, 1)] += grad_bias[:, part]

    def end_feed_forward(s):
        ffn_out = ffn[...] + b_back[...]
        outputs[s] = (resid[...] + alpha_ffn * ffn_out).astype(BF)
        small[0, ff_cols + 2 : ff_cols + 3] += jnp.sum(
            cot[s].astype(F32) * ffn_out, axis=0, keepdims=True
        )
        small[0, ff_cols + 1 : ff_cols + 2] += jnp.sum(
            grad_x[s] * live_branch[s], axis=0, keepdims=True
        )

    def add_to(k, value, s):
        if s == 0:
            acc[k] = value
        else:
            acc[k] += value

    def start_back(s):
        position = z * rows + lax.broadcasted_iota(jnp.int32, (rows, 1), 0)
        live = (position < lens[s]).astype(F32)
        grad_branch = (alpha_attn * live * grad_x[s]).astype(BF)
        add_to(0, mm(attn_t[s], grad_branch), s)
        do = mm_nt(grad_branch, wo[...]).astype(BF)
        split_heads(do, do_m)
        do_t[...] = mm_nt(wo[...], grad_branch).astype(BF)
        for h in range(HEADS):
            here = slice(h * HEAD_DIM, (h + 1) * HEAD_DIM)
            delta[h] = jnp.sum(do_t[here].astype(F32) * o_t[s, here], axis=0, keepdims=True)
        dq_t[...] = jnp.zeros_like(dq_t)
        if s == 0:
            acc[2] = jnp.zeros_like(acc[2])
            acc[3] = jnp.zeros_like(acc[3])

        @pl.when(has_up)
        def _():
            def sent(j):
                for h in (0, 1):
                    x_copy(s, j, h).wait_send()

            loop(sent, z + 1)

    def block(s, j):
        here = slot(s, j)
        if not keep:
            project(s, j)
            probabilities(s, j)
        for head in range(HEADS):
            p, half = head // 2, slice(head % 2 * rows, (head % 2 + 1) * rows)
            grad_probs = mm_nt(v_all[here, :, p * PAIR : (p + 1) * PAIR], do_m[p, half])
            probs = prob_bf[here, p, :, half].astype(F32)
            grad_bf[p, :, half] = (probs * (grad_probs - delta[head])).astype(BF)
        for p in range(pairs):
            lanes = slice(p * PAIR, (p + 1) * PAIR)
            dv[:, lanes] = mm(prob_bf[here, p], do_m[p]).astype(BF)
            dk[:, lanes] = mm(grad_bf[p], q_m[s, p]).astype(BF)
            for h in (0, 1):
                own = slice(p * PAIR + h * HEAD_DIM, p * PAIR + (h + 1) * HEAD_DIM)
                dq_t[own] += mm(k_t[here, own], grad_bf[p, :, h * rows : (h + 1) * rows])
        part = mm_nt(dk[...], wk[...]) + mm_nt(dv[...], wv[...])
        x_t[...] = x_all[s, j].T
        acc[2] += mm(x_t[...], dk[...])
        acc[3] += mm(x_t[...], dv[...])

        @pl.when(j < z)
        def _():
            x_all[s, j] = part.astype(BF)

        @pl.when(j == z)
        def _():
            grad_x[s] += part

    def send_part(s, j):
        @pl.when(jnp.logical_not(has_up) & (j < z))
        def _():
            r_copy(s, j, x_all).start()

    def end_back(s):
        dq = (dq_t[...] * 0.125).T.astype(BF)
        x_t[...] = x_all[s, z].T
        add_to(1, mm(x_t[...], dq), s)
        grad_x[s] += mm_nt(dq, wq[...])

    def pass_back(s, hop, j):
        @pl.when(z == n - 2 - hop)
        def _():
            r_copy(s, j, back_in).wait_recv()

            @pl.when(j < z)
            def _():
                back_in[s, j] = back_in[s, j] + x_all[s, j]
                r_copy(s, j, back_in).start()

    def finish_input(s):
        @pl.when(has_up)
        def _():
            grad_input[s] = (grad_x[s] + back_in[s, z].astype(F32)).astype(BF)

        @pl.when(jnp.logical_not(has_up))
        def _():
            grad_input[s] = grad_x[s].astype(BF)

    def small_bit(i):
        return pltpu.make_async_remote_copy(
            src_ref=small.at[i], dst_ref=small_land.at[i],
            send_sem=small_send.at[i], recv_sem=small_recv.at[i],
            device_id=plan.partner(*plane[i]), device_id_type=MESH,
        )

    def small_to(d):
        sem = len(plane) + d - 1
        return pltpu.make_async_remote_copy(
            src_ref=small.at[len(plane)], dst_ref=small_line.at[z],
            send_sem=small_send.at[sem], recv_sem=small_recv.at[sem],
            device_id=(b, (z + d) % n), device_id_type=MESH,
        )

    def small_step(i):
        if i > 0:
            small_bit(i - 1).wait()
            small[i] = small[i - 1] + small_land[i - 1]
        if i < len(plane):
            small_bit(i).start()
        else:
            for d in range(1, n):
                small_to(d).start()

    def small_end():
        for d in range(1, n):
            small_to(d).wait()
        small_line[z] = small[len(plane)]
        value = small_line[0]
        for d in range(1, n):
            value = value + small_line[d]
        small_out[...] = value

    def sum_stage(k, c):
        if k == 0 and c >= ff_cols:
            for i in (0, 1):
                part = acc[2 * (c - ff_cols) + i]
                grads[c, i * width : (i + 1) * width] = part.astype(BF)
        plan.stage(k, c)

    steps = {
        "attention": attention, "start_ff": start_feed_forward, "end_ff": end_feed_forward,
        "start_back": start_back, "block": block, "end_back": end_back, "send": send_part,
        "pass": pass_back, "sum": sum_stage, "small": small_step,
        "sends": lambda s: loop(functools.partial(send_part, s), z),
        "passes": lambda s, hop: loop(functools.partial(pass_back, s, hop), n - 1 - hop),
    }

    loop(start_seq, seqs)

    @pl.when(z == 0)
    def _():
        send_own(1)

    attention(0)
    start_feed_forward(0)

    def first_column(c):
        @pl.when((z > c) & has_up)
        def _():
            for h in (0, 1):
                pass_on(1, z - c - 1, h)

        column(0, c)

    loop(first_column, ff_cols // 2)
    end_feed_forward(0)

    if n == 4 and ff_cols == 4 and plan.stages == 9 and seqs == 2:
        order = ORDER
    else:
        order = default_order(plan.stages, n, ff_cols, chunks, len(plane))

    def run(step):
        @pl.when(z >= 0)
        def _():
            steps[step[0]](*step[1:])

    def run_between(group):
        at = [i for i, step in enumerate(group) if step[0] == "column"]
        if not at:
            for step in group:
                run(step)
            return
        for step in group[: at[0]]:
            run(step)

        def one(c):
            column(seqs - 1, c)
            for k in range(ff_cols // 2 - 1):
                inside = group[at[k] + 1 : at[k + 1]]
                if inside:
                    @pl.when(c == k)
                    def _():
                        for step in inside:
                            run(step)

        loop(one, ff_cols // 2)
        for step in group[at[-1] + 1 :]:
            run(step)

    at = [i for i, step in enumerate(order) if step[0] == "block"]
    for step in order[: at[0]]:
        run(step)

    def one_block(t):
        s, j = t // n, t % n

        @pl.when(j <= z)
        def _():
            block(s, j)

        for k in range(len(at) - 1):
            group = order[at[k] + 1 : at[k + 1]]
            if group:
                @pl.when(t == k)
                def _():
                    run_between(group)

    loop(one_block, len(at))
    for step in order[at[-1] + 1 :]:
        run(step)
    for s in range(seqs):
        finish_input(s)
    small_end()
    @pl.when(has_down)
    def _():
        for s in range(seqs):
            loop(lambda j: r_copy(s, j, back_in).wait_send(), z)


def expand_kernel(
    cols, total, small, outputs_in, input_in,
    back, w_in, out, query, key, value, outputs, grad_input, b_in, b_back, alpha_attn, alpha_ffn,
    full, store_sem, pass_sem,
):
    chunks, _, width = total.shape
    stores = [
        pltpu.make_async_copy(outputs_in, outputs, pass_sem.at[0]),
        pltpu.make_async_copy(input_in, grad_input, pass_sem.at[1]),
    ]
    for one in stores:
        one.start()
    places = []
    for c in range(cols):
        here = pl.ds(c * width, width)
        places.append((back.at[here], w_in.at[:, here]))
    places += [(out, query), (key, value)]
    for c in range(chunks):
        for i in (0, 1):
            full[c, i] = total[c, i * width : (i + 1) * width].astype(F32)
            stores.append(pltpu.make_async_copy(full.at[c, i], places[c][i], store_sem.at[c, i]))
            stores[-1].start()
    for c in range(cols):
        b_in[:, c * width : (c + 1) * width] = small[c : c + 1]
    b_back[...] = small[cols : cols + 1]
    alpha_attn[...] = jnp.sum(small[cols + 1 : cols + 2], axis=1, keepdims=True)
    alpha_ffn[...] = jnp.sum(small[cols + 2 : cols + 3], axis=1, keepdims=True)
    for one in stores:
        one.wait()


def expand(total, small, outputs, grad_input, ff):
    chunks, _, width = total.shape
    cols = ff // width
    square = jax.ShapeDtypeStruct((width, width), F32)
    scalar = jax.ShapeDtypeStruct((1, 1), F32)
    vmem = pl.BlockSpec(memory_space=pltpu.VMEM)
    hbm = pl.BlockSpec(memory_space=pl.ANY)
    return pl.pallas_call(
        functools.partial(expand_kernel, cols),
        out_shape=(
            jax.ShapeDtypeStruct((ff, width), F32),
            jax.ShapeDtypeStruct((width, ff), F32),
            square, square, square, square,
            jax.ShapeDtypeStruct(outputs.shape, BF),
            jax.ShapeDtypeStruct(outputs.shape, BF),
            jax.ShapeDtypeStruct((1, ff), F32),
            jax.ShapeDtypeStruct((1, width), F32),
            scalar, scalar,
        ),
        in_specs=[vmem] * 4,
        out_specs=(hbm,) * 8 + (vmem,) * 4,
        scratch_shapes=[
            pltpu.VMEM((chunks, 2, width, width), F32),
            pltpu.SemaphoreType.DMA((chunks, 2)),
            pltpu.SemaphoreType.DMA((2,)),
        ],
        name="expand",
        compiler_params=pltpu.CompilerParams(vmem_limit_bytes=40 << 20),
    )(total, small, outputs, grad_input)


def per_device(
    tokens, lengths, w_query, w_key, w_value, w_out, w_in, b_in, w_back, b_back,
    alpha_attn, alpha_ffn, cotangent,
):
    seqs, rows, width = tokens.shape
    ff = w_in.shape[1]
    nb, n = lax.axis_size("batch"), lax.axis_size("blk")
    keep = n <= 4
    slots = seqs * n if keep else 1
    ff_cols = ff // width
    chunks = ff_cols + 2
    plan = Reducer(nb, n, 2 * width)
    steps = nb.bit_length() - 1
    small_rows = -(-(ff_cols + 3) // 8) * 8
    vmem = pl.BlockSpec(memory_space=pltpu.VMEM)
    smem = pl.BlockSpec(memory_space=pltpu.SMEM)
    hbm = pl.BlockSpec(memory_space=pl.ANY)
    square = (rows, width)
    dma = pltpu.SemaphoreType.DMA
    outputs, grad_input, total, small = pl.pallas_call(
        functools.partial(layer_kernel, plan, n, keep),
        out_shape=(
            pltpu.VMEM(tokens.shape, BF),
            pltpu.VMEM(tokens.shape, BF),
            pltpu.VMEM((chunks, 2 * width, width), BF),
            pltpu.VMEM((small_rows, width), F32),
        ),
        in_specs=[smem] * 3 + [hbm] * 10,
        out_specs=(vmem,) * 4,
        scratch_shapes=[
            pltpu.VMEM((1, ff), F32), pltpu.VMEM((1, width), F32),
            pltpu.VMEM(tokens.shape, BF),
            pltpu.VMEM((width, width), BF), pltpu.VMEM((width, width), BF),
            pltpu.VMEM((width, width), BF), pltpu.VMEM((width, width), BF),
            pltpu.VMEM(w_in.shape, BF), pltpu.VMEM(w_back.shape, BF),
            dma((seqs + 9,)),
            pltpu.VMEM((seqs, n) + square, BF),
            pltpu.VMEM((width, rows), BF),
            pltpu.VMEM((n + 1 if keep else 1,) + square, BF),
            pltpu.VMEM((slots,) + square, BF),
            pltpu.VMEM((slots, width, rows), BF),
            pltpu.VMEM((n + 1 if keep else 1, width, rows), BF),
            pltpu.VMEM((seqs, HEADS // 2, 2 * rows, PAIR), BF),
            pltpu.VMEM((HEADS // 2, 2 * rows, PAIR), BF),
            pltpu.VMEM((HEADS, rows, rows), F32),
            pltpu.VMEM((slots, HEADS // 2, rows, 2 * rows), BF),
            pltpu.VMEM((HEADS // 2, rows, 2 * rows), BF),
            pltpu.VMEM((seqs, HEADS, 1, rows), F32),
            pltpu.VMEM((seqs, HEADS, 1, rows), F32),
            pltpu.VMEM((seqs, width, rows), F32),
            pltpu.VMEM((seqs, width, rows), BF),
            pltpu.VMEM((width, rows), BF),
            pltpu.VMEM((seqs,) + square, F32),
            pltpu.VMEM(square, F32),
            pltpu.VMEM(square, BF),
            pltpu.VMEM((width, rows), BF),
            pltpu.VMEM(square, BF),
            pltpu.VMEM(square, F32),
            pltpu.VMEM((seqs,) + square, F32),
            pltpu.VMEM((seqs, HEADS, 1, rows), F32),
            pltpu.VMEM((HEADS, 1, rows), F32),
            pltpu.VMEM((width, rows), F32),
            pltpu.VMEM(square, BF),
            pltpu.VMEM(square, BF),
            pltpu.VMEM((4, width, width), F32),
            pltpu.VMEM((seqs, n) + square, BF),
            dma((seqs, n, 2)), dma((seqs, n, 2)), dma((seqs, n)), dma((seqs, n)),
            pltpu.VMEM((chunks, 2 * width, width), BF),
        ]
        + plan.scratch(chunks, width)
        + [
            pltpu.VMEM((steps + 1, small_rows, width), F32),
            pltpu.VMEM((steps, small_rows, width), F32),
            pltpu.VMEM((n, small_rows, width), F32),
            dma((steps + n - 1,)),
            dma((steps + n - 1,)),
        ],
        name="layer",
        compiler_params=pltpu.CompilerParams(
            collective_id=0, has_side_effects=True, vmem_limit_bytes=113 << 19
        ),
    )(
        lengths, alpha_attn.reshape(1), alpha_ffn.reshape(1), b_in.reshape(1, ff),
        b_back.reshape(1, width), tokens, cotangent, w_query, w_key, w_value, w_out, w_in, w_back,
    )
    back, grad_in, out, query, key, value, outputs, grad_input, b_in, b_back, attn, ffn = expand(
        total, small, outputs, grad_input, ff
    )
    return (
        outputs, grad_input, query, key, value, out, grad_in, b_in.reshape(ff), back,
        b_back.reshape(width), attn.reshape(()), ffn.reshape(()),
    )


def solution(mesh):
    return jax.shard_map(
        per_device,
        mesh=mesh,
        in_specs=(
            P("batch", "blk", None),
            P("batch"),
            P(),
            P(),
            P(),
            P(),
            P(),
            P(),
            P(),
            P(),
            P(),
            P(),
            P("batch", "blk", None),
        ),
        out_specs=(
            P("batch", "blk", None),
            P("batch", "blk", None),
            P(),
            P(),
            P(),
            P(),
            P(),
            P(),
            P(),
            P(),
            P(),
            P(),
        ),
        check_vma=False,
    )
```

```python
import functools

import jax
import jax.numpy as jnp
from jax import lax
from jax.experimental import pallas as pl
from jax.experimental.pallas import tpu as pltpu
from jax.sharding import PartitionSpec as P

HEADS = 8
HEAD_DIM = 64
PAIR = 2 * HEAD_DIM
MESH = pl.DeviceIdType.MESH
BF = jnp.bfloat16
F32 = jnp.float32
NEG = -1e30
GELU_A = 0.7978845608
GELU_B = 0.7978845608 * 0.044715

ORDER = (
    ("start_back", 0), ("block", 0, 0), ("block", 0, 1), ("send", 0, 0), ("send", 0, 1), ("attention", 1),
    ("start_ff", 1), ("column", 1, 0), ("sum", 0, 0), ("column", 1, 1), ("end_ff", 1), ("small", 0),
    ("pass", 0, 0, 0), ("sum", 0, 3), ("sum", 1, 0), ("sum", 0, 1), ("block", 0, 2), ("sum", 1, 3), ("send", 0, 2),
    ("block", 0, 3), ("end_back", 0), ("sum", 0, 2), ("sum", 2, 0), ("pass", 0, 0, 1), ("sum", 1, 1),
    ("start_back", 1), ("block", 1, 0), ("small", 1), ("sum", 2, 3), ("sum", 1, 2), ("sum", 3, 0), ("block", 1, 1),
    ("block", 1, 2), ("small", 2), ("pass", 0, 1, 0), ("pass", 0, 2, 0), ("sum", 2, 1), ("sum", 3, 3),
    ("block", 1, 3), ("small", 3), ("end_back", 1), ("sum", 0, 5), ("sum", 4, 0), ("sum", 0, 4), ("sum", 2, 2),
    ("sum", 3, 1), ("sum", 1, 5), ("sum", 3, 2), ("sum", 1, 4), ("sum", 4, 3), ("sum", 2, 5), ("pass", 0, 1, 1),
    ("sum", 5, 0), ("sum", 4, 1), ("sum", 4, 2), ("sum", 2, 4), ("sum", 5, 3), ("sum", 3, 5), ("sum", 6, 0),
    ("sum", 5, 1), ("sum", 3, 4), ("send", 1, 0), ("sum", 5, 2), ("sum", 7, 0), ("sum", 6, 3), ("sum", 6, 2),
    ("sum", 4, 5), ("sum", 6, 1), ("sum", 4, 4), ("pass", 1, 0, 0), ("sum", 5, 5), ("send", 1, 1), ("sum", 7, 3),
    ("sum", 7, 2), ("send", 1, 2), ("sum", 5, 4), ("sum", 7, 1), ("sum", 6, 5), ("sum", 6, 4), ("pass", 1, 1, 0),
    ("pass", 1, 0, 1), ("sum", 8, 2), ("sum", 8, 1), ("pass", 0, 0, 2), ("sum", 7, 5), ("sum", 8, 0), ("sum", 7, 4),
    ("sum", 8, 5), ("pass", 1, 0, 2), ("sum", 8, 3), ("sum", 8, 4), ("pass", 1, 1, 1), ("pass", 1, 2, 0),
)


class Reducer:
    def __init__(self, nb, nz, rows):
        self.rows, self.nz = rows, nz
        plane = [("batch", 1 << i) for i in range(1, nb.bit_length() - 1)]
        line = [("blk", 1 << i) for i in range(nz.bit_length() - 1)]
        self.all_bits = [("batch", 1)] + plane + line
        direct = (rows // 4 >> len(plane)) // nz >= 16
        steps = line if not direct else [("blk", 0)]
        self.orders = [plane + steps, plane[::-1] + steps]
        self.steps = len(self.orders[0])
        self.kinds, self.sizes, self.lands = [], [], [[], []]
        self.messages = []
        length, land = rows // 4, rows // 2
        for axis, bit in self.orders[0]:
            if bit == 0:
                kind, length, messages = "direct", length // nz, nz - 1
            elif length >= 32:
                kind, length, messages = "half", length // 2, 1
            else:
                kind, messages = "full", 1
            self.kinds.append(kind)
            self.sizes.append(length)
            self.messages.append(messages)
            for o in (0, 1):
                self.lands[o].append(land)
                land += length * messages
        self.land_rows = land
        self.back_steps = [i for i in range(self.steps) if self.kinds[i] != "full"][::-1]
        self.stages = 3 + self.steps + len(self.back_steps)

    def scratch(self, chunks, width):
        return [
            pltpu.VMEM((chunks, self.land_rows, width), BF),
            pltpu.SemaphoreType.DMA((chunks, self.stages - 1)),
            pltpu.SemaphoreType.DMA((chunks, self.stages - 1)),
        ]

    def bind(self, grads, total, land, send_sem, recv_sem):
        self.grads, self.total, self.land = grads, total, land
        self.send_sem, self.recv_sem = send_sem, recv_sem
        self.at = {"batch": lax.axis_index("batch"), "blk": lax.axis_index("blk")}
        core = self.at["batch"] % 2
        half = self.rows // 2
        self.core_keep, self.core_send = core * half, (1 - core) * half
        self.start, self.keep, self.send = [[], []], [[], []], [[], []]
        for o in (0, 1):
            off = self.core_keep + o * (half // 2)
            for i, (axis, bit) in enumerate(self.orders[o]):
                size, here = self.sizes[i], self.at[axis]
                self.start[o].append(off)
                if self.kinds[i] == "half":
                    mine = (here // bit) % 2
                    self.keep[o].append(off + mine * size)
                    self.send[o].append(off + (1 - mine) * size)
                elif self.kinds[i] == "direct":
                    self.keep[o].append(off + here * size)
                    self.send[o].append(None)
                else:
                    self.keep[o].append(off)
                    self.send[o].append(off)
                off = self.keep[o][-1]

    def partner(self, axis, bit):
        mine = (self.at[axis] // bit) % 2
        there = self.at[axis] + bit * (1 - 2 * mine)
        if axis == "batch":
            return (there, self.at["blk"])
        return (self.at["batch"], there)

    def copy(self, c, src, src_row, dst, dst_row, size, sem, device):
        return pltpu.make_async_remote_copy(
            src_ref=src.at[c, pl.ds(pl.multiple_of(src_row, 16), size)],
            dst_ref=dst.at[c, pl.ds(pl.multiple_of(dst_row, 16), size)],
            send_sem=self.send_sem.at[c, sem],
            recv_sem=self.recv_sem.at[c, sem],
            device_id=device,
            device_id_type=MESH,
        )

    def core_out(self, c):
        there = self.partner("batch", 1)
        return self.copy(c, self.grads, self.core_send, self.land, 0, self.rows // 2, 0, there)

    def core_back(self, c):
        there, row, sem = self.partner("batch", 1), self.core_keep, self.stages - 2
        return self.copy(c, self.total, row, self.total, row, self.rows // 2, sem, there)

    def start_out(self, c, i):
        size = self.sizes[i]
        for o in (0, 1):
            axis, bit = self.orders[o][i]
            land = self.lands[o][i]
            if self.kinds[i] != "direct":
                there = self.partner(axis, bit)
                self.copy(c, self.grads, self.send[o][i], self.land, land, size, i + 1, there).start()
                continue
            for d in range(1, self.nz):
                there = (self.at["blk"] + d) % self.nz
                row, peer = self.start[o][i] + there * size, (self.at["batch"], there)
                self.copy(
                    c, self.grads, row, self.land, land + (d - 1) * size, size, i + 1, peer
                ).start()

    def start_back(self, c, place):
        i, sem = self.back_steps[place], self.steps + 1 + place
        for o in (0, 1):
            axis, bit = self.orders[o][i]
            size, row = self.sizes[i], self.keep[o][i]
            peers = [self.partner(axis, bit)]
            if self.kinds[i] == "direct":
                peers = [(self.at["batch"], (self.at["blk"] + d) % self.nz) for d in range(1, self.nz)]
            for peer in peers:
                self.copy(c, self.total, row, self.total, row, size, sem, peer).start()

    def wait(self, c, ref, i, sem):
        rows = 2 * self.sizes[i] * self.messages[i]
        every = self.copy(c, ref, 0, ref, 0, rows, sem, self.partner("batch", 1))
        every.wait_send()
        every.wait_recv()

    def add(self, c, row, land_row, size, pieces=1, last=False):
        part = min(size, 64)
        target = self.total if last else self.grads

        def body(k, carry):
            here = pl.ds(pl.multiple_of(row + k * part, 16), part)
            value = self.grads[c, here]
            if pieces > 1:
                value = value.astype(F32)
            for d in range(pieces):
                there = pl.ds(pl.multiple_of(land_row + d * size + k * part, 16), part)
                value = value + self.land[c, there].astype(value.dtype)
            target[c, here] = value.astype(BF)
            return carry

        lax.fori_loop(0, size // part, body, 0)

    def stage(self, k, c):
        if k == 0:
            self.core_out(c).start()
            return
        if k == 1:
            self.core_out(c).wait()
            self.add(c, self.core_keep, 0, self.rows // 2)
        elif k <= self.steps + 1:
            i = k - 2
            self.wait(c, self.land, i, k - 1)
            pieces = self.nz - 1 if self.kinds[i] == "direct" else 1
            last = i == self.steps - 1
            for o in (0, 1):
                self.add(c, self.keep[o][i], self.lands[o][i], self.sizes[i], pieces, last)
        elif k < self.stages - 1:
            self.wait(c, self.total, self.back_steps[k - self.steps - 2], k - 1)
        else:
            self.core_back(c).wait()
            return
        if k <= self.steps:
            self.start_out(c, k - 1)
        elif k < self.stages - 2:
            self.start_back(c, k - self.steps - 1)
        else:
            self.core_back(c).start()


def mm(left, right):
    return jnp.dot(left, right, preferred_element_type=F32)


def mm_nt(left, right):
    return lax.dot_general(left, right, (((1,), (1,)), ((), ())), preferred_element_type=F32)


def mm_tn(left, right):
    return lax.dot_general(left, right, (((0,), (0,)), ((), ())), preferred_element_type=F32)


def default_order(stages, n, ff_cols, chunks, plane_bits):
    order = [("start_back", 0)] + [("block", 0, j) for j in range(n)] + [("end_back", 0)]
    order += [("attention", 1), ("start_ff", 1)] + [("column", 1, c) for c in range(ff_cols // 2)] + [("end_ff", 1)]
    order += [("start_back", 1)] + [("block", 1, j) for j in range(n)] + [("end_back", 1)]
    order += [("sends", 0), ("sends", 1)]
    order += [("passes", s, hop) for s in (0, 1) for hop in range(n - 1)]
    order += [("small", i) for i in range(plane_bits + 1)]
    for t in range(stages + chunks - 1):
        order += [("sum", k, t - k) for k in range(stages - 1, -1, -1) if 0 <= t - k < chunks]
    return order


def layer_kernel(plan, n, keep, lens, alpha_attn_ref, alpha_ffn_ref, *refs):
    (
        b_in_hbm, b_back_hbm, tokens_hbm, cot_hbm, wq_hbm, wk_hbm, wv_hbm, wo_hbm, w_in_hbm, w_back_hbm,
        outputs, grad_input, total, small_out,
        b_in, b_back, cot, wq, wk, wv, wo, w_in, w_back, load_sem,
        x_all, x_t, k_all, v_all, k_t, v_t, q_m, do_m, score, bias, prob_bf, grad_bf, top, norm, o_t, attn_t, do_t,
        live_branch, resid, resid_bf, resid_t, grad_ffn, ffn, grad_x, lse, delta,
        dq_t, dk, dv, acc, back_in,
        x_send, x_recv, r_send, r_recv,
        grads, land, send_sem, recv_sem, small, small_land, small_line, small_send, small_recv,
    ) = refs
    seqs, _, rows, width = x_all.shape
    chunks = grads.shape[0]
    ff_cols = w_in.shape[1] // width
    pairs = width // PAIR
    plan.bind(grads, total, land, send_sem, recv_sem)
    b, z = lax.axis_index("batch"), lax.axis_index("blk")
    has_up, has_down = z < n - 1, z > 0
    alpha_attn, alpha_ffn = alpha_attn_ref[0], alpha_ffn_ref[0]

    def loop(f, count):
        def body(j, carry):
            f(j)
            return carry

        lax.fori_loop(0, count, body, 0)

    def load(i):
        if i < seqs:
            return pltpu.make_async_copy(tokens_hbm.at[i], x_all.at[i, z], load_sem.at[i])
        pairs_of = [
            (wk_hbm, wk), (wv_hbm, wv), (wq_hbm, wq), (wo_hbm, wo),
            (w_in_hbm, w_in), (w_back_hbm, w_back), (cot_hbm, cot), (b_in_hbm, b_in), (b_back_hbm, b_back),
        ]
        src, dst = pairs_of[i - seqs]
        return pltpu.make_async_copy(src, dst, load_sem.at[i])

    load(0).start()

    def x_copy(s, j, h):
        here = pl.ds(h * (rows // 2), rows // 2)
        return pltpu.make_async_remote_copy(
            src_ref=x_all.at[s, j, here], dst_ref=x_all.at[s, j, here],
            send_sem=x_send.at[s, j, h], recv_sem=x_recv.at[s, j, h],
            device_id=(b, z + 1), device_id_type=MESH,
        )

    def r_copy(s, j, src):
        return pltpu.make_async_remote_copy(
            src_ref=src.at[s, j], dst_ref=back_in.at[s, j],
            send_sem=r_send.at[s, j], recv_sem=r_recv.at[s, j],
            device_id=(b, z - 1), device_id_type=MESH,
        )

    barrier = pltpu.get_barrier_semaphore()
    plane = [(axis, bit) for axis, bit in plan.all_bits if axis == "batch"]
    peers = [plan.partner(axis, bit) for axis, bit in plane] + [(b, (z + d) % n) for d in range(1, n)]
    for peer in peers:
        pl.semaphore_signal(barrier, inc=1, device_id=peer, device_id_type=MESH)
    for i in range(1, seqs + 9):
        load(i).start()
    pl.semaphore_wait(barrier, len(peers))

    def send_own(s):
        @pl.when(has_up)
        def _():
            for h in (0, 1):
                x_copy(s, z, h).start()

    load(0).wait()
    send_own(0)
    for s in range(1, seqs):
        load(s).wait()

    for i in range(3):
        load(seqs + i).wait()
    small[0] = jnp.zeros_like(small[0])
    low_lanes = lax.broadcasted_iota(jnp.int32, (rows, PAIR), 1) < HEAD_DIM
    key_iota = lax.broadcasted_iota(jnp.int32, (rows, rows), 0)
    query_pos = z * rows + lax.broadcasted_iota(jnp.int32, (1, rows), 1)

    def split_heads(value, target):
        for h in range(HEADS):
            pair = value[:, (h // 2) * PAIR : (h // 2 + 1) * PAIR]
            mask = low_lanes if h % 2 == 0 else jnp.logical_not(low_lanes)
            target[h // 2, h % 2 * rows : (h % 2 + 1) * rows] = jnp.where(mask, pair, 0.0).astype(BF)

    def slot(s, j):
        return s * n + j if keep else 0

    def forward_slot(s, j):
        return jnp.where((s > 0) & (j == z), n, j) if keep else 0

    def project(s, j):
        here, front = slot(s, j), forward_slot(s, j)
        x = x_all[s, j]
        keys, values = mm(x, wk[...]).astype(BF), mm(x, wv[...]).astype(BF)
        k_all[front], v_all[here] = keys, values
        k_t[here], v_t[front] = keys.T, values.T

    def forbid(s, j):
        limit = jnp.minimum(query_pos + 1, lens[s]) - j * rows
        bias[...] = jnp.where(key_iota < limit, 0.0, NEG)

    def scores_of(s, j, head):
        p, half = head // 2, slice(head % 2 * rows, (head % 2 + 1) * rows)
        keys = k_all[forward_slot(s, j), :, p * PAIR : (p + 1) * PAIR]
        return mm_nt(keys, q_m[s, p, half]) + bias[...]

    def statistics(s, j):
        forbid(s, j)
        for head in range(HEADS):
            score[head] = scores_of(s, j, head)
        for head in range(HEADS):
            old = top[s, head]
            new = jnp.maximum(old, jnp.max(score[head], axis=0, keepdims=True))
            below = jnp.sum(jnp.exp(score[head] - new), axis=0, keepdims=True)
            norm[s, head] = norm[s, head] * jnp.exp(old - new) + below
            top[s, head] = new

    def probabilities(s, j):
        forbid(s, j)
        for head in range(HEADS):
            p, half = head // 2, slice(head % 2 * rows, (head % 2 + 1) * rows)
            probs = jnp.exp(scores_of(s, j, head) - lse[s, head])
            prob_bf[slot(s, j), p, :, half] = probs.astype(BF)

    def mix_values(s, j):
        if not keep:
            project(s, j)
        probabilities(s, j)
        for head in range(HEADS):
            p, half = head // 2, slice(head % 2 * rows, (head % 2 + 1) * rows)
            own = slice(head * HEAD_DIM, (head + 1) * HEAD_DIM)
            o_t[s, own] += mm(v_t[forward_slot(s, j), own], prob_bf[slot(s, j), p, :, half])

    def pass_on(s, j, h):
        x_copy(s, j, h).wait_recv()

        @pl.when(has_up)
        def _():
            x_copy(s, j, h).start()

    def start_seq(s):
        q = mm(x_all[s, z], wq[...]).astype(BF).astype(F32) * 0.125
        split_heads(q, q_m.at[s])
        top[s] = jnp.full_like(top[s], NEG)
        norm[s] = jnp.zeros_like(norm[s])
        o_t[s] = jnp.zeros_like(o_t[s])
        project(s, z)
        statistics(s, z)

    def attention(s):
        def block(i, carry):
            if s == 0:
                for h in (0, 1):
                    pass_on(s, z - i, h)
            else:
                @pl.when((2 * i > ff_cols) | jnp.logical_not(has_up))
                def _():
                    for h in (0, 1):
                        pass_on(s, z - i, h)
            project(s, z - i)
            statistics(s, z - i)
            return carry

        lax.fori_loop(1, z + 1, block, 0)
        if s == 0:
            @pl.when(z > 0)
            def _():
                send_own(1)

            load(seqs + 3).wait()
        lse[s] = top[s] + jnp.log(norm[s])
        loop(functools.partial(mix_values, s), z + 1)
        attn_t[s] = o_t[s].astype(BF)
        branch = mm(attn_t[s].T, wo[...])
        position = z * rows + lax.broadcasted_iota(jnp.int32, (rows, 1), 0)
        live = (position < lens[s]).astype(F32)
        live_branch[s] = live * branch
        resid[...] = x_all[s, z].astype(F32) + alpha_attn * live_branch[s]
        resid_bf[...] = resid[...].astype(BF)
        resid_t[...] = resid_bf[...].T

    def start_feed_forward(s):
        if s == 0:
            for i in range(4, 9):
                load(seqs + i).wait()
        grad_out = cot[s].astype(F32)
        grad_ffn[...] = (alpha_ffn * grad_out).astype(BF)
        ffn[...] = jnp.zeros_like(ffn)
        grad_x[s] = grad_out
        small[0, ff_cols : ff_cols + 1] += jnp.sum(
            grad_ffn[...].astype(F32), axis=0, keepdims=True
        )

    def column(s, c):
        lanes = pl.ds(pl.multiple_of(2 * c * width, 2 * width), 2 * width)
        hidden = mm(resid_bf[...], w_in[:, lanes]) + b_in[:, lanes]
        square = hidden * hidden
        half = 0.5 + 0.5 * jnp.tanh(hidden * (GELU_A + GELU_B * square))
        product = hidden * half
        act = product.astype(BF)
        slope = half + product * (1.0 - half) * (2 * GELU_A + 6 * GELU_B * square)
        back = w_back[lanes]
        ffn[...] += mm(act, back)
        grad_hidden = (mm_nt(grad_ffn[...], back) * slope).astype(BF)
        grad_bias = jnp.sum(grad_hidden.astype(F32), axis=0, keepdims=True)
        grad_x[s] += mm_nt(grad_hidden, w_in[:, lanes])
        grad_back = mm(act.T, grad_ffn[...])
        grad_in = mm(resid_t[...], grad_hidden)
        for i in (0, 1):
            chunk, part = 2 * c + i, slice(i * width, (i + 1) * width)
            upper, lower = grad_back[part], grad_in[:, part]
            if s > 0:
                upper += grads[chunk, :width].astype(F32)
                lower += grads[chunk, width:].astype(F32)
            grads[chunk, :width] = upper.astype(BF)
            grads[chunk, width:] = lower.astype(BF)
            small[0, pl.ds(chunk, 1)] += grad_bias[:, part]

    def end_feed_forward(s):
        ffn_out = ffn[...] + b_back[...]
        outputs[s] = (resid[...] + alpha_ffn * ffn_out).astype(BF)
        small[0, ff_cols + 2 : ff_cols + 3] += jnp.sum(
            cot[s].astype(F32) * ffn_out, axis=0, keepdims=True
        )
        small[0, ff_cols + 1 : ff_cols + 2] += jnp.sum(
            grad_x[s] * live_branch[s], axis=0, keepdims=True
        )

    def add_to(k, value, s):
        if s == 0:
            acc[k] = value
        else:
            acc[k] += value

    def start_back(s):
        position = z * rows + lax.broadcasted_iota(jnp.int32, (rows, 1), 0)
        live = (position < lens[s]).astype(F32)
        grad_branch = (alpha_attn * live * grad_x[s]).astype(BF)
        add_to(0, mm(attn_t[s], grad_branch), s)
        do = mm_nt(grad_branch, wo[...]).astype(BF)
        split_heads(do, do_m)
        do_t[...] = mm_nt(wo[...], grad_branch).astype(BF)
        for h in range(HEADS):
            here = slice(h * HEAD_DIM, (h + 1) * HEAD_DIM)
            delta[h] = jnp.sum(do_t[here].astype(F32) * o_t[s, here], axis=0, keepdims=True)
        dq_t[...] = jnp.zeros_like(dq_t)
        if s == 0:
            acc[2] = jnp.zeros_like(acc[2])
            acc[3] = jnp.zeros_like(acc[3])

        @pl.when(has_up)
        def _():
            def sent(j):
                for h in (0, 1):
                    x_copy(s, j, h).wait_send()

            loop(sent, z + 1)

    def block(s, j):
        here = slot(s, j)
        if not keep:
            project(s, j)
            probabilities(s, j)
        for head in range(HEADS):
            p, half = head // 2, slice(head % 2 * rows, (head % 2 + 1) * rows)
            grad_probs = mm_nt(v_all[here, :, p * PAIR : (p + 1) * PAIR], do_m[p, half])
            probs = prob_bf[here, p, :, half].astype(F32)
            grad_bf[p, :, half] = (probs * (grad_probs - delta[head])).astype(BF)
        for p in range(pairs):
            lanes = slice(p * PAIR, (p + 1) * PAIR)
            dv[:, lanes] = mm(prob_bf[here, p], do_m[p]).astype(BF)
            dk[:, lanes] = mm(grad_bf[p], q_m[s, p]).astype(BF)
            for h in (0, 1):
                own = slice(p * PAIR + h * HEAD_DIM, p * PAIR + (h + 1) * HEAD_DIM)
                dq_t[own] += mm(k_t[here, own], grad_bf[p, :, h * rows : (h + 1) * rows])
        part = mm_nt(dk[...], wk[...]) + mm_nt(dv[...], wv[...])
        x_t[...] = x_all[s, j].T
        acc[2] += mm(x_t[...], dk[...])
        acc[3] += mm(x_t[...], dv[...])

        @pl.when(j < z)
        def _():
            x_all[s, j] = part.astype(BF)

        @pl.when(j == z)
        def _():
            grad_x[s] += part

    def send_part(s, j):
        @pl.when(jnp.logical_not(has_up) & (j < z))
        def _():
            r_copy(s, j, x_all).start()

    def end_back(s):
        dq = (dq_t[...] * 0.125).T.astype(BF)
        x_t[...] = x_all[s, z].T
        add_to(1, mm(x_t[...], dq), s)
        grad_x[s] += mm_nt(dq, wq[...])

    def pass_back(s, hop, j):
        @pl.when(z == n - 2 - hop)
        def _():
            r_copy(s, j, back_in).wait_recv()

            @pl.when(j < z)
            def _():
                back_in[s, j] = back_in[s, j] + x_all[s, j]
                r_copy(s, j, back_in).start()

    def finish_input(s):
        @pl.when(has_up)
        def _():
            grad_input[s] = (grad_x[s] + back_in[s, z].astype(F32)).astype(BF)

        @pl.when(jnp.logical_not(has_up))
        def _():
            grad_input[s] = grad_x[s].astype(BF)

    def small_bit(i):
        return pltpu.make_async_remote_copy(
            src_ref=small.at[i], dst_ref=small_land.at[i],
            send_sem=small_send.at[i], recv_sem=small_recv.at[i],
            device_id=plan.partner(*plane[i]), device_id_type=MESH,
        )

    def small_to(d):
        sem = len(plane) + d - 1
        return pltpu.make_async_remote_copy(
            src_ref=small.at[len(plane)], dst_ref=small_line.at[z],
            send_sem=small_send.at[sem], recv_sem=small_recv.at[sem],
            device_id=(b, (z + d) % n), device_id_type=MESH,
        )

    def small_step(i):
        if i > 0:
            small_bit(i - 1).wait()
            small[i] = small[i - 1] + small_land[i - 1]
        if i < len(plane):
            small_bit(i).start()
        else:
            for d in range(1, n):
                small_to(d).start()

    def small_end():
        for d in range(1, n):
            small_to(d).wait()
        small_line[z] = small[len(plane)]
        value = small_line[0]
        for d in range(1, n):
            value = value + small_line[d]
        small_out[...] = value

    def sum_stage(k, c):
        if k == 0 and c >= ff_cols:
            for i in (0, 1):
                part = acc[2 * (c - ff_cols) + i]
                grads[c, i * width : (i + 1) * width] = part.astype(BF)
        plan.stage(k, c)

    steps = {
        "attention": attention, "start_ff": start_feed_forward, "end_ff": end_feed_forward,
        "start_back": start_back, "block": block, "end_back": end_back, "send": send_part,
        "pass": pass_back, "sum": sum_stage, "small": small_step,
        "sends": lambda s: loop(functools.partial(send_part, s), z),
        "passes": lambda s, hop: loop(functools.partial(pass_back, s, hop), n - 1 - hop),
    }

    loop(start_seq, seqs)

    @pl.when(z == 0)
    def _():
        send_own(1)

    attention(0)
    start_feed_forward(0)

    def first_column(c):
        @pl.when((z > c) & has_up)
        def _():
            for h in (0, 1):
                pass_on(1, z - c - 1, h)

        column(0, c)

    loop(first_column, ff_cols // 2)
    end_feed_forward(0)

    if n == 4 and ff_cols == 4 and plan.stages == 9 and seqs == 2:
        order = ORDER
    else:
        order = default_order(plan.stages, n, ff_cols, chunks, len(plane))

    def run(step):
        @pl.when(z >= 0)
        def _():
            steps[step[0]](*step[1:])

    def run_between(group):
        at = [i for i, step in enumerate(group) if step[0] == "column"]
        if not at:
            for step in group:
                run(step)
            return
        for step in group[: at[0]]:
            run(step)

        def one(c):
            column(seqs - 1, c)
            for k in range(ff_cols // 2 - 1):
                inside = group[at[k] + 1 : at[k + 1]]
                if inside:
                    @pl.when(c == k)
                    def _():
                        for step in inside:
                            run(step)

        loop(one, ff_cols // 2)
        for step in group[at[-1] + 1 :]:
            run(step)

    at = [i for i, step in enumerate(order) if step[0] == "block"]
    for step in order[: at[0]]:
        run(step)

    def one_block(t):
        s, j = t // n, t % n

        @pl.when(j <= z)
        def _():
            block(s, j)

        for k in range(len(at) - 1):
            group = order[at[k] + 1 : at[k + 1]]
            if group:
                @pl.when(t == k)
                def _():
                    run_between(group)

    loop(one_block, len(at))
    for step in order[at[-1] + 1 :]:
        run(step)
    for s in range(seqs):
        finish_input(s)
    small_end()
    @pl.when(has_down)
    def _():
        for s in range(seqs):
            loop(lambda j: r_copy(s, j, back_in).wait_send(), z)


def expand_kernel(
    cols, total, small, outputs_in, input_in,
    back, w_in, out, query, key, value, outputs, grad_input, b_in, b_back, alpha_attn, alpha_ffn,
    full, store_sem, pass_sem,
):
    chunks, _, width = total.shape
    stores = [
        pltpu.make_async_copy(outputs_in, outputs, pass_sem.at[0]),
        pltpu.make_async_copy(input_in, grad_input, pass_sem.at[1]),
    ]
    for one in stores:
        one.start()
    places = []
    for c in range(cols):
        here = pl.ds(c * width, width)
        places.append((back.at[here], w_in.at[:, here]))
    places += [(out, query), (key, value)]
    for c in range(chunks):
        for i in (0, 1):
            full[c, i] = total[c, i * width : (i + 1) * width].astype(F32)
            stores.append(pltpu.make_async_copy(full.at[c, i], places[c][i], store_sem.at[c, i]))
            stores[-1].start()
    for c in range(cols):
        b_in[:, c * width : (c + 1) * width] = small[c : c + 1]
    b_back[...] = small[cols : cols + 1]
    alpha_attn[...] = jnp.sum(small[cols + 1 : cols + 2], axis=1, keepdims=True)
    alpha_ffn[...] = jnp.sum(small[cols + 2 : cols + 3], axis=1, keepdims=True)
    for one in stores:
        one.wait()


def expand(total, small, outputs, grad_input, ff):
    chunks, _, width = total.shape
    cols = ff // width
    square = jax.ShapeDtypeStruct((width, width), F32)
    scalar = jax.ShapeDtypeStruct((1, 1), F32)
    vmem = pl.BlockSpec(memory_space=pltpu.VMEM)
    hbm = pl.BlockSpec(memory_space=pl.ANY)
    return pl.pallas_call(
        functools.partial(expand_kernel, cols),
        out_shape=(
            jax.ShapeDtypeStruct((ff, width), F32),
            jax.ShapeDtypeStruct((width, ff), F32),
            square, square, square, square,
            jax.ShapeDtypeStruct(outputs.shape, BF),
            jax.ShapeDtypeStruct(outputs.shape, BF),
            jax.ShapeDtypeStruct((1, ff), F32),
            jax.ShapeDtypeStruct((1, width), F32),
            scalar, scalar,
        ),
        in_specs=[vmem] * 4,
        out_specs=(hbm,) * 8 + (vmem,) * 4,
        scratch_shapes=[
            pltpu.VMEM((chunks, 2, width, width), F32),
            pltpu.SemaphoreType.DMA((chunks, 2)),
            pltpu.SemaphoreType.DMA((2,)),
        ],
        name="expand",
        compiler_params=pltpu.CompilerParams(vmem_limit_bytes=40 << 20),
    )(total, small, outputs, grad_input)


def per_device(
    tokens, lengths, w_query, w_key, w_value, w_out, w_in, b_in, w_back, b_back,
    alpha_attn, alpha_ffn, cotangent,
):
    seqs, rows, width = tokens.shape
    ff = w_in.shape[1]
    nb, n = lax.axis_size("batch"), lax.axis_size("blk")
    keep = n <= 4
    slots = seqs * n if keep else 1
    ff_cols = ff // width
    chunks = ff_cols + 2
    plan = Reducer(nb, n, 2 * width)
    steps = nb.bit_length() - 1
    small_rows = -(-(ff_cols + 3) // 8) * 8
    vmem = pl.BlockSpec(memory_space=pltpu.VMEM)
    smem = pl.BlockSpec(memory_space=pltpu.SMEM)
    hbm = pl.BlockSpec(memory_space=pl.ANY)
    square = (rows, width)
    dma = pltpu.SemaphoreType.DMA
    outputs, grad_input, total, small = pl.pallas_call(
        functools.partial(layer_kernel, plan, n, keep),
        out_shape=(
            pltpu.VMEM(tokens.shape, BF),
            pltpu.VMEM(tokens.shape, BF),
            pltpu.VMEM((chunks, 2 * width, width), BF),
            pltpu.VMEM((small_rows, width), F32),
        ),
        in_specs=[smem] * 3 + [hbm] * 10,
        out_specs=(vmem,) * 4,
        scratch_shapes=[
            pltpu.VMEM((1, ff), F32), pltpu.VMEM((1, width), F32),
            pltpu.VMEM(tokens.shape, BF),
            pltpu.VMEM((width, width), BF), pltpu.VMEM((width, width), BF),
            pltpu.VMEM((width, width), BF), pltpu.VMEM((width, width), BF),
            pltpu.VMEM(w_in.shape, BF), pltpu.VMEM(w_back.shape, BF),
            dma((seqs + 9,)),
            pltpu.VMEM((seqs, n) + square, BF),
            pltpu.VMEM((width, rows), BF),
            pltpu.VMEM((n + 1 if keep else 1,) + square, BF),
            pltpu.VMEM((slots,) + square, BF),
            pltpu.VMEM((slots, width, rows), BF),
            pltpu.VMEM((n + 1 if keep else 1, width, rows), BF),
            pltpu.VMEM((seqs, HEADS // 2, 2 * rows, PAIR), BF),
            pltpu.VMEM((HEADS // 2, 2 * rows, PAIR), BF),
            pltpu.VMEM((HEADS, rows, rows), F32),
            pltpu.VMEM((rows, rows), F32),
            pltpu.VMEM((slots, HEADS // 2, rows, 2 * rows), BF),
            pltpu.VMEM((HEADS // 2, rows, 2 * rows), BF),
            pltpu.VMEM((seqs, HEADS, 1, rows), F32),
            pltpu.VMEM((seqs, HEADS, 1, rows), F32),
            pltpu.VMEM((seqs, width, rows), F32),
            pltpu.VMEM((seqs, width, rows), BF),
            pltpu.VMEM((width, rows), BF),
            pltpu.VMEM((seqs,) + square, F32),
            pltpu.VMEM(square, F32),
            pltpu.VMEM(square, BF),
            pltpu.VMEM((width, rows), BF),
            pltpu.VMEM(square, BF),
            pltpu.VMEM(square, F32),
            pltpu.VMEM((seqs,) + square, F32),
            pltpu.VMEM((seqs, HEADS, 1, rows), F32),
            pltpu.VMEM((HEADS, 1, rows), F32),
            pltpu.VMEM((width, rows), F32),
            pltpu.VMEM(square, BF),
            pltpu.VMEM(square, BF),
            pltpu.VMEM((4, width, width), F32),
            pltpu.VMEM((seqs, n) + square, BF),
            dma((seqs, n, 2)), dma((seqs, n, 2)), dma((seqs, n)), dma((seqs, n)),
            pltpu.VMEM((chunks, 2 * width, width), BF),
        ]
        + plan.scratch(chunks, width)
        + [
            pltpu.VMEM((steps + 1, small_rows, width), F32),
            pltpu.VMEM((steps, small_rows, width), F32),
            pltpu.VMEM((n, small_rows, width), F32),
            dma((steps + n - 1,)),
            dma((steps + n - 1,)),
        ],
        name="layer",
        compiler_params=pltpu.CompilerParams(
            collective_id=0, has_side_effects=True, vmem_limit_bytes=113 << 19
        ),
    )(
        lengths, alpha_attn.reshape(1), alpha_ffn.reshape(1), b_in.reshape(1, ff),
        b_back.reshape(1, width), tokens, cotangent, w_query, w_key, w_value, w_out, w_in, w_back,
    )
    back, grad_in, out, query, key, value, outputs, grad_input, b_in, b_back, attn, ffn = expand(
        total, small, outputs, grad_input, ff
    )
    return (
        outputs, grad_input, query, key, value, out, grad_in, b_in.reshape(ff), back,
        b_back.reshape(width), attn.reshape(()), ffn.reshape(()),
    )


def solution(mesh):
    return jax.shard_map(
        per_device,
        mesh=mesh,
        in_specs=(
            P("batch", "blk", None),
            P("batch"),
            P(),
            P(),
            P(),
            P(),
            P(),
            P(),
            P(),
            P(),
            P(),
            P(),
            P("batch", "blk", None),
        ),
        out_specs=(
            P("batch", "blk", None),
            P("batch", "blk", None),
            P(),
            P(),
            P(),
            P(),
            P(),
            P(),
            P(),
            P(),
            P(),
            P(),
        ),
        check_vma=False,
    )
```
